32 devices in a mesh: gx: 4 (over y, x), gy: 4 (over z), gz: 2 (over core).
Axes of the slice: x: 2, y: 2, z: 4, core: 2. Of those that a mesh axis runs over, the one named last changes fastest.
Arguments:
- velocity: float32 [3, 32, 64, 8192], P(None, 'gz', 'gx', 'gy'), may hold values from -6 to 6
- blade_pos: float32 [64, 3, 128], P(('gx', 'gy', 'gz')), as said below
- block_turbine: int32 [64], P(('gx', 'gy', 'gz')), may hold values from 0 to 3, as said below
- blade_vel: float32 [64, 3, 128], P(('gx', 'gy', 'gz')), may hold values from -6 to 6
- lift_coeff: float32 [64, 128], P(('gx', 'gy', 'gz')), may hold values from 0.2 to 2
Outputs:
- new_velocity: float32 [3, 32, 64, 8192], P(None, 'gz', 'gx', 'gy')
- point_force: float32 [64, 3, 128], P(('gx', 'gy', 'gz'))
The draws below stay inside these ranges and needn't reach their ends.
Inputs may be any that keep to these rules, and one draw needn't show every extreme that they name: `block_turbine`: in each turbine row (blocks r * 4 * 2 * 2 onward, one row for each index of gx) every turbine number is named by exactly 4 blocks. `blade_pos`: the points of a block lie in its column: streamwise within its row's cells, spanwise within its turbine's cells, vertically between level 0 and the top level.
All inputs are finite; a program needn't handle non-finite values.
Results may differ from the reference program's by a relative error of at most 0.0003.
Values sent between devices are 32-bit elements; how exact they have to be, the bound alone decides.
No kernel may reach another device: no remote copies, remote signals or barrier semaphores. Data moves between devices by JAX's collectives and lax.ppermute only.
A program may use at most 192 MiB of HBM per device.

```python
import math
import jax
import jax.numpy as jnp
from jax import lax

CX = 16
CY = 2048
PTS = 128
BLK_OWN = 2
NX = 64
NY = 8192
NZ = 32
BLOCKS = 64
N_GX = 4
N_GY = 4
N_GZ = 2


def turbine_ids(key):
    row_blocks = N_GY * N_GZ * BLK_OWN
    row_keys = jax.random.split(jax.random.fold_in(key, 21), N_GX)
    shuffled = jax.vmap(lambda one_key: jax.random.permutation(one_key, row_blocks))(row_keys)
    return (shuffled // (N_GZ * BLK_OWN)).astype(jnp.int32).reshape(N_GX * row_blocks)


def draw_block_turbine(key, part):
    return turbine_ids(key)


def draw_blade_pos(key, part):
    turbine = turbine_ids(key).astype(jnp.float32)
    row = (jnp.arange(BLOCKS, dtype=jnp.int32) // (N_GY * N_GZ * BLK_OWN)).astype(jnp.float32)
    unit_x = jax.random.uniform(jax.random.fold_in(key, 22), (BLOCKS, PTS), jnp.float32)
    unit_y = jax.random.uniform(jax.random.fold_in(key, 23), (BLOCKS, PTS), jnp.float32)
    unit_z = jax.random.uniform(jax.random.fold_in(key, 24), (BLOCKS, PTS), jnp.float32)
    coord_x = row[:, None] * CX + unit_x * (CX - 1)
    coord_y = turbine[:, None] * CY + unit_y * (CY - 1)
    coord_z = unit_z * (NZ - 1)
    return jnp.stack([coord_x, coord_y, coord_z], axis=1).astype(jnp.float32)


def smooth_mean(key, strength):
    level = jnp.arange(NZ, dtype=jnp.int32).astype(jnp.float32) / max(NZ - 1, 1)
    stream = jnp.arange(NX, dtype=jnp.int32).astype(jnp.float32) / NX
    phase = jax.random.uniform(jax.random.fold_in(key, 2), (3,), jnp.float32, 0.0, 2.0 * math.pi)
    height = 0.85 + 0.3 * level
    wave = 1.0 + 0.1 * jnp.sin(2.0 * math.pi * stream[None, :] + phase[:, None])
    return strength[:, None, None, None] * height[None, :, None, None] * wave[:, None, :, None]


def draw_velocity(key, part):
    key = jax.random.fold_in(key, 31)
    shape = (3, NZ, NX, NY)
    strength = jnp.array([3.0, 2.5, -2.0], jnp.float32)
    noise = jax.random.normal(jax.random.fold_in(key, 1), shape, jnp.float32)
    field = smooth_mean(key, strength) + noise
    return jnp.clip(field, -6.0, 6.0).astype(jnp.float32)


def block_levels(own_key, shape, cuts, least, largest):
    gain, own = 1.0, jax.random.fold_in(own_key, 6)
    for axis_at, blocks in cuts:
        heights = jnp.exp(jax.random.uniform(jax.random.fold_in(own, axis_at), (blocks,), jnp.float32, least / len(cuts), largest / len(cuts)))
        gain = gain * jnp.repeat(heights, shape[axis_at] // blocks).reshape([-1 if axis == axis_at else 1 for axis in range(len(shape))])
    return gain


def normal_values(key, dims, scale, limit, pieces=(), held_as=jnp.bfloat16):
    drawn = scale * jax.random.normal(key, dims, jnp.float32)
    if pieces:
        drawn = drawn * block_levels(key, dims, pieces, -0.22, 0.18)
    return jnp.clip(drawn, -limit, limit).astype(held_as)


def setup_inputs(seed: int = 0) -> dict:
    arg_keys = jax.random.split(jax.random.key(seed), 6)
    return {
        "velocity": draw_velocity(jax.random.fold_in(arg_keys[5], 71), 0),
        "blade_pos": draw_blade_pos(jax.random.fold_in(arg_keys[5], 71), 0),
        "block_turbine": draw_block_turbine(jax.random.fold_in(arg_keys[5], 71), 0),
        "blade_vel": normal_values(arg_keys[3], (BLOCKS, 3, PTS), 1.0, 6.0, ((0, 32),), jnp.float32),
        "lift_coeff": jnp.clip(jnp.exp(math.log(2.0) - 2.3025851 * jax.random.uniform(arg_keys[4], (BLOCKS, PTS), jnp.float32) ** block_levels(arg_keys[4], (BLOCKS, PTS), ((0, 32),), -0.2, 0.2)), 0.2, 2.0),
    }


mean_wind = 1.0
viscosity = 0.2
smag_coeff = 0.17
time_step = 0.2
smear = 2.0
smear_norm = 1.0 / (smear ** 3 * math.pi ** 1.5)

def shifted(padded, axis_dim, offset):
    slicer = [slice(None), slice(2, -2), slice(2, -2), slice(2, -2)]
    extent = padded.shape[axis_dim] - 4
    slicer[axis_dim] = slice(2 + offset, 2 + offset + extent)
    return padded[tuple(slicer)]

def derivative(padded, axis_dim):
    near = shifted(padded, axis_dim, 1) - shifted(padded, axis_dim, -1)
    far = shifted(padded, axis_dim, 2) - shifted(padded, axis_dim, -2)
    return (8.0 * near - far) / 12.0

def second(padded, axis_dim):
    return (-shifted(padded, axis_dim, 2) + 16.0 * shifted(padded, axis_dim, 1) - 30.0 * shifted(padded, axis_dim, 0) + 16.0 * shifted(padded, axis_dim, -1) - shifted(padded, axis_dim, -2)) / 12.0

def tendency(padded, body_force):
    along_x = derivative(padded, 2)
    along_y = derivative(padded, 3)
    along_z = derivative(padded, 1)
    gradients = (along_x, along_y, along_z)
    strain_sq = jnp.zeros(along_x.shape[1:], jnp.float32)
    for row_comp in range(3):
        for col_comp in range(3):
            strain = 0.5 * (gradients[col_comp][row_comp] + gradients[row_comp][col_comp])
            strain_sq = strain_sq + strain * strain
    eddy_visc = smag_coeff * smag_coeff * jnp.sqrt(2.0 * strain_sq)
    laplacian = second(padded, 1) + second(padded, 2) + second(padded, 3)
    return -mean_wind * along_x + (viscosity + eddy_visc[None]) * laplacian + body_force

def blade_force(sampled, blade_vel, lift_coeff):
    relative = sampled - blade_vel
    rel_speed = jnp.sqrt(lax.optimization_barrier(jnp.sum(relative * relative, axis=1, keepdims=True)))
    return -lift_coeff[:, None, :] * rel_speed * relative

def profile(anchor, count, centers):
    cells = (anchor + jnp.arange(count, dtype=jnp.int32)).astype(jnp.float32)
    gap = cells[:, None] - centers[None, :]
    return jnp.exp(-gap * gap / (smear * smear))

def column_weights(centers, row, turbine):
    wx = profile(row * CX, CX, centers[0])
    wy = profile(turbine * CY, CY, centers[1])
    wz = profile(0, NZ, centers[2])
    zx = (wz[:, None, :] * wx[None, :, :]).reshape(NZ * CX, centers.shape[1])
    return (zx, wy)

def reference(velocity, blade_pos, block_turbine, blade_vel, lift_coeff):
    high = lax.Precision.HIGHEST
    row_blocks = N_GY * N_GZ * BLK_OWN
    per_turbine = N_GZ * BLK_OWN
    count = per_turbine * PTS
    turbines = block_turbine.reshape(N_GX, row_blocks).astype(jnp.int32)
    order = jnp.argsort(turbines, axis=1, stable=True).astype(jnp.int32).reshape(N_GX, N_GY, per_turbine)
    positions = blade_pos.reshape(N_GX, row_blocks, 3, PTS)
    row_vel = velocity.reshape(3, NZ, N_GX, CX, NY).transpose(2, 0, 1, 3, 4)
    rows = jnp.arange(N_GX, dtype=jnp.int32)

    def sample_row(items):
        row, vel_row, order_row, pos_row = items
        result = jnp.zeros((row_blocks, 3, PTS), jnp.float32)
        for turbine in range(N_GY):
            picked = order_row[turbine]
            centers = pos_row[picked].transpose(1, 0, 2).reshape(3, count)
            zx, wy = column_weights(centers, row, turbine)
            column = vel_row[:, :, :, turbine * CY:(turbine + 1) * CY].reshape(3 * NZ * CX, CY)
            along = jnp.dot(column, wy, precision=high, preferred_element_type=jnp.float32).reshape(3, NZ * CX, count)
            partial_value = smear_norm * lax.optimization_barrier(jnp.sum(along * zx[None], axis=1))
            partial_value = partial_value.reshape(3, per_turbine, PTS).transpose(1, 0, 2)
            result = result.at[picked].set(partial_value)
        return result
    sampled = lax.map(sample_row, (rows, row_vel, order, positions)).reshape(BLOCKS, 3, PTS)
    point_force = blade_force(sampled, blade_vel, lift_coeff)
    row_force = point_force.reshape(N_GX, row_blocks, 3, PTS)

    def spread_row(items):
        row, order_row, pos_row, force_row = items
        columns = []
        for turbine in range(N_GY):
            picked = order_row[turbine]
            centers = pos_row[picked].transpose(1, 0, 2).reshape(3, count)
            zx, wy = column_weights(centers, row, turbine)
            flat = force_row[picked].transpose(1, 0, 2).reshape(3, count)
            weighted = (smear_norm * flat[:, None, :] * zx[None]).reshape(3 * NZ * CX, count)
            spread = lax.dot_general(weighted, wy, (((1,), (1,)), ((), ())), precision=high, preferred_element_type=jnp.float32)
            columns.append(spread.reshape(3, NZ, CX, CY))
        return jnp.concatenate(columns, axis=3)
    body_rows = lax.map(spread_row, (rows, order, positions, row_force))
    body_force = body_rows.transpose(1, 2, 0, 3, 4).reshape(3, NZ, NX, NY)
    padded = jnp.pad(velocity, ((0, 0), (2, 2), (2, 2), (2, 2)))
    new_velocity = velocity + time_step * tendency(padded, body_force)
    return (new_velocity, point_force)
```

```python
import functools
import math

import jax
import jax.numpy as jnp
import ml_dtypes
import numpy as np
from jax import lax
from jax.experimental import pallas as pl
from jax.experimental.pallas import tpu as pltpu
from jax.sharding import PartitionSpec as P

mean_wind = 1.0
viscosity = 0.2
smag_coeff = 0.17
time_step = 0.2
smear = 2.0
smear_norm = 1.0 / (smear**3 * math.pi**1.5)

F32 = jnp.float32
BF16 = jnp.bfloat16
VMEM_LIMIT = 60 * 1024 * 1024
LEVELS = 8
STEP = 256
SAMPLE_STEP = 512


def split(value):
    high = value.astype(BF16)
    return high, (value - high.astype(F32)).astype(BF16)


def dot(left, right, contract=0):
    return lax.dot_general(
        left, right, (((1,), (contract,)), ((), ())), preferred_element_type=F32
    )


def gaussian(first, count, centers):
    shape = (count, centers.shape[1])
    cells = (first + lax.broadcasted_iota(jnp.int32, shape, 0)).astype(F32)
    gap = cells - centers
    return jnp.exp(-gap * gap / (smear * smear))


def stencil_operator(row_cells):
    inner = (LEVELS + 4) * row_cells
    width = inner + 4 * LEVELS
    op = np.zeros((2, LEVELS, row_cells, width), np.float32)

    def column(level, row):
        if 0 <= row < row_cells:
            return (level + 2) * row_cells + row
        if row < 0:
            return inner + level * 2 + row + 2
        return inner + 2 * LEVELS + level * 2 + row - row_cells

    for level in range(LEVELS):
        for row in range(row_cells):
            for offset, first, second in ((-2, 1, -1), (-1, -8, 16), (1, 8, 16), (2, -1, -1)):
                op[0, level, row, column(level, row + offset)] += first
                op[1, level, row, column(level, row + offset)] += second
                op[1, level, row, column(level + offset, row)] += second
            op[1, level, row, column(level, row)] -= 90
    return op.reshape(2 * LEVELS * row_cells, width).astype(ml_dtypes.bfloat16)


def edges_kernel(vel_ref, head_ref, tail_ref):
    levels, rows = vel_ref.shape[1:3]
    for level in range(levels):
        head_ref[0, 2 * level : 2 * level + 2, :] = vel_ref[0, level, 0:2, :]
        tail_ref[0, 2 * level : 2 * level + 2, :] = vel_ref[0, level, rows - 2 : rows, :]


def edges(velocity, chunk):
    components, _, rows, cols = velocity.shape
    shape = jax.ShapeDtypeStruct((components, 2 * LEVELS, cols), F32)
    return pl.pallas_call(
        edges_kernel,
        grid=(components,),
        in_specs=[pl.BlockSpec((1, LEVELS, rows, cols), lambda i: (i, chunk, 0, 0))],
        out_specs=[pl.BlockSpec((1, 2 * LEVELS, cols), lambda i: (i, 0, 0))] * 2,
        out_shape=[shape, shape],
        compiler_params=pltpu.CompilerParams(vmem_limit_bytes=VMEM_LIMIT),
        name="edges",
    )(velocity)


def find_slots(turb_ref, turbine, per_turbine, slots_ref):
    found = jnp.int32(0)
    for row in range(turb_ref.shape[0]):
        slots_ref[found] = row
        hit = turb_ref[row] == turbine.astype(F32)
        found = found + hit.astype(jnp.int32)
        found = jnp.minimum(found, per_turbine)


def sample_kernel(
    per_turbine, place_ref, turb_ref, table_ref, vel_ref,
    part_ref, own_ref, high_ref, low_ref, slots_ref, acc_ref,
):
    step = pl.program_id(0)
    components, depth, rows, width = vel_ref.shape
    points = table_ref.shape[2]
    count = per_turbine * points

    @pl.when(step == 0)
    def _():
        find_slots(turb_ref, place_ref[1], per_turbine, slots_ref)
        for k in range(per_turbine):
            own_ref[:, k * points : (k + 1) * points] = table_ref[slots_ref[k]]

    first = (place_ref[1] * pl.num_programs(0) + step) * width
    along_y = gaussian(first, width, own_ref[1:2, :])
    high, low = split(along_y)
    high_ref[...] = high
    low_ref[...] = low
    vel_high, vel_low = split(vel_ref[...].reshape(components * depth * rows, width))
    update = dot(vel_high, high) + dot(vel_high, low) + dot(vel_low, high)

    @pl.when(step == 0)
    def _():
        acc_ref[...] = update

    @pl.when(step > 0)
    def _():
        acc_ref[...] += update

    @pl.when(step == pl.num_programs(0) - 1)
    def _():
        along_x = gaussian(place_ref[0] * rows, rows, own_ref[0:1, :])
        along_z = gaussian(place_ref[2] * depth, depth, own_ref[2:3, :])
        for i in range(components):
            total = jnp.zeros((rows, count), F32)
            for level in range(depth):
                at = (i * depth + level) * rows
                total += acc_ref[at : at + rows, :] * along_z[level : level + 1, :]
            part_ref[i : i + 1, :] = smear_norm * jnp.sum(total * along_x, axis=0, keepdims=True)
        part_ref[components:, :] = jnp.zeros((8 - components, count), F32)


def sample(place, turbines, table, velocity, per_turbine):
    components, depth, rows, cols = velocity.shape
    points = table.shape[2]
    count = per_turbine * points
    smem = pl.BlockSpec(memory_space=pltpu.SMEM)
    whole = pl.BlockSpec((8, count), lambda j: (0, 0))
    weight = pl.BlockSpec((SAMPLE_STEP, count), lambda j: (j, 0))
    return pl.pallas_call(
        functools.partial(sample_kernel, per_turbine),
        grid=(cols // SAMPLE_STEP,),
        in_specs=[
            smem,
            smem,
            pl.BlockSpec(table.shape, lambda j: (0, 0, 0)),
            pl.BlockSpec((components, depth, rows, SAMPLE_STEP), lambda j: (0, 0, 0, j)),
        ],
        out_specs=[whole, whole, weight, weight],
        out_shape=[
            jax.ShapeDtypeStruct((8, count), F32),
            jax.ShapeDtypeStruct((8, count), F32),
            jax.ShapeDtypeStruct((cols, count), BF16),
            jax.ShapeDtypeStruct((cols, count), BF16),
        ],
        scratch_shapes=[
            pltpu.SMEM((per_turbine + 1,), jnp.int32),
            pltpu.VMEM((components * depth * rows, count), F32),
        ],
        compiler_params=pltpu.CompilerParams(vmem_limit_bytes=VMEM_LIMIT),
        name="sample",
    )(place, turbines, table, velocity)


def force_kernel(
    per_turbine, owned, place_ref, turb_ref, mine_ref, other_ref, own_ref,
    force_ref, home_ref, slots_ref,
):
    find_slots(turb_ref, place_ref[1], per_turbine, slots_ref)
    points = own_ref.shape[1] // per_turbine
    relative = mine_ref[0:3, :] + other_ref[0:3, :] - own_ref[3:6, :]
    speed = jnp.sqrt(jnp.sum(relative * relative, axis=0, keepdims=True))
    force = -own_ref[6:7, :] * speed * relative
    force_ref[...] = jnp.zeros(force_ref.shape, F32)
    force_ref[0:3, :] = force
    home_ref[...] = jnp.zeros(home_ref.shape, F32)
    group = 2 * owned
    for k in range(per_turbine):
        slot = slots_ref[k]
        shift = slot // group
        at = slot - shift * group - place_ref[2] * owned

        @pl.when((at >= 0) & (at < owned))
        def _():
            home_ref[shift, at, 0:3, :] = force[:, k * points : (k + 1) * points]


def point_forces(place, turbines, mine, other, own, per_turbine, owned):
    count = own.shape[1]
    points = count // per_turbine
    shifts = turbines.shape[0] // (2 * owned)
    smem = pl.BlockSpec(memory_space=pltpu.SMEM)
    return pl.pallas_call(
        functools.partial(force_kernel, per_turbine, owned),
        in_specs=[smem, smem] + [pl.BlockSpec(memory_space=pltpu.VMEM)] * 3,
        out_specs=[pl.BlockSpec(memory_space=pltpu.VMEM)] * 2,
        out_shape=[
            jax.ShapeDtypeStruct((8, count), F32),
            jax.ShapeDtypeStruct((shifts, owned, 8, points), F32),
        ],
        scratch_shapes=[pltpu.SMEM((per_turbine + 1,), jnp.int32)],
        name="force",
    )(place, turbines, mine, other, own)


def update_kernel(
    chunk, chunks, place_ref, own_ref, force_ref, op_ref, prev_ref, next_ref, high_ref, low_ref,
    vel_ref, lev_ref, left_ref, right_ref, *rest,
):
    out_ref, pad_ref, wide_high, wide_low, grad_ref, lap_ref, body_ref, sems, edge_sems = rest[-9:]
    step = pl.program_id(0)
    steps = pl.num_programs(0)
    components, _, rows, cols = vel_ref.shape
    cells = LEVELS * rows
    low_level = 2 if chunk == 0 else 0
    high_level = LEVELS + 2 if chunk == chunks - 1 else LEVELS + 4
    source = chunk * LEVELS - 2 + low_level
    levels = high_level - low_level

    def column_copy(at):
        return pltpu.make_async_copy(
            vel_ref.at[:, pl.ds(source, levels), :, pl.ds(pl.multiple_of(at * STEP, STEP), STEP)],
            pad_ref.at[:, pl.ds(low_level, levels), :, pl.ds(pl.multiple_of(at * STEP + 128, 128), STEP)],
            sems.at[at],
        )

    left_copy = pltpu.make_async_copy(
        left_ref.at[:, pl.ds(chunk * LEVELS, LEVELS)],
        pad_ref.at[:, pl.ds(2, LEVELS), :, pl.ds(0, 128)],
        edge_sems.at[0],
    )
    right_copy = pltpu.make_async_copy(
        right_ref.at[:, pl.ds(chunk * LEVELS, LEVELS)],
        pad_ref.at[:, pl.ds(2, LEVELS), :, pl.ds(cols + 128, 128)],
        edge_sems.at[1],
    )

    def level_edge(at, core, sem):
        copy = pltpu.make_async_copy(
            lev_ref, pad_ref.at[:, pl.ds(at, 2), :, pl.ds(128, cols)], edge_sems.at[sem]
        )

        @pl.when(place_ref[2] == core)
        def _():
            copy.start()
            copy.wait()

        @pl.when(place_ref[2] != core)
        def _():
            pad_ref[:, at : at + 2, :, 128 : cols + 128] = jnp.zeros((components, 2, rows, cols), F32)

    @pl.when(step == 0)
    def _():
        column_copy(0).start()
        left_copy.start()
        column_copy(1).start()
        for at in range(2, cols // STEP):
            column_copy(at).start()
        right_copy.start()
        if chunk == 0:
            level_edge(0, 1, 2)
        if chunk == chunks - 1:
            level_edge(LEVELS + 2, 0, 3)
        along_x = gaussian(place_ref[0] * rows, rows, own_ref[0:1, :])
        first = (place_ref[2] * chunks + chunk) * LEVELS
        along_z = gaussian(first, LEVELS, own_ref[2:3, :])
        for i in range(components):
            scaled = (time_step * smear_norm) * force_ref[i : i + 1, :] * along_x
            for level in range(LEVELS):
                at = i * cells + level * rows
                high, low = split(scaled * along_z[level : level + 1, :])
                wide_high[at : at + rows, :] = high
                wide_low[at : at + rows, :] = low
        left_copy.wait()
        column_copy(0).wait()

    @pl.when(step < steps - 1)
    def _():
        column_copy(step + 1).wait()

    @pl.when(step == steps - 1)
    def _():
        right_copy.wait()

    base = pl.multiple_of(step * STEP, STEP)
    center = pl.ds(pl.multiple_of(step * STEP + 128, 128), STEP)
    op = op_ref[...]
    for i in range(components):
        inner = pad_ref[i, :, :, center].reshape((LEVELS + 4) * rows, STEP)
        inner_high, inner_low = split(inner)
        prev_high, prev_low = split(prev_ref[i])
        next_high, next_low = split(next_ref[i])
        result = dot(op, jnp.concatenate([inner_high, prev_high, next_high], axis=0))
        result += dot(op, jnp.concatenate([inner_low, prev_low, next_low], axis=0))
        grad_ref[i] = result[:cells].reshape(LEVELS, rows, STEP)
        lap_ref[i] = result[cells:].reshape(LEVELS, rows, STEP)
    high = high_ref[...]
    body = dot(wide_high[...], high, 1) + dot(wide_low[...], high, 1) + dot(wide_high[...], low_ref[...], 1)
    body_ref[...] = body.reshape(components, LEVELS, rows, STEP)

    for level in range(LEVELS):
        along_y, lap, along_z = [], [], []
        for i in range(components):
            window = pad_ref[i, level + 2, :, pl.ds(base, STEP + 256)]
            width = STEP + 256
            middle = window[:, 128 : STEP + 128]
            ahead = pltpu.roll(window, width - 1, 1)[:, 128 : STEP + 128]
            behind = pltpu.roll(window, 1, 1)[:, 128 : STEP + 128]
            ahead2 = pltpu.roll(window, width - 2, 1)[:, 128 : STEP + 128]
            behind2 = pltpu.roll(window, 2, 1)[:, 128 : STEP + 128]
            along_y.append(8.0 * (ahead - behind) - (ahead2 - behind2))
            lap.append(lap_ref[i, level] + (16.0 * (ahead + behind) - (ahead2 + behind2)))
            near = pad_ref[i, level + 3, :, center] - pad_ref[i, level + 1, :, center]
            far = pad_ref[i, level + 4, :, center] - pad_ref[i, level, :, center]
            along_z.append(8.0 * near - far)
        along_x = [grad_ref[i, level] for i in range(components)]
        same = along_x[0] * along_x[0] + along_y[1] * along_y[1] + along_z[2] * along_z[2]
        xy = along_x[1] + along_y[0]
        xz = along_x[2] + along_z[0]
        yz = along_y[2] + along_z[1]
        strain = 2.0 * same + (xy * xy + xz * xz + yz * yz)
        mixing = viscosity + (smag_coeff * smag_coeff / 12.0) * jnp.sqrt(strain)
        for i in range(components):
            change = mixing * lap[i] - mean_wind * along_x[i]
            out_ref[i, level] = (
                pad_ref[i, level + 2, :, center] + (time_step / 12.0) * change + body_ref[i, level]
            )


def update(chunk, chunks, place, own, force, operator, prev, after, high, low, velocity, lev, left, right, partial):
    components, depth, rows, cols = velocity.shape
    count = own.shape[1]
    cells = LEVELS * rows
    smem = pl.BlockSpec(memory_space=pltpu.SMEM)
    hbm = pl.BlockSpec(memory_space=pl.ANY)
    whole = pl.BlockSpec((8, count), lambda j: (0, 0))
    side = pl.BlockSpec((components, 2 * LEVELS, STEP), lambda j: (0, 0, j))
    weight = pl.BlockSpec((STEP, count), lambda j: (j, 0))
    operands = [place, own, force, operator, prev, after, high, low, velocity, lev, left, right]
    in_specs = [smem, whole, whole, pl.BlockSpec(operator.shape, lambda j: (0, 0)), side, side, weight, weight]
    in_specs += [hbm] * 4
    aliases = {}
    if partial is not None:
        aliases = {len(operands): 0}
        operands.append(partial)
        in_specs.append(hbm)
    field = pltpu.VMEM((components, LEVELS, rows, STEP), F32)
    return pl.pallas_call(
        functools.partial(update_kernel, chunk, chunks),
        grid=(cols // STEP,),
        in_specs=in_specs,
        out_specs=pl.BlockSpec((components, LEVELS, rows, STEP), lambda j: (0, chunk, 0, j)),
        out_shape=jax.ShapeDtypeStruct(velocity.shape, F32),
        scratch_shapes=[
            pltpu.VMEM((components, LEVELS + 4, rows, cols + 256), F32),
            pltpu.VMEM((components * cells, count), BF16),
            pltpu.VMEM((components * cells, count), BF16),
            field,
            field,
            field,
            pltpu.SemaphoreType.DMA((cols // STEP,)),
            pltpu.SemaphoreType.DMA((4,)),
        ],
        input_output_aliases=aliases,
        compiler_params=pltpu.CompilerParams(vmem_limit_bytes=VMEM_LIMIT),
        name="update",
    )(*operands)


def local(velocity, blade_pos, block_turbine, blade_vel, lift_coeff):
    components, depth, rows, cols = velocity.shape
    owned, _, points = blade_pos.shape
    gx, gy, gz = (lax.axis_size(axis) for axis in ("gx", "gy", "gz"))
    assert gz == 2 and depth % LEVELS == 0
    core = lax.axis_index("gz")
    place = jnp.stack([lax.axis_index(axis) for axis in ("gx", "gy", "gz")]).astype(jnp.int32)
    per_turbine = owned * gz
    chunks = depth // LEVELS
    swap = [(0, 1), (1, 0)]
    up_x = [(i, i + 1) for i in range(gx - 1)]
    down_x = [(i + 1, i) for i in range(gx - 1)]
    up_y = [(i, i + 1) for i in range(gy - 1)]
    down_y = [(i + 1, i) for i in range(gy - 1)]

    packed = jnp.concatenate(
        [
            blade_pos,
            blade_vel,
            lift_coeff[:, None, :],
            jnp.broadcast_to(block_turbine.astype(F32)[:, None, None], (owned, 1, points)),
        ],
        axis=1,
    )
    twin = lax.ppermute(packed, "gz", swap)
    pair = jnp.where(
        core == 0, jnp.concatenate([packed, twin], axis=0), jnp.concatenate([twin, packed], axis=0)
    )

    before, after = [], []
    for chunk in range(chunks):
        head, tail = edges(velocity, chunk)
        before.append(lax.ppermute(tail, "gx", up_x))
        after.append(lax.ppermute(head, "gx", down_x))

    parts = [pair]
    for shift in range(1, gy):
        parts.append(lax.ppermute(pair, "gy", [(i, (i + shift) % gy) for i in range(gy)]))
    table = jnp.concatenate(parts, axis=0)
    turbines = table[:, 7, 0]

    facing = lax.dynamic_slice_in_dim(velocity, jnp.where(core == 0, depth - 2, 0), 2, axis=1)
    lev = lax.ppermute(facing, "gz", swap)
    left = lax.ppermute(velocity[..., cols - 128 :], "gy", up_y)
    right = lax.ppermute(velocity[..., :128], "gy", down_y)

    mine, own, high, low = sample(place, turbines, table, velocity, per_turbine)
    other = lax.ppermute(mine, "gz", swap)
    force, home = point_forces(place, turbines, mine, other, own, per_turbine, owned)
    result = home[0]
    for shift in range(1, gy):
        result += lax.ppermute(home[shift], "gy", [((i + shift) % gy, i) for i in range(gy)])

    operator = jnp.asarray(stencil_operator(rows))
    new_velocity = None
    for chunk in range(chunks):
        new_velocity = update(
            chunk, chunks, place, own, force, operator, before[chunk], after[chunk],
            high, low, velocity, lev, left, right, new_velocity,
        )
    return (new_velocity, result[:, :3, :])


def solution(mesh):
    in_specs = (
        P(None, "gz", "gx", "gy"),
        P(("gx", "gy", "gz"), None, None),
        P(("gx", "gy", "gz")),
        P(("gx", "gy", "gz"), None, None),
        P(("gx", "gy", "gz"), None),
    )
    out_specs = (P(None, "gz", "gx", "gy"), P(("gx", "gy", "gz"), None, None))
    return jax.shard_map(local, mesh=mesh, in_specs=in_specs, out_specs=out_specs, check_vma=False)
```

```python
import functools
import math

import jax
import jax.numpy as jnp
import ml_dtypes
import numpy as np
from jax import lax
from jax.experimental import pallas as pl
from jax.experimental.pallas import tpu as pltpu
from jax.sharding import PartitionSpec as P

mean_wind = 1.0
viscosity = 0.2
smag_coeff = 0.17
time_step = 0.2
smear = 2.0
smear_norm = 1.0 / (smear**3 * math.pi**1.5)

F32 = jnp.float32
BF16 = jnp.bfloat16
MIB = 1024 * 1024
LEVELS = 8
STEP = 256
LIGHT = pl.CostEstimate(flops=0, bytes_accessed=0, transcendentals=0)


def split(value):
    high = value.astype(BF16)
    return high, (value - high.astype(F32)).astype(BF16)


def dot(left, right, contract=0):
    return lax.dot_general(
        left, right, (((1,), (contract,)), ((), ())), preferred_element_type=F32
    )


def gaussian(first, count, centers):
    shape = (count, centers.shape[1])
    cells = (first + lax.broadcasted_iota(jnp.int32, shape, 0)).astype(F32)
    gap = cells - centers
    return jnp.exp(-gap * gap / (smear * smear))


def stencil_operator(row_cells):
    inner = (LEVELS + 4) * row_cells
    width = inner + 4 * LEVELS
    op = np.zeros((2, LEVELS, row_cells, width), np.float32)

    def column(level, row):
        if 0 <= row < row_cells:
            return (level + 2) * row_cells + row
        if row < 0:
            return inner + level * 2 + row + 2
        return inner + 2 * LEVELS + level * 2 + row - row_cells

    for level in range(LEVELS):
        for row in range(row_cells):
            for offset, first, second in ((-2, 1, -1), (-1, -8, 16), (1, 8, 16), (2, -1, -1)):
                op[0, level, row, column(level, row + offset)] += first
                op[1, level, row, column(level, row + offset)] += second
                op[1, level, row, column(level + offset, row)] += second
            op[1, level, row, column(level, row)] -= 90
    op = op.reshape(2 * LEVELS * row_cells, width)
    op = np.pad(op, ((0, 0), (0, -width % 128)))
    return np.concatenate([op, op], axis=1).astype(ml_dtypes.bfloat16)


def prep_kernel(
    turb_ref, pos_ref, speed_ref, lift_ref, vel_ref, up_ref, down_ref, lev_ref, *sides
):
    component = pl.program_id(0)
    levels, rows, cols = vel_ref.shape[1:]
    owned, coords, points = pos_ref.shape
    heads, tails = sides[: len(sides) // 2], sides[len(sides) // 2 :]

    @pl.when(component == 0)
    def _():
        for ref in (up_ref, down_ref):
            for k in range(owned):
                ref[k, 0:coords, :] = pos_ref[k]
                ref[k, coords : 2 * coords, :] = speed_ref[k]
                ref[k, 2 * coords : 2 * coords + 1, :] = lift_ref[k : k + 1, :]
                ref[k, 7:8, :] = jnp.full((1, points), turb_ref[k].astype(F32))

    lev_ref[0] = vel_ref[0, pl.ds(jnp.where(lax.axis_index("gz") == 0, levels - 2, 0), 2)]
    parts = levels * rows // 128
    last = vel_ref[0, :, :, cols - 128 :].reshape(levels * rows, 128)
    first = vel_ref[0, :, :, :128].reshape(levels * rows, 128)
    for part in range(parts):
        cells = slice(part * 128, part * 128 + 128)
        up_ref[owned + component * parts + part] = last[cells].T[120:]
        down_ref[owned + component * parts + part] = first[cells].T[:8]

    row = lax.broadcasted_iota(jnp.int32, (8, cols), 0) // 2
    for group in range(levels // 4):
        at = (group * 4) // LEVELS
        to = (group * 8) % (2 * LEVELS)
        head = tail = None
        for k in range(4):
            top = vel_ref[0, group * 4 + k, 0:8, :]
            end = vel_ref[0, group * 4 + k, rows - 8 : rows, :]
            if k:
                top = pltpu.roll(top, 2 * k, 0)
            if k < 3:
                end = pltpu.roll(end, 2 * k + 2, 0)
            head = top if head is None else jnp.where(row == k, top, head)
            tail = end if tail is None else jnp.where(row == k, end, tail)
        heads[at][0, to : to + 8, :] = head
        tails[at][0, to : to + 8, :] = tail


def prep(velocity, blade_pos, block_turbine, blade_vel, lift_coeff):
    components, levels, rows, cols = velocity.shape
    owned, coords, points = blade_pos.shape
    chunks = levels // LEVELS
    tiles = owned + components * levels * rows // 128
    whole = pl.BlockSpec((owned, coords, points), lambda i: (0, 0, 0))
    message = pl.BlockSpec((tiles, 8, 128), lambda i: (0, 0, 0))
    side = pl.BlockSpec((1, 2 * LEVELS, cols), lambda i: (i, 0, 0))
    side_shape = jax.ShapeDtypeStruct((components, 2 * LEVELS, cols), F32)
    return pl.pallas_call(
        prep_kernel,
        grid=(components,),
        in_specs=[
            pl.BlockSpec(memory_space=pltpu.SMEM),
            whole,
            whole,
            pl.BlockSpec((owned, points), lambda i: (0, 0)),
            pl.BlockSpec((1, levels, rows, cols), lambda i: (i, 0, 0, 0)),
        ],
        out_specs=[
            message,
            message,
            pl.BlockSpec((1, 2, rows, cols), lambda i: (i, 0, 0, 0)),
        ] + [side] * (2 * chunks),
        out_shape=[
            jax.ShapeDtypeStruct((tiles, 8, 128), F32),
            jax.ShapeDtypeStruct((tiles, 8, 128), F32),
            jax.ShapeDtypeStruct((components, 2, rows, cols), F32),
        ] + [side_shape] * (2 * chunks),
        compiler_params=pltpu.CompilerParams(vmem_limit_bytes=24 * MIB),
        cost_estimate=LIGHT,
        name="prep",
    )(block_turbine, blade_pos, blade_vel, lift_coeff, velocity)


def match(mine_ref, twin_ref, per_turbine):
    core = lax.axis_index("gz")
    turbine = lax.axis_index("gy").astype(F32)
    half = mine_ref.shape[0]
    first = [(mine_ref[k, 7:8, :] == turbine).astype(F32) for k in range(half)]
    second = [(twin_ref[k, 7:8, :] == turbine).astype(F32) for k in range(half)]
    masks = []
    for hits, others, leads in ((first, second, core == 0), (second, first, core == 1)):
        rank = jnp.where(leads, jnp.zeros_like(hits[0]), sum(others))
        for hit in hits:
            masks.append([(hit > 0.5) & (rank == k) for k in range(per_turbine)])
            rank = rank + hit
    return masks


def sample_kernel(
    per_turbine, mine_ref, twin_ref, vel_ref, part_ref, own_ref, weight_ref, even_ref, odd_ref, acc_ref
):
    step = pl.program_id(0)
    steps = pl.num_programs(0)
    components, depth, rows, width = vel_ref.shape
    points = mine_ref.shape[2]
    count = per_turbine * points
    half = width // 2
    start = lax.axis_index("gy") * steps * width

    def weights(at, ref):
        high, low = split(gaussian(start + at * half, half, own_ref[1:2, :]))
        ref[:, :count] = high
        ref[:, count:] = low

    def multiply(side, ref):
        cells = vel_ref[:, :, :, side * half : side * half + half]
        high, low = split(cells.reshape(components * depth * rows, half))
        acc_ref[...] += dot(
            jnp.concatenate([high, high, low], axis=1),
            jnp.concatenate([ref[:, :count], ref[:, count:], ref[:, :count]], axis=0),
        )
        weight_ref[side * half : side * half + half, :] = ref[...]

    @pl.when(step == 0)
    def _():
        masks = match(mine_ref, twin_ref, per_turbine)
        blocks = mine_ref.shape[0]
        for k in range(per_turbine):
            total = jnp.zeros((8, points), F32)
            for row, mask in enumerate(masks):
                tile = mine_ref[row] if row < blocks else twin_ref[row - blocks]
                total = jnp.where(mask[k], tile, total)
            own_ref[:, k * points : (k + 1) * points] = total
        weights(0, even_ref)
        acc_ref[...] = jnp.zeros(acc_ref.shape, F32)

    weights(2 * step + 1, odd_ref)
    multiply(0, even_ref)
    weights(2 * step + 2, even_ref)
    multiply(1, odd_ref)

    @pl.when(step == steps - 1)
    def _():
        along_x = gaussian(lax.axis_index("gx") * rows, rows, own_ref[0:1, :])
        along_z = gaussian(lax.axis_index("gz") * depth, depth, own_ref[2:3, :])
        for i in range(components):
            total = jnp.zeros((rows, count), F32)
            for level in range(depth):
                at = (i * depth + level) * rows
                total += acc_ref[at : at + rows, :] * along_z[level : level + 1, :]
            part_ref[i : i + 1, :] = smear_norm * jnp.sum(total * along_x, axis=0, keepdims=True)
        part_ref[components:, :] = jnp.zeros((8 - components, count), F32)


def sample(mine, twin, velocity, per_turbine):
    components, depth, rows, cols = velocity.shape
    points = mine.shape[2]
    count = per_turbine * points
    whole = pl.BlockSpec((8, count), lambda j: (0, 0))
    table = pl.BlockSpec(mine.shape, lambda j: (0, 0, 0))
    return pl.pallas_call(
        functools.partial(sample_kernel, per_turbine),
        grid=(cols // (2 * STEP),),
        in_specs=[
            table,
            table,
            pl.BlockSpec((components, depth, rows, 2 * STEP), lambda j: (0, 0, 0, j)),
        ],
        out_specs=[whole, whole, pl.BlockSpec((2 * STEP, 2 * count), lambda j: (j, 0))],
        out_shape=[
            jax.ShapeDtypeStruct((8, count), F32),
            jax.ShapeDtypeStruct((8, count), F32),
            jax.ShapeDtypeStruct((cols, 2 * count), BF16),
        ],
        scratch_shapes=[
            pltpu.VMEM((STEP, 2 * count), BF16),
            pltpu.VMEM((STEP, 2 * count), BF16),
            pltpu.VMEM((components * depth * rows, count), F32),
        ],
        compiler_params=pltpu.CompilerParams(vmem_limit_bytes=40 * MIB),
        cost_estimate=LIGHT,
        name="sample",
    )(mine, twin, velocity)


def force_kernel(
    per_turbine, owned, mine_ref, twin_ref, part_ref, other_ref, own_ref, force_ref, home_ref
):
    points = own_ref.shape[1] // per_turbine
    relative = part_ref[0:3, :] + other_ref[0:3, :] - own_ref[3:6, :]
    speed = jnp.sqrt(jnp.sum(relative * relative, axis=0, keepdims=True))
    force = -own_ref[6:7, :] * speed * relative
    force_ref[...] = jnp.zeros(force_ref.shape, F32)
    force_ref[0:3, :] = force
    masks = match(mine_ref, twin_ref, per_turbine)
    for row in range(mine_ref.shape[0]):
        total = jnp.zeros((3, points), F32)
        for k in range(per_turbine):
            total = jnp.where(masks[row][k], force[:, k * points : (k + 1) * points], total)
        home_ref[row // owned, row % owned, 0:3, :] = total
        home_ref[row // owned, row % owned, 3:8, :] = jnp.zeros((5, points), F32)


def point_forces(mine, twin, part, other, own, per_turbine, owned):
    count = own.shape[1]
    points = count // per_turbine
    shifts = mine.shape[0] // owned
    return pl.pallas_call(
        functools.partial(force_kernel, per_turbine, owned),
        in_specs=[pl.BlockSpec(memory_space=pltpu.VMEM)] * 5,
        out_specs=[pl.BlockSpec(memory_space=pltpu.VMEM)] * 2,
        out_shape=[
            jax.ShapeDtypeStruct((8, count), F32),
            jax.ShapeDtypeStruct((shifts, owned, 8, points), F32),
        ],
        cost_estimate=LIGHT,
        name="force",
    )(mine, twin, part, other, own)


def update_kernel(chunk, chunks, *refs):
    own_ref, force_ref, op_ref = refs[:3]
    prev_refs, next_refs, weight_refs = refs[3:6], refs[6:9], refs[9:12]
    vel_ref, lev_ref, left_ref, right_ref = refs[12:16]
    out_ref, pad_ref, wide_ref, even, odd, sems, edge_sems = refs[-7:]
    step = pl.program_id(0)
    steps = pl.num_programs(0)
    components, _, rows, cols = vel_ref.shape
    count = own_ref.shape[1]
    cells = LEVELS * rows
    inner = (LEVELS + 4) * rows
    fill = op_ref.shape[1] // 2 - inner - 4 * LEVELS
    blocks = cols // STEP
    low_level = 2 if chunk == 0 else 0
    high_level = LEVELS + 2 if chunk == chunks - 1 else LEVELS + 4
    source = chunk * LEVELS - 2 + low_level
    levels = high_level - low_level

    def column_copy(at):
        return pltpu.make_async_copy(
            vel_ref.at[:, pl.ds(source, levels), :, pl.ds(pl.multiple_of(at * STEP, STEP), STEP)],
            pad_ref.at[:, pl.ds(low_level, levels), :, pl.ds(pl.multiple_of(at * STEP + 128, 128), STEP)],
            sems.at[at],
        )

    def level_edge(at, core, sem):
        copy = pltpu.make_async_copy(
            lev_ref, pad_ref.at[:, pl.ds(at, 2), :, pl.ds(128, cols)], edge_sems.at[sem]
        )

        @pl.when(lax.axis_index("gz") == core)
        def _():
            copy.start()
            copy.wait()

        @pl.when(lax.axis_index("gz") != core)
        def _():
            pad_ref[:, at : at + 2, :, 128 : cols + 128] = jnp.zeros((components, 2, rows, cols), F32)

    def side_columns(ref, present, lane):
        per_part = 128 // rows
        parts = ref.shape[0] // components
        for i in range(components):
            for level in range(LEVELS):
                at = chunk * LEVELS + level
                tile = jnp.where(present, ref[i * parts + at // per_part], 0.0)
                if level % per_part == 0 or level == 0:
                    turned = tile.T
                row = (at % per_part) * rows
                pad_ref[i, level + 2, :, lane : lane + 8] = turned[row : row + rows, :]

    def matrix_part(at, which, bufs):
        grad_ref, lap_ref, body_ref = bufs
        center = pl.ds(pl.multiple_of(at * STEP + 128, 128), STEP)
        op = op_ref[...]
        empty = [jnp.zeros((fill, STEP), BF16)] if fill else []
        for i in range(components):
            inner_high, inner_low = split(pad_ref[i, :, :, center].reshape(inner, STEP))
            prev_high, prev_low = split(prev_refs[which][i])
            next_high, next_low = split(next_refs[which][i])
            high = [inner_high, prev_high, next_high] + empty
            low = [inner_low, prev_low, next_low] + empty
            result = dot(op, jnp.concatenate(high + low, axis=0))
            grad_ref[i] = result[:cells].reshape(LEVELS, rows, STEP)
            lap_ref[i] = result[cells:].reshape(LEVELS, rows, STEP)
        high = weight_refs[which][:, :count]
        low = weight_refs[which][:, count:]
        body = dot(wide_ref[...], jnp.concatenate([high, high, low], axis=1), 1)
        body_ref[...] = body.reshape(components, LEVELS, rows, STEP)

    def vector_part(at, bufs, lane):
        grad_ref, lap_ref, body_ref = bufs
        base = pl.multiple_of(at * STEP, STEP)
        center = pl.ds(pl.multiple_of(at * STEP + 128, 128), STEP)
        width = STEP + 256
        for level in range(LEVELS):
            for row in range(0, rows, 8):
                band = slice(row, row + 8)
                along_y, lap, along_z = [], [], []
                for i in range(components):
                    window = pad_ref[i, level + 2, band, pl.ds(base, width)]
                    ahead = pltpu.roll(window, width - 1, 1)[:, 128 : STEP + 128]
                    behind = pltpu.roll(window, 1, 1)[:, 128 : STEP + 128]
                    ahead2 = pltpu.roll(window, width - 2, 1)[:, 128 : STEP + 128]
                    behind2 = pltpu.roll(window, 2, 1)[:, 128 : STEP + 128]
                    along_y.append(8.0 * (ahead - behind) - (ahead2 - behind2))
                    lap.append(lap_ref[i, level, band] + (16.0 * (ahead + behind) - (ahead2 + behind2)))
                    near = pad_ref[i, level + 3, band, center] - pad_ref[i, level + 1, band, center]
                    far = pad_ref[i, level + 4, band, center] - pad_ref[i, level, band, center]
                    along_z.append(8.0 * near - far)
                along_x = [grad_ref[i, level, band] for i in range(components)]
                same = along_x[0] * along_x[0] + along_y[1] * along_y[1] + along_z[2] * along_z[2]
                xy = along_x[1] + along_y[0]
                xz = along_x[2] + along_z[0]
                yz = along_y[2] + along_z[1]
                strain = 2.0 * same + (xy * xy + xz * xz + yz * yz)
                mixing = viscosity + (smag_coeff * smag_coeff / 12.0) * jnp.sqrt(strain)
                for i in range(components):
                    change = mixing * lap[i] - mean_wind * along_x[i]
                    out_ref[i, level, band, lane : lane + STEP] = (
                        pad_ref[i, level + 2, band, center]
                        + (time_step / 12.0) * change
                        + body_ref[i, level, band]
                    )

    @pl.when(step == 0)
    def _():
        for at in range(blocks):
            column_copy(at).start()
        if chunk == 0:
            level_edge(0, 1, 0)
        if chunk == chunks - 1:
            level_edge(LEVELS + 2, 0, 1)
        turbine = lax.axis_index("gy")
        side_columns(left_ref, turbine > 0, 120)
        side_columns(right_ref, turbine < lax.axis_size("gy") - 1, cols + 128)
        along_x = gaussian(lax.axis_index("gx") * rows, rows, own_ref[0:1, :])
        first = (lax.axis_index("gz") * chunks + chunk) * LEVELS
        along_z = gaussian(first, LEVELS, own_ref[2:3, :])
        for i in range(components):
            scaled = (time_step * smear_norm) * force_ref[i : i + 1, :] * along_x
            for level in range(LEVELS):
                band = pl.ds(i * cells + level * rows, rows)
                high, low = split(scaled * along_z[level : level + 1, :])
                wide_ref[band, :count] = high
                wide_ref[band, count : 2 * count] = low
                wide_ref[band, 2 * count :] = high
        column_copy(0).wait()
        matrix_part(0, 0, even)

    column_copy(2 * step + 1).wait()

    @pl.when(step < steps - 1)
    def _():
        column_copy(2 * step + 2).wait()

    matrix_part(2 * step + 1, 1, odd)
    vector_part(2 * step, even, 0)
    matrix_part(jnp.minimum(2 * step + 2, blocks - 1), 2, even)
    vector_part(2 * step + 1, odd, STEP)


def update(chunk, chunks, own, force, operator, prev, after, weight, velocity, lev, left, right, partial):
    components, depth, rows, cols = velocity.shape
    count = own.shape[1]
    cells = LEVELS * rows
    blocks = cols // STEP
    hbm = pl.BlockSpec(memory_space=pl.ANY)
    places = [lambda j: 0, lambda j: 2 * j + 1, lambda j: jnp.minimum(2 * j + 2, blocks - 1)]
    whole = pl.BlockSpec((8, count), lambda j: (0, 0))
    sides = [
        pl.BlockSpec((components, 2 * LEVELS, STEP), lambda j, at=at: (0, 0, at(j))) for at in places
    ]
    weights = [pl.BlockSpec((STEP, 2 * count), lambda j, at=at: (at(j), 0)) for at in places]
    column = pl.BlockSpec(left.shape, lambda j: (0, 0, 0))
    operands = [own, force, operator] + [prev] * 3 + [after] * 3 + [weight] * 3
    operands += [velocity, lev, left, right]
    in_specs = [whole, whole, pl.BlockSpec(operator.shape, lambda j: (0, 0))]
    in_specs += sides + sides + weights + [hbm, hbm, column, column]
    aliases = {}
    if partial is not None:
        aliases = {len(operands): 0}
        operands.append(partial)
        in_specs.append(hbm)
    fields = [pltpu.VMEM((components, LEVELS, rows, STEP), F32)] * 3
    return pl.pallas_call(
        functools.partial(update_kernel, chunk, chunks),
        grid=(blocks // 2,),
        in_specs=in_specs,
        out_specs=pl.BlockSpec((components, LEVELS, rows, 2 * STEP), lambda j: (0, chunk, 0, j)),
        out_shape=jax.ShapeDtypeStruct(velocity.shape, F32),
        scratch_shapes=[
            pltpu.VMEM((components, LEVELS + 4, rows, cols + 256), F32),
            pltpu.VMEM((components * cells, 3 * count), BF16),
            fields,
            fields,
            pltpu.SemaphoreType.DMA((blocks,)),
            pltpu.SemaphoreType.DMA((2,)),
        ],
        input_output_aliases=aliases,
        compiler_params=pltpu.CompilerParams(vmem_limit_bytes=40 * MIB),
        cost_estimate=LIGHT,
        name="update",
    )(*operands)


def local(velocity, blade_pos, block_turbine, blade_vel, lift_coeff):
    components, depth, rows, cols = velocity.shape
    owned, _, points = blade_pos.shape
    gx, gy, gz = (lax.axis_size(axis) for axis in ("gx", "gy", "gz"))
    assert gz == 2 and depth % LEVELS == 0
    per_turbine = owned * gz
    chunks = depth // LEVELS
    swap = [(0, 1), (1, 0)]
    up_x = [(i, i + 1) for i in range(gx - 1)]
    down_x = [(i + 1, i) for i in range(gx - 1)]

    def around(shift):
        return [(i, (i + shift) % gy) for i in range(gy)]

    up, down, facing, *sides = prep(velocity, blade_pos, block_turbine, blade_vel, lift_coeff)
    before = [lax.ppermute(tail, "gx", up_x) for tail in sides[chunks:]]
    after = [lax.ppermute(head, "gx", down_x) for head in sides[:chunks]]
    left = lax.ppermute(up, "gy", around(1))
    right = lax.ppermute(down, "gy", around(gy - 1))
    blocks = up[:owned]
    parts = [blocks, left[:owned]]
    parts += [lax.ppermute(blocks, "gy", around(shift)) for shift in range(2, gy - 1)]
    parts.append(right[:owned])
    mine = jnp.concatenate(parts, axis=0)
    twin = lax.ppermute(mine, "gz", swap)
    lev = lax.ppermute(facing, "gz", swap)

    part, own, weight = sample(mine, twin, velocity, per_turbine)
    other = lax.ppermute(part, "gz", swap)
    force, home = point_forces(mine, twin, part, other, own, per_turbine, owned)
    result = home[0]
    for shift in range(1, gy):
        result += lax.ppermute(home[shift], "gy", around(gy - shift))

    operator = jnp.asarray(stencil_operator(rows))
    new_velocity = None
    for chunk in range(chunks):
        new_velocity = update(
            chunk, chunks, own, force, operator, before[chunk], after[chunk],
            weight, velocity, lev, left[owned:], right[owned:], new_velocity,
        )
    return (new_velocity, result[:, :3, :])


def solution(mesh):
    in_specs = (
        P(None, "gz", "gx", "gy"),
        P(("gx", "gy", "gz"), None, None),
        P(("gx", "gy", "gz")),
        P(("gx", "gy", "gz"), None, None),
        P(("gx", "gy", "gz"), None),
    )
    out_specs = (P(None, "gz", "gx", "gy"), P(("gx", "gy", "gz"), None, None))
    return jax.shard_map(local, mesh=mesh, in_specs=in_specs, out_specs=out_specs, check_vma=False)
```

```python
import functools
import math

import jax
import jax.numpy as jnp
import ml_dtypes
import numpy as np
from jax import lax
from jax.experimental import pallas as pl
from jax.experimental.pallas import tpu as pltpu
from jax.sharding import PartitionSpec as P

mean_wind = 1.0
viscosity = 0.2
smag_coeff = 0.17
time_step = 0.2
smear = 2.0
smear_norm = 1.0 / (smear**3 * math.pi**1.5)

F32 = jnp.float32
BF16 = jnp.bfloat16
MIB = 1024 * 1024
LEVELS = 8
STEP = 256
WIDE = 512
LIGHT = pl.CostEstimate(flops=0, bytes_accessed=0, transcendentals=0)


def split(value):
    high = value.astype(BF16)
    return high, (value - high.astype(F32)).astype(BF16)


def dot(left, right, contract=0):
    return lax.dot_general(
        left, right, (((1,), (contract,)), ((), ())), preferred_element_type=F32
    )


def gaussian(first, count, centers):
    shape = (count, centers.shape[1])
    cells = (first + lax.broadcasted_iota(jnp.int32, shape, 0)).astype(F32)
    gap = cells - centers
    return jnp.exp(-gap * gap / (smear * smear))


def stencil_operator(row_cells):
    inner = (LEVELS + 4) * row_cells
    width = inner + 4 * LEVELS
    op = np.zeros((2, LEVELS, row_cells, width), np.float32)

    def column(level, row):
        if 0 <= row < row_cells:
            return (level + 2) * row_cells + row
        if row < 0:
            return inner + level * 2 + row + 2
        return inner + 2 * LEVELS + level * 2 + row - row_cells

    for level in range(LEVELS):
        for row in range(row_cells):
            for offset, first, second in ((-2, 1, -1), (-1, -8, 16), (1, 8, 16), (2, -1, -1)):
                op[0, level, row, column(level, row + offset)] += first
                op[1, level, row, column(level, row + offset)] += second
                op[1, level, row, column(level + offset, row)] += second
            op[1, level, row, column(level, row)] -= 90
    op = op.reshape(2 * LEVELS * row_cells, width)
    op = np.pad(op, ((0, 0), (0, -width % 128)))
    return np.concatenate([op, op], axis=1).astype(ml_dtypes.bfloat16)


def prep_kernel(
    turb_ref, pos_ref, speed_ref, lift_ref, vel_ref, up_ref, down_ref, lev_ref, head_ref, tail_ref
):
    component = pl.program_id(0)
    levels, rows, cols = vel_ref.shape[1:]
    coords, owned, points = pos_ref.shape

    @pl.when(component == 0)
    def _():
        for ref in (up_ref, down_ref):
            for k in range(owned):
                for i in range(coords):
                    ref[k, i : i + 1, :] = pos_ref[i, k : k + 1, :]
                    ref[k, coords + i : coords + i + 1, :] = speed_ref[i, k : k + 1, :]
                ref[k, 2 * coords : 2 * coords + 1, :] = lift_ref[k : k + 1, :]
                ref[k, 7:8, :] = jnp.full((1, points), turb_ref[k].astype(F32))

    lev_ref[0] = vel_ref[0, pl.ds(jnp.where(lax.axis_index("gz") == 0, levels - 2, 0), 2)]
    parts = levels * rows // 128
    last = vel_ref[0, :, :, cols - 128 :].reshape(levels * rows, 128)
    first = vel_ref[0, :, :, :128].reshape(levels * rows, 128)
    for part in range(parts):
        cells = slice(part * 128, part * 128 + 128)
        up_ref[owned + component * parts + part] = last[cells].T[120:]
        down_ref[owned + component * parts + part] = first[cells].T[:8]

    row = lax.broadcasted_iota(jnp.int32, (8, cols), 0) // 2
    for group in range(levels // 4):
        head = tail = None
        for k in range(4):
            top = vel_ref[0, group * 4 + k, 0:8, :]
            end = vel_ref[0, group * 4 + k, rows - 8 : rows, :]
            if k:
                top = pltpu.roll(top, 2 * k, 0)
            if k < 3:
                end = pltpu.roll(end, 2 * k + 2, 0)
            head = top if head is None else jnp.where(row == k, top, head)
            tail = end if tail is None else jnp.where(row == k, end, tail)
        head_ref[0, group * 8 : group * 8 + 8, :] = head
        tail_ref[0, group * 8 : group * 8 + 8, :] = tail


def prep(velocity, blade_pos, block_turbine, blade_vel, lift_coeff):
    components, levels, rows, cols = velocity.shape
    owned, coords, points = blade_pos.shape
    tiles = owned + components * levels * rows // 128
    whole = pl.BlockSpec((coords, owned, points), lambda i: (0, 0, 0))
    message = pl.BlockSpec((tiles, 8, 128), lambda i: (0, 0, 0))
    side = pl.BlockSpec((1, 2 * levels, cols), lambda i: (i, 0, 0))
    return pl.pallas_call(
        prep_kernel,
        grid=(components,),
        in_specs=[
            pl.BlockSpec(memory_space=pltpu.SMEM),
            whole,
            whole,
            pl.BlockSpec((owned, points), lambda i: (0, 0)),
            pl.BlockSpec((1, levels, rows, cols), lambda i: (i, 0, 0, 0)),
        ],
        out_specs=[
            message,
            message,
            pl.BlockSpec((1, 2, rows, cols), lambda i: (i, 0, 0, 0)),
            side,
            side,
        ],
        out_shape=[
            jax.ShapeDtypeStruct((tiles, 8, 128), F32),
            jax.ShapeDtypeStruct((tiles, 8, 128), F32),
            jax.ShapeDtypeStruct((components, 2, rows, cols), F32),
            jax.ShapeDtypeStruct((components, 2 * levels, cols), F32),
            jax.ShapeDtypeStruct((components, 2 * levels, cols), F32),
        ],
        compiler_params=pltpu.CompilerParams(vmem_limit_bytes=60 * MIB),
        cost_estimate=LIGHT,
        name="prep",
    )(
        block_turbine,
        blade_pos.transpose(1, 0, 2),
        blade_vel.transpose(1, 0, 2),
        lift_coeff,
        velocity,
    )


def match(mine_ref, twin_ref, per_turbine):
    core = lax.axis_index("gz")
    turbine = lax.axis_index("gy").astype(F32)
    half = mine_ref.shape[0]
    first = [(mine_ref[k, 7:8, :] == turbine).astype(F32) for k in range(half)]
    second = [(twin_ref[k, 7:8, :] == turbine).astype(F32) for k in range(half)]
    masks = []
    for hits, others, leads in ((first, second, core == 0), (second, first, core == 1)):
        rank = jnp.where(leads, jnp.zeros_like(hits[0]), sum(others))
        for hit in hits:
            masks.append([(hit > 0.5) & (rank == k) for k in range(per_turbine)])
            rank = rank + hit
    return masks


def sample_kernel(
    per_turbine, mine_ref, twin_ref, vel_ref, part_ref, own_ref, weight_ref,
    even_ref, odd_ref, center_ref, plane_ref, acc_ref,
):
    step = pl.program_id(0)
    steps = pl.num_programs(0)
    components, depth, rows, width = vel_ref.shape
    points = mine_ref.shape[2]
    count = per_turbine * points
    cells = depth * rows
    half = width // 2
    start = lax.axis_index("gy") * steps * width

    def bell(cell, center):
        gap = cell.astype(F32) - center
        return jnp.exp(-gap * gap / (smear * smear))

    def weights(at, ref):
        lane = lax.broadcasted_iota(jnp.int32, (1, 128), 1)
        for part in range(half // 128):
            cell = start + at * half + part * 128 + lane
            ref[:, part * 128 : part * 128 + 128] = bell(cell, center_ref[...])

    def multiply(side, ref):
        for i in range(components):
            column = vel_ref[i, :, :, side * half : side * half + half].reshape(cells, half)
            high, low = split(column)
            field = dot(plane_ref[...], jnp.concatenate([high, high, low], axis=0))
            product = field * ref[...]
            total = acc_ref[i]
            for part in range(half // 128):
                total += product[:, part * 128 : part * 128 + 128]
            acc_ref[i] = total
        high, low = split(ref[...])
        weight_ref[:count, side * half : side * half + half] = high
        weight_ref[count:, side * half : side * half + half] = low

    @pl.when(step == 0)
    def _():
        masks = match(mine_ref, twin_ref, per_turbine)
        blocks = mine_ref.shape[0]
        lane = lax.broadcasted_iota(jnp.int32, (1, cells), 1)
        level = lax.axis_index("gz") * depth + lane // rows
        row = lax.axis_index("gx") * rows + lane % rows
        for k in range(per_turbine):
            total = jnp.zeros((8, points), F32)
            for at, mask in enumerate(masks):
                tile = mine_ref[at] if at < blocks else twin_ref[at - blocks]
                total = jnp.where(mask[k], tile, total)
            band = slice(k * points, (k + 1) * points)
            own_ref[:, band] = total
            turned = total.T
            center_ref[band, :] = jnp.broadcast_to(turned[:, 1:2], (points, 128))
            plane = bell(row, turned[:, 0:1]) * bell(level, turned[:, 2:3])
            high, low = split(plane)
            plane_ref[band, :cells] = high
            plane_ref[band, cells : 2 * cells] = low
            plane_ref[band, 2 * cells :] = high
        acc_ref[...] = jnp.zeros(acc_ref.shape, F32)
        weights(0, even_ref)

    weights(2 * step + 1, odd_ref)
    multiply(0, even_ref)
    weights(2 * step + 2, even_ref)
    multiply(1, odd_ref)

    @pl.when(step == steps - 1)
    def _():
        for i in range(components):
            for k in range(per_turbine):
                band = slice(k * points, (k + 1) * points)
                total = jnp.sum(acc_ref[i, band, :].T, axis=0, keepdims=True)
                part_ref[i : i + 1, band] = smear_norm * total
        part_ref[components:, :] = jnp.zeros((8 - components, count), F32)


def sample(mine, twin, velocity, per_turbine):
    components, depth, rows, cols = velocity.shape
    points = mine.shape[2]
    count = per_turbine * points
    whole = pl.BlockSpec((8, count), lambda j: (0, 0))
    table = pl.BlockSpec(mine.shape, lambda j: (0, 0, 0))
    return pl.pallas_call(
        functools.partial(sample_kernel, per_turbine),
        grid=(cols // (2 * STEP),),
        in_specs=[
            table,
            table,
            pl.BlockSpec((components, depth, rows, 2 * STEP), lambda j: (0, 0, 0, j)),
        ],
        out_specs=[whole, whole, pl.BlockSpec((2 * count, 2 * STEP), lambda j: (0, j))],
        out_shape=[
            jax.ShapeDtypeStruct((8, count), F32),
            jax.ShapeDtypeStruct((8, count), F32),
            jax.ShapeDtypeStruct((2 * count, cols), BF16),
        ],
        scratch_shapes=[
            pltpu.VMEM((count, STEP), F32),
            pltpu.VMEM((count, STEP), F32),
            pltpu.VMEM((count, 128), F32),
            pltpu.VMEM((count, 3 * depth * rows), BF16),
            pltpu.VMEM((components, count, 128), F32),
        ],
        compiler_params=pltpu.CompilerParams(vmem_limit_bytes=20 * MIB),
        cost_estimate=LIGHT,
        name="sample",
    )(mine, twin, velocity)


def force_kernel(
    per_turbine, owned, mine_ref, twin_ref, part_ref, other_ref, own_ref, force_ref, home_ref
):
    points = own_ref.shape[1] // per_turbine
    relative = part_ref[0:3, :] + other_ref[0:3, :] - own_ref[3:6, :]
    speed = jnp.sqrt(jnp.sum(relative * relative, axis=0, keepdims=True))
    force = -own_ref[6:7, :] * speed * relative
    force_ref[...] = jnp.zeros(force_ref.shape, F32)
    force_ref[0:3, :] = force
    masks = match(mine_ref, twin_ref, per_turbine)
    for row in range(mine_ref.shape[0]):
        total = jnp.zeros((3, points), F32)
        for k in range(per_turbine):
            total = jnp.where(masks[row][k], force[:, k * points : (k + 1) * points], total)
        home_ref[row // owned, row % owned, 0:3, :] = total
        home_ref[row // owned, row % owned, 3:8, :] = jnp.zeros((5, points), F32)


def point_forces(mine, twin, part, other, own, per_turbine, owned):
    count = own.shape[1]
    points = count // per_turbine
    shifts = mine.shape[0] // owned
    return pl.pallas_call(
        functools.partial(force_kernel, per_turbine, owned),
        in_specs=[pl.BlockSpec(memory_space=pltpu.VMEM)] * 5,
        out_specs=[pl.BlockSpec(memory_space=pltpu.VMEM)] * 2,
        out_shape=[
            jax.ShapeDtypeStruct((8, count), F32),
            jax.ShapeDtypeStruct((shifts, owned, 8, points), F32),
        ],
        compiler_params=pltpu.CompilerParams(vmem_limit_bytes=8 * MIB),
        cost_estimate=LIGHT,
        name="force",
    )(mine, twin, part, other, own)


def update_kernel(
    own_ref, force_ref, op_ref, prev0_ref, prev1_ref, prev2_ref, next0_ref, next1_ref, next2_ref,
    weight0_ref, weight1_ref, weight2_ref, vel_ref, lev_ref, left_ref, right_ref,
    out_ref, pad_ref, wide_ref, even, odd, sems, edge_sem,
):
    step = pl.program_id(0)
    steps = pl.num_programs(0)
    components, depth, rows, cols = vel_ref.shape
    width = cols // steps
    cells = LEVELS * rows
    inner = (LEVELS + 4) * rows
    fill = op_ref.shape[1] // 2 - inner - 4 * LEVELS
    core = lax.axis_index("gz")
    turbine = lax.axis_index("gy")

    def column_copy(at):
        here = pl.multiple_of(at * width, 128)
        there = pl.multiple_of(at * width + 128, 128)
        return pltpu.make_async_copy(
            vel_ref.at[:, :, :, pl.ds(here, width)],
            pad_ref.at[:, pl.ds(2, depth), :, pl.ds(there, width)],
            sems.at[at],
        )

    def level_edge(at, owner):
        copy = pltpu.make_async_copy(
            lev_ref, pad_ref.at[:, pl.ds(at, 2), :, pl.ds(128, cols)], edge_sem
        )

        @pl.when(core == owner)
        def _():
            copy.start()
            copy.wait()

        @pl.when(core != owner)
        def _():
            pad_ref[:, at : at + 2, :, 128 : cols + 128] = jnp.zeros((components, 2, rows, cols), F32)

    def side_columns(ref, present, lane):
        per_part = 128 // rows
        parts = ref.shape[0] // components
        for tile in range(ref.shape[0]):
            turned = jnp.where(present, ref[tile], 0.0).T
            for k in range(per_part):
                level = (tile % parts) * per_part + k
                pad_ref[tile // parts, level + 2, :, lane : lane + 8] = turned[k * rows : (k + 1) * rows, :]

    def matrix_part(half, at, prev_ref, next_ref, weight_ref, bufs):
        grad_ref, lap_ref, body_ref = bufs
        center = pl.ds(pl.multiple_of(at * width + 128, 128), width)
        op = op_ref[...]
        empty = [jnp.zeros((fill, width), BF16)] if fill else []
        for i in range(components):
            column = pad_ref[i, half * LEVELS : (half + 1) * LEVELS + 4, :, center]
            inner_high, inner_low = split(column.reshape(inner, width))
            prev_high, prev_low = split(prev_ref[i])
            next_high, next_low = split(next_ref[i])
            high = [inner_high, prev_high, next_high] + empty
            low = [inner_low, prev_low, next_low] + empty
            result = dot(op, jnp.concatenate(high + low, axis=0))
            grad_ref[i] = result[:cells].reshape(LEVELS, rows, width)
            lap_ref[i] = result[cells:].reshape(LEVELS, rows, width)
        count = weight_ref.shape[0] // 2
        high = weight_ref[:count, :]
        body = dot(wide_ref[half], jnp.concatenate([high, high, weight_ref[count:, :]], axis=0))
        body_ref[...] = body.reshape(components, LEVELS, rows, width)

    def vector_part(half, at, bufs):
        grad_ref, lap_ref, body_ref = bufs
        base = at * width
        lane = lax.broadcasted_iota(jnp.int32, (8, 128), 1)
        shifts = ((1, lane < 1), (2, lane < 2), (127, lane >= 127), (126, lane >= 126))

        def cell(i, level, band, block):
            return pad_ref[i, level, band, pl.ds(pl.multiple_of(base + block * 128, 128), 128)]

        for level in range(LEVELS):
            here = half * LEVELS + level + 2
            for row in range(0, rows, 8):
                band = slice(row, row + 8)
                turned = {}

                def turn(i, block, shift, here=here, band=band, turned=turned):
                    if (i, block, shift) not in turned:
                        turned[i, block, shift] = pltpu.roll(cell(i, here, band, block), shift, 1)
                    return turned[i, block, shift]

                for block in range(1, width // 128 + 1):
                    lanes = slice(block * 128 - 128, block * 128)
                    along_y, lap, along_z = [], [], []
                    for i in range(components):
                        behind, behind2, ahead, ahead2 = [
                            jnp.where(
                                wrapped,
                                turn(i, block - 1 if shift < 64 else block + 1, shift),
                                turn(i, block, shift),
                            )
                            for shift, wrapped in shifts
                        ]
                        along_y.append(8.0 * (ahead - behind) - (ahead2 - behind2))
                        lap.append(
                            lap_ref[i, level, band, lanes]
                            + (16.0 * (ahead + behind) - (ahead2 + behind2))
                        )
                        near = cell(i, here + 1, band, block) - cell(i, here - 1, band, block)
                        far = cell(i, here + 2, band, block) - cell(i, here - 2, band, block)
                        along_z.append(8.0 * near - far)
                    along_x = [grad_ref[i, level, band, lanes] for i in range(components)]
                    same = along_x[0] * along_x[0] + along_y[1] * along_y[1] + along_z[2] * along_z[2]
                    xy = along_x[1] + along_y[0]
                    xz = along_x[2] + along_z[0]
                    yz = along_y[2] + along_z[1]
                    strain = 2.0 * same + (xy * xy + xz * xz + yz * yz)
                    mixing = (time_step / 12.0) * viscosity + (
                        time_step * smag_coeff * smag_coeff / 144.0
                    ) * jnp.sqrt(strain)
                    for i in range(components):
                        change = mixing * lap[i] - (time_step * mean_wind / 12.0) * along_x[i]
                        out_ref[i, half * LEVELS + level, band, lanes] = (
                            cell(i, here, band, block) + body_ref[i, level, band, lanes] + change
                        )

    @pl.when(step == 0)
    def _():
        for at in range(cols // width):
            column_copy(at).start()
        level_edge(0, 1)
        level_edge(depth + 2, 0)
        side_columns(left_ref, turbine > 0, 120)
        side_columns(right_ref, turbine < lax.axis_size("gy") - 1, cols + 128)
        along_x = gaussian(lax.axis_index("gx") * rows, rows, own_ref[0:1, :])
        along_z = gaussian(core * depth, depth, own_ref[2:3, :])
        count = own_ref.shape[1]
        for i in range(components):
            scaled = (time_step * smear_norm) * force_ref[i : i + 1, :] * along_x
            for level in range(depth):
                band = slice(i * cells + level % LEVELS * rows, i * cells + (level % LEVELS + 1) * rows)
                high, low = split(scaled * along_z[level : level + 1, :])
                wide_ref[level // LEVELS, band, :count] = high
                wide_ref[level // LEVELS, band, count : 2 * count] = low
                wide_ref[level // LEVELS, band, 2 * count :] = high
        column_copy(0).wait()
        matrix_part(0, 0, prev0_ref, next0_ref, weight0_ref, even)

    @pl.when(step < steps - 1)
    def _():
        column_copy(step + 1).wait()

    matrix_part(1, step, prev1_ref, next1_ref, weight1_ref, odd)
    vector_part(0, step, even)
    matrix_part(0, jnp.minimum(step + 1, steps - 1), prev2_ref, next2_ref, weight2_ref, even)
    vector_part(1, step, odd)


def update(own, force, operator, prev, after, weight, velocity, lev, left, right):
    components, depth, rows, cols = velocity.shape
    count = own.shape[1]
    steps = cols // WIDE
    hbm = pl.BlockSpec(memory_space=pl.ANY)
    places = [(0, lambda j: 0), (1, lambda j: j), (0, lambda j: jnp.minimum(j + 1, steps - 1))]
    whole = pl.BlockSpec((8, count), lambda j: (0, 0))
    sides = [
        pl.BlockSpec((components, 2 * LEVELS, WIDE), lambda j, half=half, at=at: (0, half, at(j)))
        for half, at in places
    ]
    weights = [pl.BlockSpec((2 * count, WIDE), lambda j, at=at: (0, at(j))) for _, at in places]
    column = pl.BlockSpec(left.shape, lambda j: (0, 0, 0))
    fields = [pltpu.VMEM((components, LEVELS, rows, WIDE), F32)] * 3
    return pl.pallas_call(
        update_kernel,
        grid=(steps,),
        in_specs=[whole, whole, pl.BlockSpec(operator.shape, lambda j: (0, 0))]
        + sides + sides + weights + [hbm, hbm, column, column],
        out_specs=pl.BlockSpec((components, depth, rows, WIDE), lambda j: (0, 0, 0, j)),
        out_shape=jax.ShapeDtypeStruct(velocity.shape, F32),
        scratch_shapes=[
            pltpu.VMEM((components, depth + 4, rows, cols + 256), F32),
            pltpu.VMEM((2, components * LEVELS * rows, 3 * count), BF16),
            fields,
            fields,
            pltpu.SemaphoreType.DMA((steps,)),
            pltpu.SemaphoreType.DMA,
        ],
        compiler_params=pltpu.CompilerParams(vmem_limit_bytes=44 * MIB),
        cost_estimate=LIGHT,
        name="update",
    )(
        own, force, operator, *([prev] * 3), *([after] * 3), *([weight] * 3),
        velocity, lev, left, right,
    )


def local(velocity, blade_pos, block_turbine, blade_vel, lift_coeff):
    components, depth, rows, cols = velocity.shape
    owned, _, points = blade_pos.shape
    gx, gy, gz = (lax.axis_size(axis) for axis in ("gx", "gy", "gz"))
    assert gz == 2 and depth == 2 * LEVELS
    per_turbine = owned * gz
    swap = [(0, 1), (1, 0)]

    def around(shift):
        return [(i, (i + shift) % gy) for i in range(gy)]

    up, down, facing, head, tail = prep(velocity, blade_pos, block_turbine, blade_vel, lift_coeff)
    before = lax.ppermute(tail, "gx", [(i, i + 1) for i in range(gx - 1)])
    after = lax.ppermute(head, "gx", [(i + 1, i) for i in range(gx - 1)])
    left = lax.ppermute(up, "gy", around(1))
    right = lax.ppermute(down, "gy", around(gy - 1))
    blocks = up[:owned]
    parts = [blocks, left[:owned]]
    parts += [lax.ppermute(blocks, "gy", around(shift)) for shift in range(2, gy - 1)]
    parts.append(right[:owned])
    mine = jnp.concatenate(parts, axis=0)
    twin = lax.ppermute(mine, "gz", swap)
    lev = lax.ppermute(facing, "gz", swap)

    part, own, weight = sample(mine, twin, velocity, per_turbine)
    other = lax.ppermute(part, "gz", swap)
    force, home = point_forces(mine, twin, part, other, own, per_turbine, owned)
    result = home[0]
    for shift in range(1, gy):
        result += lax.ppermute(home[shift], "gy", around(gy - shift))

    operator = jnp.asarray(stencil_operator(rows))
    new_velocity = update(
        own, force, operator, before, after, weight, velocity, lev, left[owned:], right[owned:]
    )
    return (new_velocity, result[:, :3, :])


def solution(mesh):
    in_specs = (
        P(None, "gz", "gx", "gy"),
        P(("gx", "gy", "gz"), None, None),
        P(("gx", "gy", "gz")),
        P(("gx", "gy", "gz"), None, None),
        P(("gx", "gy", "gz"), None),
    )
    out_specs = (P(None, "gz", "gx", "gy"), P(("gx", "gy", "gz"), None, None))
    return jax.shard_map(local, mesh=mesh, in_specs=in_specs, out_specs=out_specs, check_vma=False)
```

```python
import functools
import math

import jax
import jax.numpy as jnp
import ml_dtypes
import numpy as np
from jax import lax
from jax.experimental import pallas as pl
from jax.experimental.pallas import tpu as pltpu
from jax.sharding import PartitionSpec as P

mean_wind = 1.0
viscosity = 0.2
smag_coeff = 0.17
time_step = 0.2
smear = 2.0
smear_norm = 1.0 / (smear**3 * math.pi**1.5)

F32 = jnp.float32
BF16 = jnp.bfloat16
MIB = 1024 * 1024
LEVELS = 8
STEP = 256
WIDE = 256
LIGHT = pl.CostEstimate(flops=0, bytes_accessed=0, transcendentals=0)


def split(value):
    high = value.astype(BF16)
    return high, (value - high.astype(F32)).astype(BF16)


def dot(left, right, contract=0):
    return lax.dot_general(
        left, right, (((1,), (contract,)), ((), ())), preferred_element_type=F32
    )


def gaussian(first, count, centers):
    shape = (count, centers.shape[1])
    cells = (first + lax.broadcasted_iota(jnp.int32, shape, 0)).astype(F32)
    gap = cells - centers
    return jnp.exp(-gap * gap / (smear * smear))


def stencil_operator(row_cells):
    inner = (LEVELS + 4) * row_cells
    width = inner + 4 * LEVELS
    op = np.zeros((2, LEVELS, row_cells, width), np.float32)

    def column(level, row):
        if 0 <= row < row_cells:
            return (level + 2) * row_cells + row
        if row < 0:
            return inner + level * 2 + row + 2
        return inner + 2 * LEVELS + level * 2 + row - row_cells

    for level in range(LEVELS):
        for row in range(row_cells):
            for offset, first, second in ((-2, 1, -1), (-1, -8, 16), (1, 8, 16), (2, -1, -1)):
                op[0, level, row, column(level, row + offset)] += first
                op[1, level, row, column(level, row + offset)] += second
                op[1, level, row, column(level + offset, row)] += second
            op[1, level, row, column(level, row)] -= 90
    op = op.reshape(2 * LEVELS * row_cells, width)
    op = np.pad(op, ((0, 0), (0, -width % 128)))
    return np.concatenate([op, op], axis=1).astype(ml_dtypes.bfloat16)


def prep_kernel(
    turb_in, pos_in, speed_in, lift_in, vel_in, blocks_ref, up_ref, down_ref, head_ref, tail_ref,
    turb_ref, pos_ref, speed_ref, lift_ref, vel_ref, sems,
):
    components, levels, rows, cols = vel_ref.shape
    coords, owned, points = pos_ref.shape
    small = [
        pltpu.make_async_copy(source, target, sems.at[components + k])
        for k, (source, target) in enumerate(
            ((turb_in, turb_ref), (pos_in, pos_ref), (speed_in, speed_ref), (lift_in, lift_ref))
        )
    ]
    large = [
        pltpu.make_async_copy(vel_in.at[i], vel_ref.at[i], sems.at[i]) for i in range(components)
    ]
    for copy in small + large:
        copy.start()
    for copy in small:
        copy.wait()
    for ref in (blocks_ref, up_ref, down_ref):
        for k in range(owned):
            for i in range(coords):
                ref[k, i : i + 1, :] = pos_ref[i, k : k + 1, :]
                ref[k, coords + i : coords + i + 1, :] = speed_ref[i, k : k + 1, :]
            ref[k, 2 * coords : 2 * coords + 1, :] = lift_ref[k : k + 1, :]
            ref[k, 7:8, :] = jnp.full((1, points), turb_ref[k].astype(F32))
    parts = levels * rows // 128
    row = lax.broadcasted_iota(jnp.int32, (8, cols), 0) // 2
    for component in range(components):
        large[component].wait()
        last = vel_ref[component, :, :, cols - 128 :].reshape(levels * rows, 128)
        first = vel_ref[component, :, :, :128].reshape(levels * rows, 128)
        for part in range(parts):
            cells = slice(part * 128, part * 128 + 128)
            up_ref[owned + component * parts + part] = last[cells].T[120:]
            down_ref[owned + component * parts + part] = first[cells].T[:8]
        for group in range(levels // 4):
            head = tail = None
            for k in range(4):
                top = vel_ref[component, group * 4 + k, 0:8, :]
                end = vel_ref[component, group * 4 + k, rows - 8 : rows, :]
                if k:
                    top = pltpu.roll(top, 2 * k, 0)
                if k < 3:
                    end = pltpu.roll(end, 2 * k + 2, 0)
                head = top if head is None else jnp.where(row == k, top, head)
                tail = end if tail is None else jnp.where(row == k, end, tail)
            head_ref[component, group * 8 : group * 8 + 8, :] = head
            tail_ref[component, group * 8 : group * 8 + 8, :] = tail


def prep(velocity, blade_pos, block_turbine, blade_vel, lift_coeff):
    components, levels, rows, cols = velocity.shape
    owned, coords, points = blade_pos.shape
    tiles = owned + components * levels * rows // 128
    return pl.pallas_call(
        prep_kernel,
        in_specs=[pl.BlockSpec(memory_space=pltpu.HBM)] * 5,
        out_specs=[pl.BlockSpec(memory_space=pltpu.VMEM)] * 5,
        out_shape=[
            jax.ShapeDtypeStruct((owned, 8, points), F32),
            jax.ShapeDtypeStruct((tiles, 8, 128), F32),
            jax.ShapeDtypeStruct((tiles, 8, 128), F32),
            jax.ShapeDtypeStruct((components, 2 * levels, cols), F32),
            jax.ShapeDtypeStruct((components, 2 * levels, cols), F32),
        ],
        scratch_shapes=[
            pltpu.SMEM((owned,), jnp.int32),
            pltpu.VMEM((coords, owned, points), F32),
            pltpu.VMEM((coords, owned, points), F32),
            pltpu.VMEM((owned, points), F32),
            pltpu.VMEM(velocity.shape, F32),
            pltpu.SemaphoreType.DMA((components + 4,)),
        ],
        compiler_params=pltpu.CompilerParams(vmem_limit_bytes=60 * MIB),
        cost_estimate=LIGHT,
        name="prep",
    )(
        block_turbine,
        blade_pos.transpose(1, 0, 2),
        blade_vel.transpose(1, 0, 2),
        lift_coeff,
        velocity,
    )


def match(mine_ref, twin_ref, per_turbine):
    core = lax.axis_index("gz")
    turbine = lax.axis_index("gy").astype(F32)
    half = mine_ref.shape[0]
    first = [(mine_ref[k, 7:8, :] == turbine).astype(F32) for k in range(half)]
    second = [(twin_ref[k, 7:8, :] == turbine).astype(F32) for k in range(half)]
    masks = []
    for hits, others, leads in ((first, second, core == 0), (second, first, core == 1)):
        rank = jnp.where(leads, jnp.zeros_like(hits[0]), sum(others))
        for hit in hits:
            masks.append([(hit > 0.5) & (rank == k) for k in range(per_turbine)])
            rank = rank + hit
    return masks


def sample_kernel(
    per_turbine, mine_ref, twin_ref, vel_in, part_ref, own_ref, weight_ref, lev_ref,
    even_ref, odd_ref, center_ref, plane_ref, acc_ref, vel_ref, sems, lev_sem,
):
    step = pl.program_id(0)
    steps = pl.num_programs(0)
    components, depth, rows, cols = vel_ref.shape
    points = mine_ref.shape[2]
    count = per_turbine * points
    cells = depth * rows
    half = cols // (2 * steps)
    core = lax.axis_index("gz")
    start = lax.axis_index("gy") * cols

    def column_copy(at):
        column = pl.ds(pl.multiple_of(at * 2 * half, 128), 2 * half)
        return pltpu.make_async_copy(
            vel_in.at[:, :, :, column], vel_ref.at[:, :, :, column], sems.at[at]
        )

    lev_copy = pltpu.make_async_copy(
        vel_in.at[:, pl.ds(jnp.where(core == 0, depth - 2, 0), 2)], lev_ref, lev_sem
    )

    def bell(cell, center):
        gap = cell.astype(F32) - center
        return jnp.exp(gap * gap * (-1.0 / (smear * smear)))

    def weights(at, ref, slot):
        band = slice(slot * points, (slot + 1) * points)
        lane = lax.broadcasted_iota(jnp.int32, (1, 128), 1)
        for part in range(half // 128):
            cell = start + at * half + part * 128 + lane
            ref[band, part * 128 : part * 128 + 128] = bell(cell, center_ref[band, :])

    def multiply(side, ref, i):
        column = pl.ds(pl.multiple_of((2 * step + side) * half, 128), half)
        high, low = split(vel_ref[i, :, :, column].reshape(cells, half))
        field = dot(plane_ref[...], jnp.concatenate([high, high, low], axis=0))
        product = field * ref[...]
        total = acc_ref[i]
        for part in range(half // 128):
            total += product[:, part * 128 : part * 128 + 128]
        acc_ref[i] = total

    def hand_out(side, ref, slot):
        band = slice(slot * points, (slot + 1) * points)
        high, low = split(ref[band, :])
        column = slice(side * half, side * half + half)
        weight_ref[band, column] = high
        weight_ref[count + slot * points : count + (slot + 1) * points, column] = low

    @pl.when(step == 0)
    def _():
        for at in range(cols // (2 * half)):
            column_copy(at).start()
        lev_copy.start()
        masks = match(mine_ref, twin_ref, per_turbine)
        blocks = mine_ref.shape[0]
        lane = lax.broadcasted_iota(jnp.int32, (1, cells), 1)
        level = core * depth + lane // rows
        row = lax.axis_index("gx") * rows + lane % rows
        for k in range(per_turbine):
            total = jnp.zeros((8, points), F32)
            for at, mask in enumerate(masks):
                tile = mine_ref[at] if at < blocks else twin_ref[at - blocks]
                total = jnp.where(mask[k], tile, total)
            band = slice(k * points, (k + 1) * points)
            own_ref[:, band] = total
            turned = total.T
            center_ref[band, :] = jnp.broadcast_to(turned[:, 1:2], (points, 128))
            plane = bell(row, turned[:, 0:1]) * bell(level, turned[:, 2:3])
            high, low = split(plane)
            plane_ref[band, :cells] = high
            plane_ref[band, cells : 2 * cells] = low
            plane_ref[band, 2 * cells :] = high
            weights(0, even_ref, k)
        acc_ref[...] = jnp.zeros(acc_ref.shape, F32)

    column_copy(step).wait()
    for side, now, later in ((0, even_ref, odd_ref), (1, odd_ref, even_ref)):
        for k in range(max(per_turbine, components)):
            if k < per_turbine:
                weights(2 * step + side + 1, later, k)
                hand_out(side, now, k)
            if k < components:
                multiply(side, now, k)

    @pl.when(step == steps - 1)
    def _():
        for i in range(components):
            for k in range(per_turbine):
                band = slice(k * points, (k + 1) * points)
                total = jnp.sum(acc_ref[i, band, :].T, axis=0, keepdims=True)
                part_ref[i : i + 1, band] = smear_norm * total
        part_ref[components:, :] = jnp.zeros((8 - components, count), F32)
        lev_copy.wait()


def sample(mine, twin, velocity, per_turbine):
    components, depth, rows, cols = velocity.shape
    points = mine.shape[2]
    count = per_turbine * points
    steps = cols // (2 * STEP)
    whole = pl.BlockSpec((8, count), lambda j: (0, 0))
    table = pl.BlockSpec(mine.shape, lambda j: (0, 0, 0))
    return pl.pallas_call(
        functools.partial(sample_kernel, per_turbine),
        grid=(steps,),
        in_specs=[table, table, pl.BlockSpec(memory_space=pltpu.HBM)],
        out_specs=[
            whole,
            whole,
            pl.BlockSpec((2 * count, 2 * STEP), lambda j: (0, j)),
            pl.BlockSpec((components, 2, rows, cols), lambda j: (0, 0, 0, 0)),
        ],
        out_shape=[
            jax.ShapeDtypeStruct((8, count), F32),
            jax.ShapeDtypeStruct((8, count), F32),
            jax.ShapeDtypeStruct((2 * count, cols), BF16),
            jax.ShapeDtypeStruct((components, 2, rows, cols), F32),
        ],
        scratch_shapes=[
            pltpu.VMEM((count, STEP), F32),
            pltpu.VMEM((count, STEP), F32),
            pltpu.VMEM((count, 128), F32),
            pltpu.VMEM((count, 3 * depth * rows), BF16),
            pltpu.VMEM((components, count, 128), F32),
            pltpu.VMEM(velocity.shape, F32),
            pltpu.SemaphoreType.DMA((steps,)),
            pltpu.SemaphoreType.DMA,
        ],
        compiler_params=pltpu.CompilerParams(vmem_limit_bytes=60 * MIB),
        cost_estimate=LIGHT,
        name="sample",
    )(mine, twin, velocity)


def force_kernel(
    per_turbine, owned, mine_ref, twin_ref, part_ref, other_ref, own_ref, force_ref, home_ref
):
    points = own_ref.shape[1] // per_turbine
    relative = part_ref[0:3, :] + other_ref[0:3, :] - own_ref[3:6, :]
    speed = jnp.sqrt(jnp.sum(relative * relative, axis=0, keepdims=True))
    force = -own_ref[6:7, :] * speed * relative
    force_ref[...] = jnp.zeros(force_ref.shape, F32)
    force_ref[0:3, :] = force
    masks = match(mine_ref, twin_ref, per_turbine)
    for row in range(mine_ref.shape[0]):
        total = jnp.zeros((3, points), F32)
        for k in range(per_turbine):
            total = jnp.where(masks[row][k], force[:, k * points : (k + 1) * points], total)
        for i in range(3):
            home_ref[row // owned, i, row % owned : row % owned + 1, :] = total[i : i + 1]


def point_forces(mine, twin, part, other, own, per_turbine, owned):
    count = own.shape[1]
    points = count // per_turbine
    shifts = mine.shape[0] // owned
    return pl.pallas_call(
        functools.partial(force_kernel, per_turbine, owned),
        in_specs=[pl.BlockSpec(memory_space=pltpu.VMEM)] * 5,
        out_specs=[pl.BlockSpec(memory_space=pltpu.VMEM)] * 2,
        out_shape=[
            jax.ShapeDtypeStruct((8, count), F32),
            jax.ShapeDtypeStruct((shifts, 3, owned, points), F32),
        ],
        compiler_params=pltpu.CompilerParams(vmem_limit_bytes=8 * MIB),
        cost_estimate=LIGHT,
        name="force",
    )(mine, twin, part, other, own)


def update_kernel(
    own_ref, force_ref, op_ref, prev0_ref, prev1_ref, prev2_ref, next0_ref, next1_ref, next2_ref,
    weight0_ref, weight1_ref, weight2_ref, vel_ref, lev_ref, left_ref, right_ref,
    out_ref, pad_ref, high_ref, low_ref, even, odd, sems, edge_sem,
):
    step = pl.program_id(0)
    steps = pl.num_programs(0)
    components, depth, rows, cols = vel_ref.shape
    halves = depth // LEVELS
    width = cols // (2 * steps)
    cells = LEVELS * rows
    inner = (LEVELS + 4) * rows
    fill = op_ref.shape[1] // 2 - inner - 4 * LEVELS
    count = own_ref.shape[1]
    core = lax.axis_index("gz")
    turbine = lax.axis_index("gy")

    def column_copy(at):
        here = pl.multiple_of(at * width, 128)
        there = pl.multiple_of(at * width + 128, 128)
        return pltpu.make_async_copy(
            vel_ref.at[:, :, :, pl.ds(here, width)],
            pad_ref.at[:, pl.ds(2, depth), :, pl.ds(there, width)],
            sems.at[at],
        )

    def level_edge(at, owner):
        copy = pltpu.make_async_copy(
            lev_ref, pad_ref.at[:, pl.ds(at, 2), :, pl.ds(128, cols)], edge_sem
        )

        @pl.when(core == owner)
        def _():
            copy.start()
            copy.wait()

        @pl.when(core != owner)
        def _():
            pad_ref[:, at : at + 2, :, 128 : cols + 128] = jnp.zeros((components, 2, rows, cols), F32)

    def side_columns(ref, present, lane):
        per_part = 128 // rows
        parts = ref.shape[0] // components
        for tile in range(ref.shape[0]):
            turned = jnp.where(present, ref[tile], 0.0).T
            for k in range(per_part):
                level = (tile % parts) * per_part + k
                pad_ref[tile // parts, level + 2, :, lane : lane + 8] = turned[k * rows : (k + 1) * rows, :]

    def matrix_parts(at, prev_ref, next_ref, weight_ref, bufs):
        grad_ref, lap_ref, body_ref = bufs
        center = pl.ds(pl.multiple_of(at * width + 128, 128), width)

        def stencil(i, half):
            levels = slice(half * LEVELS, (half + 1) * LEVELS)
            column = pad_ref[i, half * LEVELS : (half + 1) * LEVELS + 4, :, center]
            inner_high, inner_low = split(column.reshape(inner, width))
            side = slice(half * 2 * LEVELS, (half + 1) * 2 * LEVELS)
            prev_high, prev_low = split(prev_ref[i, side])
            next_high, next_low = split(next_ref[i, side])
            empty = [jnp.zeros((fill, width), BF16)] if fill else []
            high = [inner_high, prev_high, next_high] + empty
            low = [inner_low, prev_low, next_low] + empty
            result = dot(op_ref[...], jnp.concatenate(high + low, axis=0))
            grad_ref[i, levels] = result[:cells].reshape(LEVELS, rows, width)
            lap_ref[i, levels] = result[cells:].reshape(LEVELS, rows, width)

        def body(wide_ref, band, first):
            result = dot(wide_ref[...], weight_ref[band, :])
            result = result.reshape(components, depth, rows, width)
            body_ref[...] = result if first else body_ref[...] + result

        upper, lower = slice(0, count), slice(count, 2 * count)
        yield lambda: body(high_ref, upper, True)
        yield lambda: stencil(0, 0)
        yield lambda: stencil(0, 1)
        yield lambda: body(low_ref, upper, False)
        yield lambda: stencil(1, 0)
        yield lambda: stencil(1, 1)
        yield lambda: body(high_ref, lower, False)
        yield lambda: stencil(2, 0)
        yield lambda: stencil(2, 1)

    def vector_parts(at, bufs, offset):
        grad_ref, lap_ref, body_ref = bufs
        base = at * width
        lane = lax.broadcasted_iota(jnp.int32, (8, 128), 1)
        shifts = ((1, lane < 1), (2, lane < 2), (127, lane >= 127), (126, lane >= 126))

        def cell(i, level, band, block):
            return pad_ref[i, level, band, pl.ds(pl.multiple_of(base + block * 128, 128), 128)]

        def work(level, band):
            here = level + 2
            turned = {}

            def turn(i, block, shift):
                if (i, block, shift) not in turned:
                    turned[i, block, shift] = pltpu.roll(cell(i, here, band, block), shift, 1)
                return turned[i, block, shift]

            for block in range(1, width // 128 + 1):
                lanes = slice(block * 128 - 128, block * 128)
                along_y, lap, along_z = [], [], []
                for i in range(components):
                    behind, behind2, ahead, ahead2 = [
                        jnp.where(
                            wrapped,
                            turn(i, block - 1 if shift < 64 else block + 1, shift),
                            turn(i, block, shift),
                        )
                        for shift, wrapped in shifts
                    ]
                    along_y.append(8.0 * (ahead - behind) - (ahead2 - behind2))
                    lap.append(
                        lap_ref[i, level, band, lanes]
                        + (16.0 * (ahead + behind) - (ahead2 + behind2))
                    )
                    near = cell(i, here + 1, band, block) - cell(i, here - 1, band, block)
                    far = cell(i, here + 2, band, block) - cell(i, here - 2, band, block)
                    along_z.append(8.0 * near - far)
                along_x = [grad_ref[i, level, band, lanes] for i in range(components)]
                same = along_x[0] * along_x[0] + along_y[1] * along_y[1] + along_z[2] * along_z[2]
                xy = along_x[1] + along_y[0]
                xz = along_x[2] + along_z[0]
                yz = along_y[2] + along_z[1]
                strain = 2.0 * same + (xy * xy + xz * xz + yz * yz)
                mixing = (time_step / 12.0) * viscosity + (
                    time_step * smag_coeff * smag_coeff / 144.0
                ) * jnp.sqrt(strain)
                out_lanes = slice(offset + block * 128 - 128, offset + block * 128)
                for i in range(components):
                    change = mixing * lap[i] - (time_step * mean_wind / 12.0) * along_x[i]
                    out_ref[i, level, band, out_lanes] = (
                        cell(i, here, band, block) + body_ref[i, level, band, lanes] + change
                    )

        for level in range(depth):
            for row in range(0, rows, 8):
                yield functools.partial(work, level, slice(row, row + 8))

    def together(matrix, vector):
        matrix, vector = list(matrix), list(vector)
        done = 0
        for k, piece in enumerate(matrix):
            piece()
            until = (k + 1) * len(vector) // len(matrix)
            for other in vector[done:until]:
                other()
            done = until

    @pl.when(step == 0)
    def _():
        for at in range(cols // width):
            column_copy(at).start()
        level_edge(0, 1)
        level_edge(depth + 2, 0)
        side_columns(left_ref, turbine > 0, 120)
        side_columns(right_ref, turbine < lax.axis_size("gy") - 1, cols + 128)
        along_x = gaussian(lax.axis_index("gx") * rows, rows, own_ref[0:1, :])
        along_z = gaussian(core * depth, depth, own_ref[2:3, :])
        for i in range(components):
            scaled = (time_step * smear_norm) * force_ref[i : i + 1, :] * along_x
            for level in range(depth):
                band = slice((i * depth + level) * rows, (i * depth + level + 1) * rows)
                high, low = split(scaled * along_z[level : level + 1, :])
                high_ref[band, :] = high
                low_ref[band, :] = low
        column_copy(0).wait()
        for piece in matrix_parts(0, prev0_ref, next0_ref, weight0_ref, even):
            piece()

    column_copy(2 * step + 1).wait()

    @pl.when(step < steps - 1)
    def _():
        column_copy(2 * step + 2).wait()

    last = 2 * steps - 1
    together(
        matrix_parts(2 * step + 1, prev1_ref, next1_ref, weight1_ref, odd),
        vector_parts(2 * step, even, 0),
    )
    together(
        matrix_parts(jnp.minimum(2 * step + 2, last), prev2_ref, next2_ref, weight2_ref, even),
        vector_parts(2 * step + 1, odd, width),
    )


def update(own, force, operator, prev, after, weight, velocity, lev, left, right):
    components, depth, rows, cols = velocity.shape
    count = own.shape[1]
    steps = cols // (2 * WIDE)
    hbm = pl.BlockSpec(memory_space=pltpu.HBM)
    places = [lambda j: 0, lambda j: 2 * j + 1, lambda j: jnp.minimum(2 * j + 2, 2 * steps - 1)]
    whole = pl.BlockSpec((8, count), lambda j: (0, 0))
    sides = [
        pl.BlockSpec((components, 2 * depth, WIDE), lambda j, at=at: (0, 0, at(j))) for at in places
    ]
    weights = [pl.BlockSpec((2 * count, WIDE), lambda j, at=at: (0, at(j))) for at in places]
    column = pl.BlockSpec(left.shape, lambda j: (0, 0, 0))
    fields = [pltpu.VMEM((components, depth, rows, WIDE), F32)] * 3
    macs = components * depth * rows * cols * (3 * count + 4 * 256)
    return pl.pallas_call(
        update_kernel,
        grid=(steps,),
        in_specs=[whole, whole, pl.BlockSpec(operator.shape, lambda j: (0, 0))]
        + sides + sides + weights
        + [hbm, pl.BlockSpec(memory_space=pl.ANY), column, column],
        out_specs=pl.BlockSpec((components, depth, rows, 2 * WIDE), lambda j: (0, 0, 0, j)),
        out_shape=jax.ShapeDtypeStruct(velocity.shape, F32),
        scratch_shapes=[
            pltpu.VMEM((components, depth + 4, rows, cols + 256), F32),
            pltpu.VMEM((components * depth * rows, count), BF16),
            pltpu.VMEM((components * depth * rows, count), BF16),
            fields,
            fields,
            pltpu.SemaphoreType.DMA((2 * steps,)),
            pltpu.SemaphoreType.DMA,
        ],
        compiler_params=pltpu.CompilerParams(vmem_limit_bytes=63 * MIB),
        cost_estimate=pl.CostEstimate(
            flops=2 * macs, bytes_accessed=8 * velocity.size, transcendentals=velocity.size // 3
        ),
        name="update",
    )(
        own, force, operator, *([prev] * 3), *([after] * 3), *([weight] * 3),
        velocity, lev, left, right,
    )


def local(velocity, blade_pos, block_turbine, blade_vel, lift_coeff):
    components, depth, rows, cols = velocity.shape
    owned, _, points = blade_pos.shape
    gx, gy, gz = (lax.axis_size(axis) for axis in ("gx", "gy", "gz"))
    assert gz == 2 and depth == 2 * LEVELS
    per_turbine = owned * gz
    swap = [(0, 1), (1, 0)]

    def around(shift):
        return [(i, (i + shift) % gy) for i in range(gy)]

    blocks, up, down, head, tail = prep(velocity, blade_pos, block_turbine, blade_vel, lift_coeff)
    before = lax.ppermute(tail, "gx", [(i, i + 1) for i in range(gx - 1)])
    after = lax.ppermute(head, "gx", [(i + 1, i) for i in range(gx - 1)])
    def blade(blocks, up, down, velocity):
        left = lax.ppermute(up, "gy", around(1))
        right = lax.ppermute(down, "gy", around(gy - 1))
        parts = [blocks, left[:owned]]
        parts += [lax.ppermute(blocks, "gy", around(shift)) for shift in range(2, gy - 1)]
        parts.append(right[:owned])
        mine = jnp.concatenate(parts, axis=0)
        twin = lax.ppermute(mine, "gz", swap)
        part, own, weight, facing = sample(mine, twin, velocity, per_turbine)
        other = lax.ppermute(part, "gz", swap)
        force, home = point_forces(mine, twin, part, other, own, per_turbine, owned)
        return own, force, home, weight, facing, left[owned:], right[owned:]

    operands = (blocks, up, down, velocity)
    empty = [jnp.zeros(out.shape, out.dtype) for out in jax.eval_shape(blade, *operands)]
    own, force, home, weight, facing, left, right = lax.cond(
        block_turbine[0] >= 0, blade, lambda *_: tuple(empty), *operands
    )
    lev = lax.ppermute(facing, "gz", swap)
    result = home[0]
    for shift in range(1, gy):
        result += lax.ppermute(home[shift], "gy", around(gy - shift))

    operator = jnp.asarray(stencil_operator(rows))
    new_velocity = update(
        own, force, operator, before, after, weight, velocity, lev, left, right
    )
    return (new_velocity, result.transpose(1, 0, 2))


def solution(mesh):
    in_specs = (
        P(None, "gz", "gx", "gy"),
        P(("gx", "gy", "gz"), None, None),
        P(("gx", "gy", "gz")),
        P(("gx", "gy", "gz"), None, None),
        P(("gx", "gy", "gz"), None),
    )
    out_specs = (P(None, "gz", "gx", "gy"), P(("gx", "gy", "gz"), None, None))
    return jax.shard_map(local, mesh=mesh, in_specs=in_specs, out_specs=out_specs, check_vma=False)
```

```python
import functools
import math

import jax
import jax.numpy as jnp
import ml_dtypes
import numpy as np
from jax import lax
from jax.experimental import pallas as pl
from jax.experimental.pallas import tpu as pltpu
from jax.sharding import PartitionSpec as P

mean_wind = 1.0
viscosity = 0.2
smag_coeff = 0.17
time_step = 0.2
smear = 2.0
smear_norm = 1.0 / (smear**3 * math.pi**1.5)

F32 = jnp.float32
BF16 = jnp.bfloat16
MIB = 1024 * 1024
LEVELS = 8
STEP = 256
LIGHT = pl.CostEstimate(flops=0, bytes_accessed=0, transcendentals=0)


def split(value):
    high = value.astype(BF16)
    return high, (value - high.astype(F32)).astype(BF16)


def dot(left, right, contract=0):
    return lax.dot_general(
        left, right, (((1,), (contract,)), ((), ())), preferred_element_type=F32
    )


def gaussian(first, count, centers):
    shape = (count, centers.shape[1])
    cells = (first + lax.broadcasted_iota(jnp.int32, shape, 0)).astype(F32)
    gap = cells - centers
    return jnp.exp(-gap * gap / (smear * smear))


def stencil_operator(row_cells):
    inner = (LEVELS + 4) * row_cells
    width = inner + 4 * LEVELS
    op = np.zeros((2, LEVELS, row_cells, width), np.float32)

    def column(level, row):
        if 0 <= row < row_cells:
            return (level + 2) * row_cells + row
        if row < 0:
            return inner + level * 2 + row + 2
        return inner + 2 * LEVELS + level * 2 + row - row_cells

    for level in range(LEVELS):
        for row in range(row_cells):
            for offset, first, second in ((-2, 1, -1), (-1, -8, 16), (1, 8, 16), (2, -1, -1)):
                op[0, level, row, column(level, row + offset)] += first
                op[1, level, row, column(level, row + offset)] += second
                op[1, level, row, column(level + offset, row)] += second
            op[1, level, row, column(level, row)] -= 90
    op = op.reshape(2 * LEVELS * row_cells, width)
    op = np.pad(op, ((0, 0), (0, -width % 128)))
    return np.concatenate([op, op], axis=1).astype(ml_dtypes.bfloat16)


def prep_kernel(
    turb_in, pos_in, speed_in, lift_in, vel_in, blocks_ref, up_ref, down_ref, head_ref, tail_ref,
    turb_ref, pos_ref, speed_ref, lift_ref, vel_ref, sems,
):
    components, levels, rows, cols = vel_ref.shape
    coords, owned, points = pos_ref.shape
    small = [
        pltpu.make_async_copy(source, target, sems.at[components + k])
        for k, (source, target) in enumerate(
            ((turb_in, turb_ref), (pos_in, pos_ref), (speed_in, speed_ref), (lift_in, lift_ref))
        )
    ]
    large = [
        pltpu.make_async_copy(vel_in.at[i], vel_ref.at[i], sems.at[i]) for i in range(components)
    ]
    for copy in small + large:
        copy.start()
    for copy in small:
        copy.wait()
    for ref in (blocks_ref, up_ref, down_ref):
        for k in range(owned):
            for i in range(coords):
                ref[k, i : i + 1, :] = pos_ref[i, k : k + 1, :]
                ref[k, coords + i : coords + i + 1, :] = speed_ref[i, k : k + 1, :]
            ref[k, 2 * coords : 2 * coords + 1, :] = lift_ref[k : k + 1, :]
            ref[k, 7:8, :] = jnp.full((1, points), turb_ref[k].astype(F32))
    parts = levels * rows // 128
    row = lax.broadcasted_iota(jnp.int32, (8, cols), 0) // 2
    for component in range(components):
        large[component].wait()
        last = vel_ref[component, :, :, cols - 128 :].reshape(levels * rows, 128)
        first = vel_ref[component, :, :, :128].reshape(levels * rows, 128)
        for part in range(parts):
            cells = slice(part * 128, part * 128 + 128)
            up_ref[owned + component * parts + part] = last[cells].T[120:]
            down_ref[owned + component * parts + part] = first[cells].T[:8]
        for group in range(levels // 4):
            head = tail = None
            for k in range(4):
                top = vel_ref[component, group * 4 + k, 0:8, :]
                end = vel_ref[component, group * 4 + k, rows - 8 : rows, :]
                if k:
                    top = pltpu.roll(top, 2 * k, 0)
                if k < 3:
                    end = pltpu.roll(end, 2 * k + 2, 0)
                head = top if head is None else jnp.where(row == k, top, head)
                tail = end if tail is None else jnp.where(row == k, end, tail)
            head_ref[component, group * 8 : group * 8 + 8, :] = head
            tail_ref[component, group * 8 : group * 8 + 8, :] = tail


def prep(velocity, blade_pos, block_turbine, blade_vel, lift_coeff):
    components, levels, rows, cols = velocity.shape
    owned, coords, points = blade_pos.shape
    tiles = owned + components * levels * rows // 128
    return pl.pallas_call(
        prep_kernel,
        in_specs=[pl.BlockSpec(memory_space=pltpu.HBM)] * 5,
        out_specs=[pl.BlockSpec(memory_space=pltpu.VMEM)] * 5,
        out_shape=[
            jax.ShapeDtypeStruct((owned, 8, points), F32),
            jax.ShapeDtypeStruct((tiles, 8, 128), F32),
            jax.ShapeDtypeStruct((tiles, 8, 128), F32),
            jax.ShapeDtypeStruct((components, 2 * levels, cols), F32),
            jax.ShapeDtypeStruct((components, 2 * levels, cols), F32),
        ],
        scratch_shapes=[
            pltpu.SMEM((owned,), jnp.int32),
            pltpu.VMEM((coords, owned, points), F32),
            pltpu.VMEM((coords, owned, points), F32),
            pltpu.VMEM((owned, points), F32),
            pltpu.VMEM(velocity.shape, F32),
            pltpu.SemaphoreType.DMA((components + 4,)),
        ],
        compiler_params=pltpu.CompilerParams(vmem_limit_bytes=60 * MIB),
        cost_estimate=LIGHT,
        name="prep",
    )(
        block_turbine,
        blade_pos.transpose(1, 0, 2),
        blade_vel.transpose(1, 0, 2),
        lift_coeff,
        velocity,
    )


def match(mine_ref, twin_ref, per_turbine):
    core = lax.axis_index("gz")
    turbine = lax.axis_index("gy").astype(F32)
    half = mine_ref.shape[0]
    first = [(mine_ref[k, 7:8, :] == turbine).astype(F32) for k in range(half)]
    second = [(twin_ref[k, 7:8, :] == turbine).astype(F32) for k in range(half)]
    masks = []
    for hits, others, leads in ((first, second, core == 0), (second, first, core == 1)):
        rank = jnp.where(leads, jnp.zeros_like(hits[0]), sum(others))
        for hit in hits:
            masks.append([(hit > 0.5) & (rank == k) for k in range(per_turbine)])
            rank = rank + hit
    return masks


def sample_kernel(
    per_turbine, mine_ref, twin_ref, vel_in, part_ref, own_ref, mask_ref, weight_out, lev_ref,
    even_ref, odd_ref, center_ref, plane_ref, acc_ref, vel_ref, weight_ref, sems, out_sems, lev_sem,
):
    components, depth, rows, cols = vel_ref.shape
    points = mine_ref.shape[2]
    count = per_turbine * points
    cells = depth * rows
    chunks = cols // STEP
    core = lax.axis_index("gz")
    start = lax.axis_index("gy") * cols

    def column(at):
        return pl.ds(pl.multiple_of(at * STEP, STEP), STEP)

    def column_copy(at):
        return pltpu.make_async_copy(
            vel_in.at[:, :, :, column(at)], vel_ref.at[:, :, :, column(at)], sems.at[at]
        )

    def weight_copy(at):
        return pltpu.make_async_copy(
            weight_ref.at[:, column(at)], weight_out.at[:, column(at)], out_sems.at[at]
        )

    lev_copy = pltpu.make_async_copy(
        vel_in.at[:, pl.ds(jnp.where(core == 0, depth - 2, 0), 2)], lev_ref, lev_sem
    )

    def bell(cell, center):
        gap = cell.astype(F32) - center
        return jnp.exp(gap * gap * (-1.0 / (smear * smear)))

    def weights(at, ref):
        lane = lax.broadcasted_iota(jnp.int32, (1, 128), 1)
        for part in range(STEP // 128):
            cell = start + at * STEP + part * 128 + lane
            ref[:, part * 128 : part * 128 + 128] = bell(cell, center_ref[...])

    def multiply(at, ref):
        for i in range(components):
            high, low = split(vel_ref[i, :, :, column(at)].reshape(cells, STEP))
            field = dot(plane_ref[...], jnp.concatenate([high, high, low], axis=0))
            product = field * ref[...]
            total = acc_ref[i]
            for part in range(STEP // 128):
                total += product[:, part * 128 : part * 128 + 128]
            acc_ref[i] = total
        high, low = split(ref[...])
        weight_ref[:count, column(at)] = high
        weight_ref[count:, column(at)] = low

    for at in range(chunks):
        column_copy(at).start()
    lev_copy.start()
    masks = match(mine_ref, twin_ref, per_turbine)
    blocks = mine_ref.shape[0]
    lane = lax.broadcasted_iota(jnp.int32, (1, cells), 1)
    level = core * depth + lane // rows
    row = lax.axis_index("gx") * rows + lane % rows
    for k in range(per_turbine):
        total = jnp.zeros((8, points), F32)
        for at, mask in enumerate(masks):
            tile = mine_ref[at] if at < blocks else twin_ref[at - blocks]
            total = jnp.where(mask[k], tile, total)
        band = slice(k * points, (k + 1) * points)
        own_ref[:, band] = total
        turned = total.T
        center_ref[band, :] = jnp.broadcast_to(turned[:, 1:2], (points, 128))
        plane = bell(row, turned[:, 0:1]) * bell(level, turned[:, 2:3])
        high, low = split(plane)
        plane_ref[band, :cells] = high
        plane_ref[band, cells : 2 * cells] = low
        plane_ref[band, 2 * cells :] = high
    for at in range(blocks):
        for k in range(per_turbine):
            mask_ref[at, k : k + 1, :] = masks[at][k].astype(F32)
    acc_ref[...] = jnp.zeros(acc_ref.shape, F32)
    weights(0, even_ref)

    def pair(step, carry):
        column_copy(2 * step).wait()
        column_copy(2 * step + 1).wait()
        weights(2 * step + 1, odd_ref)
        multiply(2 * step, even_ref)
        weights(2 * step + 2, even_ref)
        multiply(2 * step + 1, odd_ref)
        weight_copy(2 * step).start()
        weight_copy(2 * step + 1).start()
        return carry

    lax.fori_loop(0, chunks // 2, pair, 0)
    for i in range(components):
        for k in range(per_turbine):
            band = slice(k * points, (k + 1) * points)
            total = jnp.sum(acc_ref[i, band, :].T, axis=0, keepdims=True)
            part_ref[i : i + 1, band] = smear_norm * total
    part_ref[components:, :] = jnp.zeros((8 - components, count), F32)
    lev_copy.wait()
    for at in range(chunks):
        weight_copy(at).wait()


def sample(mine, twin, velocity, per_turbine):
    components, depth, rows, cols = velocity.shape
    points = mine.shape[2]
    count = per_turbine * points
    chunks = cols // STEP
    vmem = pl.BlockSpec(memory_space=pltpu.VMEM)
    hbm = pl.BlockSpec(memory_space=pltpu.HBM)
    return pl.pallas_call(
        functools.partial(sample_kernel, per_turbine),
        in_specs=[vmem, vmem, hbm],
        out_specs=[vmem, vmem, vmem, hbm, vmem],
        out_shape=[
            jax.ShapeDtypeStruct((8, count), F32),
            jax.ShapeDtypeStruct((8, count), F32),
            jax.ShapeDtypeStruct((mine.shape[0], per_turbine, points), F32),
            jax.ShapeDtypeStruct((2 * count, cols), BF16),
            jax.ShapeDtypeStruct((components, 2, rows, cols), F32),
        ],
        scratch_shapes=[
            pltpu.VMEM((count, STEP), F32),
            pltpu.VMEM((count, STEP), F32),
            pltpu.VMEM((count, 128), F32),
            pltpu.VMEM((count, 3 * depth * rows), BF16),
            pltpu.VMEM((components, count, 128), F32),
            pltpu.VMEM(velocity.shape, F32),
            pltpu.VMEM((2 * count, cols), BF16),
            pltpu.SemaphoreType.DMA((chunks,)),
            pltpu.SemaphoreType.DMA((chunks,)),
            pltpu.SemaphoreType.DMA,
        ],
        compiler_params=pltpu.CompilerParams(vmem_limit_bytes=58 * MIB),
        cost_estimate=LIGHT,
        name="sample",
    )(mine, twin, velocity)


def force_kernel(
    per_turbine, owned, mask_ref, part_ref, other_ref, own_ref, force_ref, home_ref
):
    points = own_ref.shape[1] // per_turbine
    relative = part_ref[0:3, :] + other_ref[0:3, :] - own_ref[3:6, :]
    speed = jnp.sqrt(jnp.sum(relative * relative, axis=0, keepdims=True))
    force = -own_ref[6:7, :] * speed * relative
    force_ref[...] = jnp.zeros(force_ref.shape, F32)
    force_ref[0:3, :] = force
    for row in range(mask_ref.shape[0]):
        total = jnp.zeros((3, points), F32)
        for k in range(per_turbine):
            total = jnp.where(mask_ref[row, k : k + 1, :] > 0.5, force[:, k * points : (k + 1) * points], total)
        for i in range(3):
            home_ref[row // owned, i, row % owned : row % owned + 1, :] = total[i : i + 1]


def point_forces(mask, part, other, own, per_turbine, owned):
    count = own.shape[1]
    points = count // per_turbine
    shifts = mask.shape[0] // owned
    return pl.pallas_call(
        functools.partial(force_kernel, per_turbine, owned),
        in_specs=[pl.BlockSpec(memory_space=pltpu.VMEM)] * 4,
        out_specs=[pl.BlockSpec(memory_space=pltpu.VMEM)] * 2,
        out_shape=[
            jax.ShapeDtypeStruct((8, count), F32),
            jax.ShapeDtypeStruct((shifts, 3, owned, points), F32),
        ],
        compiler_params=pltpu.CompilerParams(vmem_limit_bytes=58 * MIB),
        cost_estimate=LIGHT,
        name="force",
    )(mask, part, other, own)


def update_kernel(
    own_ref, force_ref, op_ref, left_ref, right_ref, prev_in, next_in, weight_in, vel_in, lev_in,
    new_out, pad_ref, new_ref, prev_ref, next_ref, weight_ref, high_ref, low_ref, even, odd,
    vel_sems, side_sems, weight_sems, new_sems, lev_sem,
):
    components, depth, rows, cols = new_ref.shape
    chunks = cols // STEP
    cells = LEVELS * rows
    inner = (LEVELS + 4) * rows
    fill = op_ref.shape[1] // 2 - inner - 4 * LEVELS
    count = own_ref.shape[1]
    core = lax.axis_index("gz")
    turbine = lax.axis_index("gy")
    lane = lax.broadcasted_iota(jnp.int32, (8, 128), 1)
    shifts = ((1, lane < 1), (2, lane < 2), (127, lane >= 127), (126, lane >= 126))

    def column(at, first=0):
        return pl.ds(pl.multiple_of(at * STEP + first, 128), STEP)

    def arrivals(at):
        return [
            pltpu.make_async_copy(
                vel_in.at[:, :, :, column(at)],
                pad_ref.at[:, pl.ds(2, depth), :, column(at, 128)],
                vel_sems.at[at],
            ),
            pltpu.make_async_copy(
                weight_in.at[:, column(at)], weight_ref.at[:, column(at)], weight_sems.at[at]
            ),
            pltpu.make_async_copy(
                prev_in.at[:, :, column(at)], prev_ref.at[:, :, column(at)], side_sems.at[0, at]
            ),
            pltpu.make_async_copy(
                next_in.at[:, :, column(at)], next_ref.at[:, :, column(at)], side_sems.at[1, at]
            ),
        ]

    def departure(at):
        return pltpu.make_async_copy(
            new_ref.at[:, :, :, column(at)], new_out.at[:, :, :, column(at)], new_sems.at[at]
        )

    def level_copy(at):
        return pltpu.make_async_copy(
            lev_in, pad_ref.at[:, pl.ds(at, 2), :, pl.ds(128, cols)], lev_sem
        )

    def side_columns(ref, present, lane):
        per_part = 128 // rows
        parts = ref.shape[0] // components
        for tile in range(ref.shape[0]):
            turned = jnp.where(present, ref[tile], 0.0).T
            for k in range(per_part):
                level = (tile % parts) * per_part + k
                pad_ref[tile // parts, level + 2, :, lane : lane + 8] = turned[k * rows : (k + 1) * rows, :]

    def matrix_part(at, bufs):
        grad_ref, lap_ref, body_ref = bufs
        for i in range(components):
            for half in range(depth // LEVELS):
                levels = slice(half * LEVELS, (half + 1) * LEVELS)
                field = pad_ref[i, half * LEVELS : (half + 1) * LEVELS + 4, :, column(at, 128)]
                inner_high, inner_low = split(field.reshape(inner, STEP))
                side = slice(half * 2 * LEVELS, (half + 1) * 2 * LEVELS)
                prev_high, prev_low = split(prev_ref[i, side, column(at)])
                next_high, next_low = split(next_ref[i, side, column(at)])
                empty = [jnp.zeros((fill, STEP), BF16)] if fill else []
                high = [inner_high, prev_high, next_high] + empty
                low = [inner_low, prev_low, next_low] + empty
                result = dot(op_ref[...], jnp.concatenate(high + low, axis=0))
                grad_ref[i, levels] = result[:cells].reshape(LEVELS, rows, STEP)
                lap_ref[i, levels] = result[cells:].reshape(LEVELS, rows, STEP)
        upper = weight_ref[:count, column(at)]
        lower = weight_ref[count:, column(at)]
        wide = jnp.concatenate([high_ref[...], low_ref[...], high_ref[...]], axis=1)
        result = dot(wide, jnp.concatenate([upper, upper, lower], axis=0))
        body_ref[...] = result.reshape(components, depth, rows, STEP)

    def vector_part(at, bufs):
        grad_ref, lap_ref, body_ref = bufs

        def cell(i, level, band, block):
            return pad_ref[i, level, band, pl.ds(pl.multiple_of(at * STEP + block * 128, 128), 128)]

        def work(level, band):
            here = level + 2
            turned = {}

            def turn(i, block, shift):
                if (i, block, shift) not in turned:
                    turned[i, block, shift] = pltpu.roll(cell(i, here, band, block), shift, 1)
                return turned[i, block, shift]

            for block in range(1, STEP // 128 + 1):
                lanes = slice(block * 128 - 128, block * 128)
                along_y, lap, along_z = [], [], []
                for i in range(components):
                    behind, behind2, ahead, ahead2 = [
                        jnp.where(
                            wrapped,
                            turn(i, block - 1 if shift < 64 else block + 1, shift),
                            turn(i, block, shift),
                        )
                        for shift, wrapped in shifts
                    ]
                    along_y.append(8.0 * (ahead - behind) - (ahead2 - behind2))
                    lap.append(
                        lap_ref[i, level, band, lanes]
                        + (16.0 * (ahead + behind) - (ahead2 + behind2))
                    )
                    near = cell(i, here + 1, band, block) - cell(i, here - 1, band, block)
                    far = cell(i, here + 2, band, block) - cell(i, here - 2, band, block)
                    along_z.append(8.0 * near - far)
                along_x = [grad_ref[i, level, band, lanes] for i in range(components)]
                same = along_x[0] * along_x[0] + along_y[1] * along_y[1] + along_z[2] * along_z[2]
                xy = along_x[1] + along_y[0]
                xz = along_x[2] + along_z[0]
                yz = along_y[2] + along_z[1]
                strain = 2.0 * same + (xy * xy + xz * xz + yz * yz)
                mixing = (time_step / 12.0) * viscosity + (
                    time_step * smag_coeff * smag_coeff / 144.0
                ) * jnp.sqrt(strain)
                out_lanes = pl.ds(pl.multiple_of(at * STEP + block * 128 - 128, 128), 128)
                for i in range(components):
                    change = mixing * lap[i] - (time_step * mean_wind / 12.0) * along_x[i]
                    new_ref[i, level, band, out_lanes] = (
                        cell(i, here, band, block) + body_ref[i, level, band, lanes] + change
                    )

        for level in range(depth):
            for row in range(0, rows, 8):
                work(level, slice(row, row + 8))
        departure(at).start()

    for at in range(chunks):
        for copy in arrivals(at):
            copy.start()

    @pl.when(core == 1)
    def _():
        level_copy(0).start()
        pad_ref[:, depth + 2 :, :, 128 : cols + 128] = jnp.zeros((components, 2, rows, cols), F32)

    @pl.when(core == 0)
    def _():
        level_copy(depth + 2).start()
        pad_ref[:, 0:2, :, 128 : cols + 128] = jnp.zeros((components, 2, rows, cols), F32)

    side_columns(left_ref, turbine > 0, 120)
    side_columns(right_ref, turbine < lax.axis_size("gy") - 1, cols + 128)
    along_x = gaussian(lax.axis_index("gx") * rows, rows, own_ref[0:1, :])
    along_z = gaussian(core * depth, depth, own_ref[2:3, :])
    for i in range(components):
        scaled = (time_step * smear_norm) * force_ref[i : i + 1, :] * along_x
        for level in range(depth):
            band = slice((i * depth + level) * rows, (i * depth + level + 1) * rows)
            high, low = split(scaled * along_z[level : level + 1, :])
            high_ref[band, :] = high
            low_ref[band, :] = low
    level_copy(0).wait()
    for copy in arrivals(0):
        copy.wait()
    matrix_part(0, even)

    def pair(step, carry):
        for copy in arrivals(2 * step + 1) + arrivals(2 * step + 2):
            copy.wait()
        matrix_part(2 * step + 1, odd)
        vector_part(2 * step, even)
        matrix_part(2 * step + 2, even)
        vector_part(2 * step + 1, odd)
        return carry

    lax.fori_loop(0, chunks // 2 - 1, pair, 0)
    for copy in arrivals(chunks - 1):
        copy.wait()
    matrix_part(chunks - 1, odd)
    vector_part(chunks - 2, even)
    vector_part(chunks - 1, odd)
    for at in range(chunks):
        departure(at).wait()


def update(own, force, operator, prev, after, weight, velocity, lev, left, right):
    components, depth, rows, cols = velocity.shape
    count = own.shape[1]
    chunks = cols // STEP
    vmem = pl.BlockSpec(memory_space=pltpu.VMEM)
    hbm = pl.BlockSpec(memory_space=pltpu.HBM)
    fields = [pltpu.VMEM((components, depth, rows, STEP), F32)] * 3
    macs = components * depth * rows * cols * (3 * count + 4 * 256)
    return pl.pallas_call(
        update_kernel,
        in_specs=[vmem] * 5 + [hbm] * 5,
        out_specs=hbm,
        out_shape=jax.ShapeDtypeStruct(velocity.shape, F32),
        scratch_shapes=[
            pltpu.VMEM((components, depth + 4, rows, cols + 256), F32),
            pltpu.VMEM(velocity.shape, F32),
            pltpu.VMEM(prev.shape, F32),
            pltpu.VMEM(prev.shape, F32),
            pltpu.VMEM((2 * count, cols), BF16),
            pltpu.VMEM((components * depth * rows, count), BF16),
            pltpu.VMEM((components * depth * rows, count), BF16),
            fields,
            fields,
            pltpu.SemaphoreType.DMA((chunks,)),
            pltpu.SemaphoreType.DMA((2, chunks)),
            pltpu.SemaphoreType.DMA((chunks,)),
            pltpu.SemaphoreType.DMA((chunks,)),
            pltpu.SemaphoreType.DMA,
        ],
        compiler_params=pltpu.CompilerParams(vmem_limit_bytes=44 * MIB),
        cost_estimate=pl.CostEstimate(
            flops=2 * macs, bytes_accessed=8 * velocity.size, transcendentals=velocity.size // 3
        ),
        name="update",
    )(own, force, operator, left, right, prev, after, weight, velocity, lev)


def local(velocity, blade_pos, block_turbine, blade_vel, lift_coeff):
    components, depth, rows, cols = velocity.shape
    owned, _, points = blade_pos.shape
    gx, gy, gz = (lax.axis_size(axis) for axis in ("gx", "gy", "gz"))
    assert gz == 2 and depth == 2 * LEVELS
    per_turbine = owned * gz
    swap = [(0, 1), (1, 0)]

    def around(shift):
        return [(i, (i + shift) % gy) for i in range(gy)]

    blocks, up, down, head, tail = prep(velocity, blade_pos, block_turbine, blade_vel, lift_coeff)
    before = lax.ppermute(tail, "gx", [(i, i + 1) for i in range(gx - 1)])
    after = lax.ppermute(head, "gx", [(i + 1, i) for i in range(gx - 1)])
    def blade(blocks, up, down, velocity):
        left = lax.ppermute(up, "gy", around(1))
        right = lax.ppermute(down, "gy", around(gy - 1))
        parts = [blocks, left[:owned]]
        parts += [lax.ppermute(blocks, "gy", around(shift)) for shift in range(2, gy - 1)]
        parts.append(right[:owned])
        mine = jnp.concatenate(parts, axis=0)
        twin = lax.ppermute(mine, "gz", swap)
        part, own, mask, weight, facing = sample(mine, twin, velocity, per_turbine)
        other = lax.ppermute(part, "gz", swap)
        force, home = point_forces(mask, part, other, own, per_turbine, owned)
        return own, force, home, weight, facing, left[owned:], right[owned:]

    operands = (blocks, up, down, velocity)
    empty = [jnp.zeros(out.shape, out.dtype) for out in jax.eval_shape(blade, *operands)]
    own, force, home, weight, facing, left, right = lax.cond(
        block_turbine[0] >= 0, blade, lambda *_: tuple(empty), *operands
    )
    lev = lax.ppermute(facing, "gz", swap)
    result = home[0]
    for shift in range(1, gy):
        result += lax.ppermute(home[shift], "gy", around(gy - shift))

    operator = jnp.asarray(stencil_operator(rows))
    new_velocity = update(
        own, force, operator, before, after, weight, velocity, lev, left, right
    )
    return (new_velocity, result.transpose(1, 0, 2))


def solution(mesh):
    in_specs = (
        P(None, "gz", "gx", "gy"),
        P(("gx", "gy", "gz"), None, None),
        P(("gx", "gy", "gz")),
        P(("gx", "gy", "gz"), None, None),
        P(("gx", "gy", "gz"), None),
    )
    out_specs = (P(None, "gz", "gx", "gy"), P(("gx", "gy", "gz"), None, None))
    return jax.shard_map(local, mesh=mesh, in_specs=in_specs, out_specs=out_specs, check_vma=False)
```

```python
import functools
import math

import jax
import jax.numpy as jnp
import ml_dtypes
import numpy as np
from jax import lax
from jax.experimental import pallas as pl
from jax.experimental.pallas import tpu as pltpu
from jax.sharding import PartitionSpec as P

mean_wind = 1.0
viscosity = 0.2
smag_coeff = 0.17
time_step = 0.2
smear = 2.0
smear_norm = 1.0 / (smear**3 * math.pi**1.5)

F32 = jnp.float32
BF16 = jnp.bfloat16
MIB = 1024 * 1024
LEVELS = 8
STEP = 256
LIGHT = pl.CostEstimate(flops=0, bytes_accessed=0, transcendentals=0)


def split(value):
    high = value.astype(BF16)
    return high, (value - high.astype(F32)).astype(BF16)


def dot(left, right, contract=0):
    return lax.dot_general(
        left, right, (((1,), (contract,)), ((), ())), preferred_element_type=F32
    )


def gaussian(first, count, centers):
    shape = (count, centers.shape[1])
    cells = (first + lax.broadcasted_iota(jnp.int32, shape, 0)).astype(F32)
    gap = cells - centers
    return jnp.exp(-gap * gap / (smear * smear))


def stencil_operator(row_cells):
    inner = (LEVELS + 4) * row_cells
    width = inner + 4 * LEVELS
    op = np.zeros((2, LEVELS, row_cells, width), np.float32)

    def column(level, row):
        if 0 <= row < row_cells:
            return (level + 2) * row_cells + row
        if row < 0:
            return inner + level * 2 + row + 2
        return inner + 2 * LEVELS + level * 2 + row - row_cells

    for level in range(LEVELS):
        for row in range(row_cells):
            for offset, first, second in ((-2, 1, -1), (-1, -8, 16), (1, 8, 16), (2, -1, -1)):
                op[0, level, row, column(level, row + offset)] += first
                op[1, level, row, column(level, row + offset)] += second
                op[1, level, row, column(level + offset, row)] += second
            op[1, level, row, column(level, row)] -= 90
    op = op.reshape(2 * LEVELS * row_cells, width)
    op = np.pad(op, ((0, 0), (0, -width % 128)))
    return np.concatenate([op, op], axis=1).astype(ml_dtypes.bfloat16)


def prep_kernel(
    turb_in, pos_in, speed_in, lift_in, vel_in, blocks_ref, up_ref, down_ref, near_ref, far_ref, relay_ref,
    turb_ref, pos_ref, speed_ref, lift_ref, vel_ref, sems,
):
    components, levels, rows, cols = vel_ref.shape
    coords, owned, points = pos_ref.shape
    small = [
        pltpu.make_async_copy(source, target, sems.at[components + k])
        for k, (source, target) in enumerate(
            ((turb_in, turb_ref), (pos_in, pos_ref), (speed_in, speed_ref), (lift_in, lift_ref))
        )
    ]
    large = [
        pltpu.make_async_copy(vel_in.at[i], vel_ref.at[i], sems.at[i]) for i in range(components)
    ]
    for copy in small + large:
        copy.start()
    for copy in small:
        copy.wait()
    for ref in (blocks_ref, up_ref, down_ref):
        for k in range(owned):
            for i in range(coords):
                ref[k, i : i + 1, :] = pos_ref[i, k : k + 1, :]
                ref[k, coords + i : coords + i + 1, :] = speed_ref[i, k : k + 1, :]
            ref[k, 2 * coords : 2 * coords + 1, :] = lift_ref[k : k + 1, :]
            ref[k, 7:8, :] = jnp.full((1, points), turb_ref[k].astype(F32))
    parts = levels * rows // 128
    odd = lax.axis_index("gx") % 2 == 1
    row = lax.broadcasted_iota(jnp.int32, (8, cols), 0) // 2
    for component in range(components):
        large[component].wait()
        last = vel_ref[component, :, :, cols - 128 :].reshape(levels * rows, 128)
        first = vel_ref[component, :, :, :128].reshape(levels * rows, 128)
        for part in range(parts):
            cells = slice(part * 128, part * 128 + 128)
            up_ref[owned + component * parts + part] = last[cells].T[120:]
            down_ref[owned + component * parts + part] = first[cells].T[:8]
        for group in range(levels // 4):
            head = tail = None
            for k in range(4):
                top = vel_ref[component, group * 4 + k, 0:8, :]
                end = vel_ref[component, group * 4 + k, rows - 8 : rows, :]
                if k:
                    top = pltpu.roll(top, 2 * k, 0)
                if k < 3:
                    end = pltpu.roll(end, 2 * k + 2, 0)
                head = top if head is None else jnp.where(row == k, top, head)
                tail = end if tail is None else jnp.where(row == k, end, tail)
            near_ref[component, group * 8 : group * 8 + 8, :] = jnp.where(odd, head, tail)
            ref, to = (far_ref, group * 8) if group * 8 < levels else (relay_ref, group * 8 - levels)
            ref[component, to : to + 8, :] = jnp.where(odd, tail, head)


def prep(velocity, blade_pos, block_turbine, blade_vel, lift_coeff):
    components, levels, rows, cols = velocity.shape
    owned, coords, points = blade_pos.shape
    tiles = owned + components * levels * rows // 128
    return pl.pallas_call(
        prep_kernel,
        in_specs=[pl.BlockSpec(memory_space=pltpu.HBM)] * 5,
        out_specs=[pl.BlockSpec(memory_space=pltpu.VMEM)] * 6,
        out_shape=[
            jax.ShapeDtypeStruct((owned, 8, points), F32),
            jax.ShapeDtypeStruct((tiles, 8, 128), F32),
            jax.ShapeDtypeStruct((tiles, 8, 128), F32),
            jax.ShapeDtypeStruct((components, 2 * levels, cols), F32),
            jax.ShapeDtypeStruct((components, levels, cols), F32),
            jax.ShapeDtypeStruct((components, levels, cols), F32),
        ],
        scratch_shapes=[
            pltpu.SMEM((owned,), jnp.int32),
            pltpu.VMEM((coords, owned, points), F32),
            pltpu.VMEM((coords, owned, points), F32),
            pltpu.VMEM((owned, points), F32),
            pltpu.VMEM(velocity.shape, F32),
            pltpu.SemaphoreType.DMA((components + 4,)),
        ],
        compiler_params=pltpu.CompilerParams(vmem_limit_bytes=60 * MIB),
        cost_estimate=LIGHT,
        name="prep",
    )(
        block_turbine,
        blade_pos.transpose(1, 0, 2),
        blade_vel.transpose(1, 0, 2),
        lift_coeff,
        velocity,
    )


def match(mine_ref, twin_ref, per_turbine):
    core = lax.axis_index("gz")
    turbine = lax.axis_index("gy").astype(F32)
    half = mine_ref.shape[0]
    first = [(mine_ref[k, 7:8, :] == turbine).astype(F32) for k in range(half)]
    second = [(twin_ref[k, 7:8, :] == turbine).astype(F32) for k in range(half)]
    masks = []
    for hits, others, leads in ((first, second, core == 0), (second, first, core == 1)):
        rank = jnp.where(leads, jnp.zeros_like(hits[0]), sum(others))
        for hit in hits:
            masks.append([(hit > 0.5) & (rank == k) for k in range(per_turbine)])
            rank = rank + hit
    return masks


def sample_kernel(
    per_turbine, mine_ref, twin_ref, vel_in, part_ref, own_ref, mask_ref, weight_out, lev_ref,
    even_ref, odd_ref, center_ref, plane_ref, acc_ref, vel_ref, weight_ref, sems, out_sems, lev_sem,
):
    components, depth, rows, cols = vel_ref.shape
    points = mine_ref.shape[2]
    count = per_turbine * points
    cells = depth * rows
    chunks = cols // STEP
    core = lax.axis_index("gz")
    start = lax.axis_index("gy") * cols

    def column(at):
        return pl.ds(pl.multiple_of(at * STEP, STEP), STEP)

    def column_copy(at):
        return pltpu.make_async_copy(
            vel_in.at[:, :, :, column(at)], vel_ref.at[:, :, :, column(at)], sems.at[at]
        )

    def weight_copy(at):
        return pltpu.make_async_copy(
            weight_ref.at[:, column(at)], weight_out.at[:, column(at)], out_sems.at[at]
        )

    lev_copy = pltpu.make_async_copy(
        vel_in.at[:, pl.ds(jnp.where(core == 0, depth - 2, 0), 2)], lev_ref, lev_sem
    )

    def bell(cell, center):
        gap = cell.astype(F32) - center
        return jnp.exp(gap * gap * (-1.0 / (smear * smear)))

    def weights(at, ref):
        lane = lax.broadcasted_iota(jnp.int32, (1, 128), 1)
        for part in range(STEP // 128):
            cell = start + at * STEP + part * 128 + lane
            ref[:, part * 128 : part * 128 + 128] = bell(cell, center_ref[...])

    def multiply(at, ref):
        for i in range(components):
            high, low = split(vel_ref[i, :, :, column(at)].reshape(cells, STEP))
            field = dot(plane_ref[...], jnp.concatenate([high, high, low], axis=0))
            product = field * ref[...]
            total = acc_ref[i]
            for part in range(STEP // 128):
                total += product[:, part * 128 : part * 128 + 128]
            acc_ref[i] = total
        high, low = split(ref[...])
        weight_ref[:count, column(at)] = high
        weight_ref[count:, column(at)] = low

    column_copy(0).start()
    column_copy(1).start()
    masks = match(mine_ref, twin_ref, per_turbine)
    blocks = mine_ref.shape[0]
    lane = lax.broadcasted_iota(jnp.int32, (1, cells), 1)
    level = core * depth + lane // rows
    row = lax.axis_index("gx") * rows + lane % rows
    for k in range(per_turbine):
        total = jnp.zeros((8, points), F32)
        for at, mask in enumerate(masks):
            tile = mine_ref[at] if at < blocks else twin_ref[at - blocks]
            total = jnp.where(mask[k], tile, total)
        band = slice(k * points, (k + 1) * points)
        own_ref[:, band] = total
        turned = total.T
        center_ref[band, :] = jnp.broadcast_to(turned[:, 1:2], (points, 128))
        plane = bell(row, turned[:, 0:1]) * bell(level, turned[:, 2:3])
        high, low = split(plane)
        plane_ref[band, :cells] = high
        plane_ref[band, cells : 2 * cells] = low
        plane_ref[band, 2 * cells :] = high
    for at in range(blocks):
        for k in range(per_turbine):
            mask_ref[at, k : k + 1, :] = masks[at][k].astype(F32)
    acc_ref[...] = jnp.zeros(acc_ref.shape, F32)
    weights(0, even_ref)

    def pair(step, carry):
        column_copy(2 * step).wait()
        column_copy(2 * step + 1).wait()

        @pl.when(step < chunks // 2 - 1)
        def _():
            column_copy(2 * step + 2).start()
            column_copy(2 * step + 3).start()

        @pl.when(step == chunks // 2 - 1)
        def _():
            lev_copy.start()

        weights(2 * step + 1, odd_ref)
        multiply(2 * step, even_ref)
        weights(2 * step + 2, even_ref)
        multiply(2 * step + 1, odd_ref)
        weight_copy(2 * step).start()
        weight_copy(2 * step + 1).start()
        return carry

    lax.fori_loop(0, chunks // 2, pair, 0)
    for i in range(components):
        for k in range(per_turbine):
            band = slice(k * points, (k + 1) * points)
            total = jnp.sum(acc_ref[i, band, :].T, axis=0, keepdims=True)
            part_ref[i : i + 1, band] = smear_norm * total
    part_ref[components:, :] = jnp.zeros((8 - components, count), F32)
    lev_copy.wait()
    for at in range(chunks):
        weight_copy(at).wait()


def sample(mine, twin, velocity, per_turbine):
    components, depth, rows, cols = velocity.shape
    points = mine.shape[2]
    count = per_turbine * points
    chunks = cols // STEP
    vmem = pl.BlockSpec(memory_space=pltpu.VMEM)
    hbm = pl.BlockSpec(memory_space=pltpu.HBM)
    return pl.pallas_call(
        functools.partial(sample_kernel, per_turbine),
        in_specs=[vmem, vmem, hbm],
        out_specs=[vmem, vmem, vmem, hbm, vmem],
        out_shape=[
            jax.ShapeDtypeStruct((8, count), F32),
            jax.ShapeDtypeStruct((8, count), F32),
            jax.ShapeDtypeStruct((mine.shape[0], per_turbine, points), F32),
            jax.ShapeDtypeStruct((2 * count, cols), BF16),
            jax.ShapeDtypeStruct((components, 2, rows, cols), F32),
        ],
        scratch_shapes=[
            pltpu.VMEM((count, STEP), F32),
            pltpu.VMEM((count, STEP), F32),
            pltpu.VMEM((count, 128), F32),
            pltpu.VMEM((count, 3 * depth * rows), BF16),
            pltpu.VMEM((components, count, 128), F32),
            pltpu.VMEM(velocity.shape, F32),
            pltpu.VMEM((2 * count, cols), BF16),
            pltpu.SemaphoreType.DMA((chunks,)),
            pltpu.SemaphoreType.DMA((chunks,)),
            pltpu.SemaphoreType.DMA,
        ],
        compiler_params=pltpu.CompilerParams(vmem_limit_bytes=58 * MIB),
        cost_estimate=LIGHT,
        name="sample",
    )(mine, twin, velocity)


def force_kernel(
    per_turbine, owned, mask_ref, part_ref, other_ref, own_ref, force_ref, home_ref
):
    points = own_ref.shape[1] // per_turbine
    relative = part_ref[0:3, :] + other_ref[0:3, :] - own_ref[3:6, :]
    speed = jnp.sqrt(jnp.sum(relative * relative, axis=0, keepdims=True))
    force = -own_ref[6:7, :] * speed * relative
    force_ref[...] = jnp.zeros(force_ref.shape, F32)
    force_ref[0:3, :] = force
    for row in range(mask_ref.shape[0]):
        total = jnp.zeros((3, points), F32)
        for k in range(per_turbine):
            total = jnp.where(mask_ref[row, k : k + 1, :] > 0.5, force[:, k * points : (k + 1) * points], total)
        for i in range(3):
            home_ref[row // owned, i, row % owned : row % owned + 1, :] = total[i : i + 1]


def point_forces(mask, part, other, own, per_turbine, owned):
    count = own.shape[1]
    points = count // per_turbine
    shifts = mask.shape[0] // owned
    return pl.pallas_call(
        functools.partial(force_kernel, per_turbine, owned),
        in_specs=[pl.BlockSpec(memory_space=pltpu.VMEM)] * 4,
        out_specs=[pl.BlockSpec(memory_space=pltpu.VMEM)] * 2,
        out_shape=[
            jax.ShapeDtypeStruct((8, count), F32),
            jax.ShapeDtypeStruct((shifts, 3, owned, points), F32),
        ],
        compiler_params=pltpu.CompilerParams(vmem_limit_bytes=58 * MIB),
        cost_estimate=LIGHT,
        name="force",
    )(mask, part, other, own)


def update_kernel(
    own_ref, force_ref, op_ref, left_ref, right_ref, near_in, far_in, relay_in, weight_in, vel_in, lev_in,
    new_out, zero_ref, pad_ref, new_ref, side_ref, weight_ref, high_ref, low_ref, even, odd,
    vel_sems, side_sems, weight_sems, new_sems, lev_sem,
):
    components, depth, rows, cols = new_ref.shape
    chunks = cols // STEP
    cells = LEVELS * rows
    inner = (LEVELS + 4) * rows
    fill = op_ref.shape[1] // 2 - inner - 4 * LEVELS
    count = own_ref.shape[1]
    core = lax.axis_index("gz")
    turbine = lax.axis_index("gy")
    parity = lax.axis_index("gx") % 2
    lane = lax.broadcasted_iota(jnp.int32, (8, 128), 1)
    shifts = ((1, lane < 1), (2, lane < 2), (127, lane >= 127), (126, lane >= 126))

    def column(at, first=0):
        return pl.ds(pl.multiple_of(at * STEP + first, 128), STEP)

    def arrivals(at):
        return [
            pltpu.make_async_copy(
                vel_in.at[:, :, :, column(at)],
                pad_ref.at[:, pl.ds(2, depth), :, column(at, 128)],
                vel_sems.at[at],
            ),
            pltpu.make_async_copy(
                weight_in.at[:, column(at)], weight_ref.at[:, column(at)], weight_sems.at[at]
            ),
            pltpu.make_async_copy(
                near_in.at[:, :, column(at)], side_ref.at[1 - parity, :, :, column(at)], side_sems.at[0, at]
            ),
            pltpu.make_async_copy(
                far_in.at[:, :, column(at)],
                side_ref.at[parity, :, pl.ds(0, depth), column(at)],
                side_sems.at[1, at],
            ),
            pltpu.make_async_copy(
                relay_in.at[:, :, column(at)],
                side_ref.at[parity, :, pl.ds(depth, depth), column(at)],
                side_sems.at[2, at],
            ),
        ]

    def departure(at):
        return pltpu.make_async_copy(
            new_ref.at[:, :, :, column(at)], new_out.at[:, :, :, column(at)], new_sems.at[at]
        )

    def level_copy(at):
        return pltpu.make_async_copy(
            lev_in, pad_ref.at[:, pl.ds(at, 2), :, pl.ds(128, cols)], lev_sem
        )

    def side_columns(ref, present, lane):
        per_part = 128 // rows
        parts = ref.shape[0] // components
        for tile in range(ref.shape[0]):
            turned = jnp.where(present, ref[tile], 0.0).T
            for k in range(per_part):
                level = (tile % parts) * per_part + k
                pad_ref[tile // parts, level + 2, :, lane : lane + 8] = turned[k * rows : (k + 1) * rows, :]

    def matrix_part(at, bufs):
        grad_ref, lap_ref, body_ref = bufs
        for i in range(components):
            for half in range(depth // LEVELS):
                levels = slice(half * LEVELS, (half + 1) * LEVELS)
                field = pad_ref[i, half * LEVELS : (half + 1) * LEVELS + 4, :, column(at, 128)]
                inner_high, inner_low = split(field.reshape(inner, STEP))
                side = slice(half * 2 * LEVELS, (half + 1) * 2 * LEVELS)
                prev_high, prev_low = split(side_ref[0, i, side, column(at)])
                next_high, next_low = split(side_ref[1, i, side, column(at)])
                empty = [jnp.zeros((fill, STEP), BF16)] if fill else []
                high = [inner_high, prev_high, next_high] + empty
                low = [inner_low, prev_low, next_low] + empty
                result = dot(op_ref[...], jnp.concatenate(high + low, axis=0))
                grad_ref[i, levels] = result[:cells].reshape(LEVELS, rows, STEP)
                lap_ref[i, levels] = result[cells:].reshape(LEVELS, rows, STEP)
        upper = weight_ref[:count, column(at)]
        lower = weight_ref[count:, column(at)]
        wide = jnp.concatenate([high_ref[...], low_ref[...], high_ref[...]], axis=1)
        result = dot(wide, jnp.concatenate([upper, upper, lower], axis=0))
        body_ref[...] = result.reshape(components, depth, rows, STEP)

    def vector_part(at, bufs):
        grad_ref, lap_ref, body_ref = bufs

        def cell(i, level, band, block):
            return pad_ref[i, level, band, pl.ds(pl.multiple_of(at * STEP + block * 128, 128), 128)]

        def work(level, band):
            here = level + 2
            turned = {}

            def turn(i, block, shift):
                if (i, block, shift) not in turned:
                    turned[i, block, shift] = pltpu.roll(cell(i, here, band, block), shift, 1)
                return turned[i, block, shift]

            for block in range(1, STEP // 128 + 1):
                lanes = slice(block * 128 - 128, block * 128)
                along_y, lap, along_z = [], [], []
                for i in range(components):
                    behind, behind2, ahead, ahead2 = [
                        jnp.where(
                            wrapped,
                            turn(i, block - 1 if shift < 64 else block + 1, shift),
                            turn(i, block, shift),
                        )
                        for shift, wrapped in shifts
                    ]
                    along_y.append(8.0 * (ahead - behind) - (ahead2 - behind2))
                    lap.append(
                        lap_ref[i, level, band, lanes]
                        + (16.0 * (ahead + behind) - (ahead2 + behind2))
                    )
                    near = cell(i, here + 1, band, block) - cell(i, here - 1, band, block)
                    far = cell(i, here + 2, band, block) - cell(i, here - 2, band, block)
                    along_z.append(8.0 * near - far)
                along_x = [grad_ref[i, level, band, lanes] for i in range(components)]
                same = along_x[0] * along_x[0] + along_y[1] * along_y[1] + along_z[2] * along_z[2]
                xy = along_x[1] + along_y[0]
                xz = along_x[2] + along_z[0]
                yz = along_y[2] + along_z[1]
                strain = 2.0 * same + (xy * xy + xz * xz + yz * yz)
                mixing = (time_step / 12.0) * viscosity + (
                    time_step * smag_coeff * smag_coeff / 144.0
                ) * jnp.sqrt(strain)
                out_lanes = pl.ds(pl.multiple_of(at * STEP + block * 128 - 128, 128), 128)
                for i in range(components):
                    change = mixing * lap[i] - (time_step * mean_wind / 12.0) * along_x[i]
                    new_ref[i, level, band, out_lanes] = (
                        cell(i, here, band, block) + body_ref[i, level, band, lanes] + change
                    )

        for level in range(depth):
            for row in range(0, rows, 8):
                work(level, slice(row, row + 8))
        departure(at).start()

    for copy in arrivals(0):
        copy.start()
    zero_ref[...] = jnp.zeros(zero_ref.shape, F32)

    @pl.when(core == 1)
    def _():
        level_copy(0).start()
        pad_ref[:, depth + 2 :, :, 128 : cols + 128] = jnp.zeros((components, 2, rows, cols), F32)

    @pl.when(core == 0)
    def _():
        level_copy(depth + 2).start()
        pad_ref[:, 0:2, :, 128 : cols + 128] = jnp.zeros((components, 2, rows, cols), F32)

    side_columns(left_ref, turbine > 0, 120)
    side_columns(right_ref, turbine < lax.axis_size("gy") - 1, cols + 128)
    along_x = gaussian(lax.axis_index("gx") * rows, rows, own_ref[0:1, :])
    along_z = gaussian(core * depth, depth, own_ref[2:3, :])
    for i in range(components):
        scaled = (time_step * smear_norm) * force_ref[i : i + 1, :] * along_x
        for level in range(depth):
            band = slice((i * depth + level) * rows, (i * depth + level + 1) * rows)
            high, low = split(scaled * along_z[level : level + 1, :])
            high_ref[band, :] = high
            low_ref[band, :] = low
    level_copy(0).wait()
    for copy in arrivals(0):
        copy.wait()
    for copy in arrivals(1) + arrivals(2):
        copy.start()
    matrix_part(0, even)

    def pair(step, carry):
        for copy in arrivals(2 * step + 1) + arrivals(2 * step + 2):
            copy.wait()
        for copy in arrivals(2 * step + 3):
            copy.start()

        @pl.when(step < chunks // 2 - 2)
        def _():
            for copy in arrivals(2 * step + 4):
                copy.start()

        matrix_part(2 * step + 1, odd)
        vector_part(2 * step, even)
        matrix_part(2 * step + 2, even)
        vector_part(2 * step + 1, odd)
        return carry

    lax.fori_loop(0, chunks // 2 - 1, pair, 0)
    for copy in arrivals(chunks - 1):
        copy.wait()
    matrix_part(chunks - 1, odd)
    vector_part(chunks - 2, even)
    vector_part(chunks - 1, odd)
    for at in range(chunks):
        departure(at).wait()


def update(own, force, operator, near, far, relay, weight, velocity, lev, left, right, home_shape):
    components, depth, rows, cols = velocity.shape
    count = own.shape[1]
    chunks = cols // STEP
    vmem = pl.BlockSpec(memory_space=pltpu.VMEM)
    hbm = pl.BlockSpec(memory_space=pltpu.HBM)
    fields = [pltpu.VMEM((components, depth, rows, STEP), F32)] * 3
    macs = components * depth * rows * cols * (3 * count + 4 * 256)
    return pl.pallas_call(
        update_kernel,
        in_specs=[vmem] * 5 + [hbm] * 6,
        out_specs=[hbm, vmem],
        out_shape=[
            jax.ShapeDtypeStruct(velocity.shape, F32),
            jax.ShapeDtypeStruct(home_shape, F32),
        ],
        scratch_shapes=[
            pltpu.VMEM((components, depth + 4, rows, cols + 256), F32),
            pltpu.VMEM(velocity.shape, F32),
            pltpu.VMEM((2, *near.shape), F32),
            pltpu.VMEM((2 * count, cols), BF16),
            pltpu.VMEM((components * depth * rows, count), BF16),
            pltpu.VMEM((components * depth * rows, count), BF16),
            fields,
            fields,
            pltpu.SemaphoreType.DMA((chunks,)),
            pltpu.SemaphoreType.DMA((3, chunks)),
            pltpu.SemaphoreType.DMA((chunks,)),
            pltpu.SemaphoreType.DMA((chunks,)),
            pltpu.SemaphoreType.DMA,
        ],
        compiler_params=pltpu.CompilerParams(vmem_limit_bytes=44 * MIB),
        cost_estimate=pl.CostEstimate(
            flops=2 * macs, bytes_accessed=8 * velocity.size, transcendentals=velocity.size // 3
        ),
        name="update",
    )(own, force, operator, left, right, near, far, relay, weight, velocity, lev)


def local(velocity, blade_pos, block_turbine, blade_vel, lift_coeff):
    components, depth, rows, cols = velocity.shape
    owned, _, points = blade_pos.shape
    gx, gy, gz = (lax.axis_size(axis) for axis in ("gx", "gy", "gz"))
    assert gz == 2 and depth == 2 * LEVELS
    per_turbine = owned * gz
    swap = [(0, 1), (1, 0)]

    def around(shift):
        return [(i, (i + shift) % gy) for i in range(gy)]

    blocks, up, down, near, far, relay = prep(
        velocity, blade_pos, block_turbine, blade_vel, lift_coeff
    )
    near = lax.ppermute(near, "gx", [(i, i ^ 1) for i in range(gx)])
    across = [(i, i + 1) for i in range(1, gx - 1, 2)] + [(i + 1, i) for i in range(1, gx - 1, 2)]
    if gx == 4:
        relay = lax.ppermute(relay, "gx", [(1, 3), (2, 0)])

    def gather(blocks, up, down):
        left = lax.ppermute(up, "gy", around(1))
        right = lax.ppermute(down, "gy", around(gy - 1))
        parts = [blocks, left[:owned]]
        parts += [lax.ppermute(blocks, "gy", around(shift)) for shift in range(2, gy - 1)]
        parts.append(right[:owned])
        mine = jnp.concatenate(parts, axis=0)
        return mine, lax.ppermute(mine, "gz", swap), left[owned:], right[owned:]

    def blade(mine, twin, velocity):
        part, own, mask, weight, facing = sample(mine, twin, velocity, per_turbine)
        other = lax.ppermute(part, "gz", swap)
        lev = lax.ppermute(facing, "gz", swap)
        force, home = point_forces(mask, part, other, own, per_turbine, owned)
        return own, force, home, weight, lev

    def stage(run, *operands):
        empty = [jnp.zeros(out.shape, out.dtype) for out in jax.eval_shape(run, *operands)]
        return lax.cond(block_turbine[0] >= 0, run, lambda *_: tuple(empty), *operands)

    mine, twin, left, right = stage(gather, blocks, up, down)
    if gx == 4:
        relay = lax.ppermute(relay, "gx", [(3, 2), (0, 1)])
    else:
        relay = lax.ppermute(relay, "gx", across)
    far = lax.ppermute(far, "gx", across)
    own, force, home, weight, lev = stage(blade, mine, twin, velocity)
    result = home[0]
    for shift in range(1, gy):
        result += lax.ppermute(home[shift], "gy", around(gy - shift))

    operator = jnp.asarray(stencil_operator(rows))
    new_velocity, zero = update(
        own, force, operator, near, far, relay, weight, velocity, lev, left, right, result.shape
    )
    return (new_velocity, (result + zero).transpose(1, 0, 2))


def solution(mesh):
    in_specs = (
        P(None, "gz", "gx", "gy"),
        P(("gx", "gy", "gz"), None, None),
        P(("gx", "gy", "gz")),
        P(("gx", "gy", "gz"), None, None),
        P(("gx", "gy", "gz"), None),
    )
    out_specs = (P(None, "gz", "gx", "gy"), P(("gx", "gy", "gz"), None, None))
    return jax.shard_map(local, mesh=mesh, in_specs=in_specs, out_specs=out_specs, check_vma=False)
```

```python
import functools
import math

import jax
import jax.numpy as jnp
import ml_dtypes
import numpy as np
from jax import lax
from jax.experimental import pallas as pl
from jax.experimental.pallas import tpu as pltpu
from jax.sharding import PartitionSpec as P

mean_wind = 1.0
viscosity = 0.2
smag_coeff = 0.17
time_step = 0.2
smear = 2.0
smear_norm = 1.0 / (smear**3 * math.pi**1.5)

F32 = jnp.float32
BF16 = jnp.bfloat16
MIB = 1024 * 1024
LEVELS = 8
STEP = 256
LIGHT = pl.CostEstimate(flops=0, bytes_accessed=0, transcendentals=0)


def split(value):
    high = value.astype(BF16)
    return high, (value - high.astype(F32)).astype(BF16)


def dot(left, right, contract=0):
    return lax.dot_general(
        left, right, (((1,), (contract,)), ((), ())), preferred_element_type=F32
    )


def gaussian(first, count, centers):
    shape = (count, centers.shape[1])
    cells = (first + lax.broadcasted_iota(jnp.int32, shape, 0)).astype(F32)
    gap = cells - centers
    return jnp.exp(-gap * gap / (smear * smear))


def stencil_operator(row_cells):
    inner = (LEVELS + 4) * row_cells
    width = inner + 4 * LEVELS
    op = np.zeros((2, LEVELS, row_cells, width), np.float32)

    def column(level, row):
        if 0 <= row < row_cells:
            return (level + 2) * row_cells + row
        if row < 0:
            return inner + level * 2 + row + 2
        return inner + 2 * LEVELS + level * 2 + row - row_cells

    for level in range(LEVELS):
        for row in range(row_cells):
            for offset, first, second in ((-2, 1, -1), (-1, -8, 16), (1, 8, 16), (2, -1, -1)):
                op[0, level, row, column(level, row + offset)] += first
                op[1, level, row, column(level, row + offset)] += second
                op[1, level, row, column(level + offset, row)] += second
            op[1, level, row, column(level, row)] -= 90
    op = op.reshape(2 * LEVELS * row_cells, width)
    op = np.pad(op, ((0, 0), (0, -width % 128)))
    return np.concatenate([op, op], axis=1).astype(ml_dtypes.bfloat16)


def prep_kernel(
    turb_in, pos_in, speed_in, lift_in, vel_in, blocks_ref, up_ref, down_ref, near_ref, far_ref, relay_ref,
    turb_ref, pos_ref, speed_ref, lift_ref, vel_ref, sems,
):
    components, levels, rows, cols = vel_ref.shape
    coords, owned, points = pos_ref.shape
    small = [
        pltpu.make_async_copy(source, target, sems.at[components + k])
        for k, (source, target) in enumerate(
            ((turb_in, turb_ref), (pos_in, pos_ref), (speed_in, speed_ref), (lift_in, lift_ref))
        )
    ]
    large = [
        pltpu.make_async_copy(vel_in.at[i], vel_ref.at[i], sems.at[i]) for i in range(components)
    ]
    for copy in small + large:
        copy.start()
    for copy in small:
        copy.wait()
    for ref in (blocks_ref, up_ref, down_ref):
        for k in range(owned):
            for i in range(coords):
                ref[k, i : i + 1, :] = pos_ref[i, k : k + 1, :]
                ref[k, coords + i : coords + i + 1, :] = speed_ref[i, k : k + 1, :]
            ref[k, 2 * coords : 2 * coords + 1, :] = lift_ref[k : k + 1, :]
            ref[k, 7:8, :] = jnp.full((1, points), turb_ref[k].astype(F32))
    parts = levels * rows // 128
    odd = lax.axis_index("gx") % 2 == 1
    row = lax.broadcasted_iota(jnp.int32, (8, cols), 0) // 2
    for component in range(components):
        large[component].wait()
        last = vel_ref[component, :, :, cols - 128 :].reshape(levels * rows, 128)
        first = vel_ref[component, :, :, :128].reshape(levels * rows, 128)
        for part in range(parts):
            cells = slice(part * 128, part * 128 + 128)
            up_ref[owned + component * parts + part] = last[cells].T[120:]
            down_ref[owned + component * parts + part] = first[cells].T[:8]
        for group in range(levels // 4):
            head = tail = None
            for k in range(4):
                top = vel_ref[component, group * 4 + k, 0:8, :]
                end = vel_ref[component, group * 4 + k, rows - 8 : rows, :]
                if k:
                    top = pltpu.roll(top, 2 * k, 0)
                if k < 3:
                    end = pltpu.roll(end, 2 * k + 2, 0)
                head = top if head is None else jnp.where(row == k, top, head)
                tail = end if tail is None else jnp.where(row == k, end, tail)
            near_ref[component, group * 8 : group * 8 + 8, :] = jnp.where(odd, head, tail)
            ref, to = (far_ref, group * 8) if group * 8 < levels else (relay_ref, group * 8 - levels)
            ref[component, to : to + 8, :] = jnp.where(odd, tail, head)


def prep(velocity, blade_pos, block_turbine, blade_vel, lift_coeff):
    components, levels, rows, cols = velocity.shape
    owned, coords, points = blade_pos.shape
    tiles = owned + components * levels * rows // 128
    return pl.pallas_call(
        prep_kernel,
        in_specs=[pl.BlockSpec(memory_space=pltpu.HBM)] * 5,
        out_specs=[pl.BlockSpec(memory_space=pltpu.VMEM)] * 6,
        out_shape=[
            jax.ShapeDtypeStruct((owned, 8, points), F32),
            jax.ShapeDtypeStruct((tiles, 8, 128), F32),
            jax.ShapeDtypeStruct((tiles, 8, 128), F32),
            jax.ShapeDtypeStruct((components, 2 * levels, cols), F32),
            jax.ShapeDtypeStruct((components, levels, cols), F32),
            jax.ShapeDtypeStruct((components, levels, cols), F32),
        ],
        scratch_shapes=[
            pltpu.SMEM((owned,), jnp.int32),
            pltpu.VMEM((coords, owned, points), F32),
            pltpu.VMEM((coords, owned, points), F32),
            pltpu.VMEM((owned, points), F32),
            pltpu.VMEM(velocity.shape, F32),
            pltpu.SemaphoreType.DMA((components + 4,)),
        ],
        compiler_params=pltpu.CompilerParams(vmem_limit_bytes=60 * MIB),
        cost_estimate=LIGHT,
        name="prep",
    )(
        block_turbine,
        blade_pos.transpose(1, 0, 2),
        blade_vel.transpose(1, 0, 2),
        lift_coeff,
        velocity,
    )


def match(mine_ref, twin_ref, per_turbine):
    core = lax.axis_index("gz")
    turbine = lax.axis_index("gy").astype(F32)
    half = mine_ref.shape[0]
    first = [(mine_ref[k, 7:8, :] == turbine).astype(F32) for k in range(half)]
    second = [(twin_ref[k, 7:8, :] == turbine).astype(F32) for k in range(half)]
    masks = []
    for hits, others, leads in ((first, second, core == 0), (second, first, core == 1)):
        rank = jnp.where(leads, jnp.zeros_like(hits[0]), sum(others))
        for hit in hits:
            masks.append([(hit > 0.5) & (rank == k) for k in range(per_turbine)])
            rank = rank + hit
    return masks


def sample_kernel(
    per_turbine, mine_ref, twin_ref, vel_in, part_ref, own_ref, mask_ref, weight_out, lev_ref,
    even_ref, odd_ref, center_ref, plane_ref, acc_ref, vel_ref, weight_ref, sems, out_sems, lev_sem,
):
    components, depth, rows, cols = vel_ref.shape
    points = mine_ref.shape[2]
    count = per_turbine * points
    cells = depth * rows
    chunks = cols // STEP
    core = lax.axis_index("gz")
    start = lax.axis_index("gy") * cols

    def column(at):
        return pl.ds(pl.multiple_of(at * STEP, STEP), STEP)

    def column_copy(at):
        return pltpu.make_async_copy(
            vel_in.at[:, :, :, column(at)], vel_ref.at[:, :, :, column(at)], sems.at[at]
        )

    def weight_copy(at):
        return pltpu.make_async_copy(
            weight_ref.at[:, column(at)], weight_out.at[:, column(at)], out_sems.at[at]
        )

    lev_copy = pltpu.make_async_copy(
        vel_in.at[:, pl.ds(jnp.where(core == 0, depth - 2, 0), 2)], lev_ref, lev_sem
    )

    def bell(cell, center):
        gap = cell.astype(F32) - center
        return jnp.exp(gap * gap * (-1.0 / (smear * smear)))

    def weights(at, ref):
        lane = lax.broadcasted_iota(jnp.int32, (1, 128), 1)
        for part in range(STEP // 128):
            cell = start + at * STEP + part * 128 + lane
            ref[:, part * 128 : part * 128 + 128] = bell(cell, center_ref[...])

    def multiply(at, ref):
        vel = vel_ref.at[:, :, :, column(at)]
        out = weight_ref.at[:, column(at)]
        for i in range(components):
            high, low = split(vel[i].reshape(cells, STEP))
            field = dot(plane_ref[...], jnp.concatenate([high, high, low], axis=0))
            product = field * ref[...]
            total = acc_ref[i]
            for part in range(STEP // 128):
                total += product[:, part * 128 : part * 128 + 128]
            acc_ref[i] = total
        high, low = split(ref[...])
        out[:count, :] = high
        out[count:, :] = low

    column_copy(0).start()
    column_copy(1).start()
    masks = match(mine_ref, twin_ref, per_turbine)
    blocks = mine_ref.shape[0]
    lane = lax.broadcasted_iota(jnp.int32, (1, cells), 1)
    level = core * depth + lane // rows
    row = lax.axis_index("gx") * rows + lane % rows
    for k in range(per_turbine):
        total = jnp.zeros((8, points), F32)
        for at, mask in enumerate(masks):
            tile = mine_ref[at] if at < blocks else twin_ref[at - blocks]
            total = jnp.where(mask[k], tile, total)
        band = slice(k * points, (k + 1) * points)
        own_ref[:, band] = total
        turned = total.T
        center_ref[band, :] = jnp.broadcast_to(turned[:, 1:2], (points, 128))
        plane = bell(row, turned[:, 0:1]) * bell(level, turned[:, 2:3])
        high, low = split(plane)
        plane_ref[band, :cells] = high
        plane_ref[band, cells : 2 * cells] = low
        plane_ref[band, 2 * cells :] = high
    for at in range(blocks):
        for k in range(per_turbine):
            mask_ref[at, k : k + 1, :] = masks[at][k].astype(F32)
    acc_ref[...] = jnp.zeros(acc_ref.shape, F32)
    weights(0, even_ref)

    def pair(step, carry):
        column_copy(2 * step).wait()
        column_copy(2 * step + 1).wait()

        @pl.when(step < chunks // 2 - 1)
        def _():
            column_copy(2 * step + 2).start()
            column_copy(2 * step + 3).start()

        @pl.when(step == chunks // 2 - 1)
        def _():
            lev_copy.start()

        weights(2 * step + 1, odd_ref)
        multiply(2 * step, even_ref)
        weights(2 * step + 2, even_ref)
        multiply(2 * step + 1, odd_ref)
        weight_copy(2 * step).start()
        weight_copy(2 * step + 1).start()
        return carry

    lax.fori_loop(0, chunks // 2, pair, 0)
    for i in range(components):
        for k in range(per_turbine):
            band = slice(k * points, (k + 1) * points)
            total = jnp.sum(acc_ref[i, band, :].T, axis=0, keepdims=True)
            part_ref[i : i + 1, band] = smear_norm * total
    part_ref[components:, :] = jnp.zeros((8 - components, count), F32)
    lev_copy.wait()
    for at in range(chunks):
        weight_copy(at).wait()


def sample(mine, twin, velocity, per_turbine):
    components, depth, rows, cols = velocity.shape
    points = mine.shape[2]
    count = per_turbine * points
    chunks = cols // STEP
    vmem = pl.BlockSpec(memory_space=pltpu.VMEM)
    hbm = pl.BlockSpec(memory_space=pltpu.HBM)
    return pl.pallas_call(
        functools.partial(sample_kernel, per_turbine),
        in_specs=[vmem, vmem, hbm],
        out_specs=[vmem, vmem, vmem, hbm, vmem],
        out_shape=[
            jax.ShapeDtypeStruct((8, count), F32),
            jax.ShapeDtypeStruct((8, count), F32),
            jax.ShapeDtypeStruct((mine.shape[0], per_turbine, points), F32),
            jax.ShapeDtypeStruct((2 * count, cols), BF16),
            jax.ShapeDtypeStruct((components, 2, rows, cols), F32),
        ],
        scratch_shapes=[
            pltpu.VMEM((count, STEP), F32),
            pltpu.VMEM((count, STEP), F32),
            pltpu.VMEM((count, 128), F32),
            pltpu.VMEM((count, 3 * depth * rows), BF16),
            pltpu.VMEM((components, count, 128), F32),
            pltpu.VMEM(velocity.shape, F32),
            pltpu.VMEM((2 * count, cols), BF16),
            pltpu.SemaphoreType.DMA((chunks,)),
            pltpu.SemaphoreType.DMA((chunks,)),
            pltpu.SemaphoreType.DMA,
        ],
        compiler_params=pltpu.CompilerParams(vmem_limit_bytes=58 * MIB),
        cost_estimate=LIGHT,
        name="sample",
    )(mine, twin, velocity)


def force_kernel(
    per_turbine, owned, mask_ref, part_ref, other_ref, own_ref, force_ref, home_ref
):
    points = own_ref.shape[1] // per_turbine
    relative = part_ref[0:3, :] + other_ref[0:3, :] - own_ref[3:6, :]
    speed = jnp.sqrt(jnp.sum(relative * relative, axis=0, keepdims=True))
    force = -own_ref[6:7, :] * speed * relative
    force_ref[...] = jnp.zeros(force_ref.shape, F32)
    force_ref[0:3, :] = force
    for row in range(mask_ref.shape[0]):
        total = jnp.zeros((3, points), F32)
        for k in range(per_turbine):
            total = jnp.where(mask_ref[row, k : k + 1, :] > 0.5, force[:, k * points : (k + 1) * points], total)
        for i in range(3):
            home_ref[row // owned, i, row % owned : row % owned + 1, :] = total[i : i + 1]


def point_forces(mask, part, other, own, per_turbine, owned):
    count = own.shape[1]
    points = count // per_turbine
    shifts = mask.shape[0] // owned
    return pl.pallas_call(
        functools.partial(force_kernel, per_turbine, owned),
        in_specs=[pl.BlockSpec(memory_space=pltpu.VMEM)] * 4,
        out_specs=[pl.BlockSpec(memory_space=pltpu.VMEM)] * 2,
        out_shape=[
            jax.ShapeDtypeStruct((8, count), F32),
            jax.ShapeDtypeStruct((shifts, 3, owned, points), F32),
        ],
        compiler_params=pltpu.CompilerParams(vmem_limit_bytes=58 * MIB),
        cost_estimate=LIGHT,
        name="force",
    )(mask, part, other, own)


def update_kernel(
    own_ref, force_ref, op_ref, left_ref, right_ref, near_in, far_in, relay_in, weight_in, vel_in, lev_in,
    new_out, zero_ref, pad_ref, new_ref, side_ref, weight_ref, high_ref, low_ref, even, odd,
    vel_sems, side_sems, weight_sems, new_sems, lev_sem,
):
    components, depth, rows, cols = new_ref.shape
    chunks = cols // STEP
    cells = LEVELS * rows
    inner = (LEVELS + 4) * rows
    fill = op_ref.shape[1] // 2 - inner - 4 * LEVELS
    count = own_ref.shape[1]
    core = lax.axis_index("gz")
    turbine = lax.axis_index("gy")
    parity = lax.axis_index("gx") % 2
    lane = lax.broadcasted_iota(jnp.int32, (8, 128), 1)
    shifts = ((1, lane < 1), (2, lane < 2), (127, lane >= 127), (126, lane >= 126))

    def column(at, first=0):
        return pl.ds(pl.multiple_of(at * STEP + first, 128), STEP)

    def arrivals(at):
        return [
            pltpu.make_async_copy(
                vel_in.at[:, :, :, column(at)],
                pad_ref.at[:, pl.ds(2, depth), :, column(at, 128)],
                vel_sems.at[at],
            ),
            pltpu.make_async_copy(
                weight_in.at[:, column(at)], weight_ref.at[:, column(at)], weight_sems.at[at]
            ),
            pltpu.make_async_copy(
                near_in.at[:, :, column(at)], side_ref.at[1 - parity, :, :, column(at)], side_sems.at[0, at]
            ),
            pltpu.make_async_copy(
                far_in.at[:, :, column(at)],
                side_ref.at[parity, :, pl.ds(0, depth), column(at)],
                side_sems.at[1, at],
            ),
            pltpu.make_async_copy(
                relay_in.at[:, :, column(at)],
                side_ref.at[parity, :, pl.ds(depth, depth), column(at)],
                side_sems.at[2, at],
            ),
        ]

    def departure(at):
        return pltpu.make_async_copy(
            new_ref.at[:, :, :, column(at)], new_out.at[:, :, :, column(at)], new_sems.at[at]
        )

    def level_copy(at):
        return pltpu.make_async_copy(
            lev_in, pad_ref.at[:, pl.ds(at, 2), :, pl.ds(128, cols)], lev_sem
        )

    def side_columns(ref, present, lane):
        per_part = 128 // rows
        parts = ref.shape[0] // components
        for tile in range(ref.shape[0]):
            turned = jnp.where(present, ref[tile], 0.0).T
            for k in range(per_part):
                level = (tile % parts) * per_part + k
                pad_ref[tile // parts, level + 2, :, lane : lane + 8] = turned[k * rows : (k + 1) * rows, :]

    def matrix_part(at, bufs):
        grad_ref, lap_ref, body_ref = bufs
        pad = pad_ref.at[:, :, :, column(at, 128)]
        sides = side_ref.at[:, :, :, column(at)]
        weight = weight_ref.at[:, column(at)]
        for i in range(components):
            for half in range(depth // LEVELS):
                levels = slice(half * LEVELS, (half + 1) * LEVELS)
                field = pad[i, half * LEVELS : (half + 1) * LEVELS + 4]
                inner_high, inner_low = split(field.reshape(inner, STEP))
                side = slice(half * 2 * LEVELS, (half + 1) * 2 * LEVELS)
                prev_high, prev_low = split(sides[0, i, side])
                next_high, next_low = split(sides[1, i, side])
                empty = [jnp.zeros((fill, STEP), BF16)] if fill else []
                high = [inner_high, prev_high, next_high] + empty
                low = [inner_low, prev_low, next_low] + empty
                result = dot(op_ref[...], jnp.concatenate(high + low, axis=0))
                grad_ref[i, levels] = result[:cells].reshape(LEVELS, rows, STEP)
                lap_ref[i, levels] = result[cells:].reshape(LEVELS, rows, STEP)
        upper = weight[:count]
        lower = weight[count:]
        wide = jnp.concatenate([high_ref[...], low_ref[...], high_ref[...]], axis=1)
        result = dot(wide, jnp.concatenate([upper, upper, lower], axis=0))
        body_ref[...] = result.reshape(components, depth, rows, STEP)

    def vector_part(at, bufs):
        grad_ref, lap_ref, body_ref = bufs
        pad = pad_ref.at[:, :, :, pl.ds(pl.multiple_of(at * STEP, 128), STEP + 256)]
        new = new_ref.at[:, :, :, column(at)]

        def cell(i, level, band, block):
            return pad[i, level, band, block * 128 : block * 128 + 128]

        def work(level, band):
            here = level + 2
            turned = {}

            def turn(i, block, shift):
                if (i, block, shift) not in turned:
                    turned[i, block, shift] = pltpu.roll(cell(i, here, band, block), shift, 1)
                return turned[i, block, shift]

            for block in range(1, STEP // 128 + 1):
                lanes = slice(block * 128 - 128, block * 128)
                along_y, lap, along_z = [], [], []
                for i in range(components):
                    behind, behind2, ahead, ahead2 = [
                        jnp.where(
                            wrapped,
                            turn(i, block - 1 if shift < 64 else block + 1, shift),
                            turn(i, block, shift),
                        )
                        for shift, wrapped in shifts
                    ]
                    along_y.append(8.0 * (ahead - behind) - (ahead2 - behind2))
                    lap.append(
                        lap_ref[i, level, band, lanes]
                        + (16.0 * (ahead + behind) - (ahead2 + behind2))
                    )
                    near = cell(i, here + 1, band, block) - cell(i, here - 1, band, block)
                    far = cell(i, here + 2, band, block) - cell(i, here - 2, band, block)
                    along_z.append(8.0 * near - far)
                along_x = [grad_ref[i, level, band, lanes] for i in range(components)]
                same = along_x[0] * along_x[0] + along_y[1] * along_y[1] + along_z[2] * along_z[2]
                xy = along_x[1] + along_y[0]
                xz = along_x[2] + along_z[0]
                yz = along_y[2] + along_z[1]
                strain = 2.0 * same + (xy * xy + xz * xz + yz * yz)
                mixing = (time_step / 12.0) * viscosity + (
                    time_step * smag_coeff * smag_coeff / 144.0
                ) * jnp.sqrt(strain)
                for i in range(components):
                    change = mixing * lap[i] - (time_step * mean_wind / 12.0) * along_x[i]
                    new[i, level, band, lanes] = (
                        cell(i, here, band, block) + body_ref[i, level, band, lanes] + change
                    )

        for level in range(depth):
            for row in range(0, rows, 8):
                work(level, slice(row, row + 8))
        departure(at).start()

    for copy in arrivals(0):
        copy.start()
    zero_ref[...] = jnp.zeros(zero_ref.shape, F32)

    @pl.when(core == 1)
    def _():
        level_copy(0).start()
        pad_ref[:, depth + 2 :, :, 128 : cols + 128] = jnp.zeros((components, 2, rows, cols), F32)

    @pl.when(core == 0)
    def _():
        level_copy(depth + 2).start()
        pad_ref[:, 0:2, :, 128 : cols + 128] = jnp.zeros((components, 2, rows, cols), F32)

    side_columns(left_ref, turbine > 0, 120)
    side_columns(right_ref, turbine < lax.axis_size("gy") - 1, cols + 128)
    along_x = gaussian(lax.axis_index("gx") * rows, rows, own_ref[0:1, :])
    along_z = gaussian(core * depth, depth, own_ref[2:3, :])
    for i in range(components):
        scaled = (time_step * smear_norm) * force_ref[i : i + 1, :] * along_x
        for level in range(depth):
            band = slice((i * depth + level) * rows, (i * depth + level + 1) * rows)
            high, low = split(scaled * along_z[level : level + 1, :])
            high_ref[band, :] = high
            low_ref[band, :] = low
    level_copy(0).wait()
    for copy in arrivals(0):
        copy.wait()
    for copy in arrivals(1) + arrivals(2):
        copy.start()
    matrix_part(0, even)

    def pair(step, carry):
        for copy in arrivals(2 * step + 1) + arrivals(2 * step + 2):
            copy.wait()
        for copy in arrivals(2 * step + 3):
            copy.start()

        @pl.when(step < chunks // 2 - 2)
        def _():
            for copy in arrivals(2 * step + 4):
                copy.start()

        matrix_part(2 * step + 1, odd)
        vector_part(2 * step, even)
        matrix_part(2 * step + 2, even)
        vector_part(2 * step + 1, odd)
        return carry

    lax.fori_loop(0, chunks // 2 - 1, pair, 0)
    for copy in arrivals(chunks - 1):
        copy.wait()
    matrix_part(chunks - 1, odd)
    vector_part(chunks - 2, even)
    vector_part(chunks - 1, odd)
    for at in range(chunks):
        departure(at).wait()


def update(own, force, operator, near, far, relay, weight, velocity, lev, left, right, home_shape):
    components, depth, rows, cols = velocity.shape
    count = own.shape[1]
    chunks = cols // STEP
    vmem = pl.BlockSpec(memory_space=pltpu.VMEM)
    hbm = pl.BlockSpec(memory_space=pltpu.HBM)
    fields = [pltpu.VMEM((components, depth, rows, STEP), F32)] * 3
    macs = components * depth * rows * cols * (3 * count + 4 * 256)
    return pl.pallas_call(
        update_kernel,
        in_specs=[vmem] * 5 + [hbm] * 6,
        out_specs=[hbm, vmem],
        out_shape=[
            jax.ShapeDtypeStruct(velocity.shape, F32),
            jax.ShapeDtypeStruct(home_shape, F32),
        ],
        scratch_shapes=[
            pltpu.VMEM((components, depth + 4, rows, cols + 256), F32),
            pltpu.VMEM(velocity.shape, F32),
            pltpu.VMEM((2, *near.shape), F32),
            pltpu.VMEM((2 * count, cols), BF16),
            pltpu.VMEM((components * depth * rows, count), BF16),
            pltpu.VMEM((components * depth * rows, count), BF16),
            fields,
            fields,
            pltpu.SemaphoreType.DMA((chunks,)),
            pltpu.SemaphoreType.DMA((3, chunks)),
            pltpu.SemaphoreType.DMA((chunks,)),
            pltpu.SemaphoreType.DMA((chunks,)),
            pltpu.SemaphoreType.DMA,
        ],
        compiler_params=pltpu.CompilerParams(vmem_limit_bytes=44 * MIB),
        cost_estimate=pl.CostEstimate(
            flops=2 * macs, bytes_accessed=8 * velocity.size, transcendentals=velocity.size // 3
        ),
        name="update",
    )(own, force, operator, left, right, near, far, relay, weight, velocity, lev)


def local(velocity, blade_pos, block_turbine, blade_vel, lift_coeff):
    components, depth, rows, cols = velocity.shape
    owned, _, points = blade_pos.shape
    gx, gy, gz = (lax.axis_size(axis) for axis in ("gx", "gy", "gz"))
    assert gz == 2 and depth == 2 * LEVELS
    per_turbine = owned * gz
    swap = [(0, 1), (1, 0)]

    def around(shift):
        return [(i, (i + shift) % gy) for i in range(gy)]

    blocks, up, down, near, far, relay = prep(
        velocity, blade_pos, block_turbine, blade_vel, lift_coeff
    )
    near = lax.ppermute(near, "gx", [(i, i ^ 1) for i in range(gx)])
    across = [(i, i + 1) for i in range(1, gx - 1, 2)] + [(i + 1, i) for i in range(1, gx - 1, 2)]
    if gx == 4:
        relay = lax.ppermute(relay, "gx", [(1, 3), (2, 0)])

    def gather(blocks, up, down):
        left = lax.ppermute(up, "gy", around(1))
        right = lax.ppermute(down, "gy", around(gy - 1))
        parts = [blocks, left[:owned]]
        parts += [lax.ppermute(blocks, "gy", around(shift)) for shift in range(2, gy - 1)]
        parts.append(right[:owned])
        mine = jnp.concatenate(parts, axis=0)
        return mine, lax.ppermute(mine, "gz", swap), left[owned:], right[owned:]

    def blade(mine, twin, velocity):
        part, own, mask, weight, facing = sample(mine, twin, velocity, per_turbine)
        other = lax.ppermute(part, "gz", swap)
        lev = lax.ppermute(facing, "gz", swap)
        force, home = point_forces(mask, part, other, own, per_turbine, owned)
        return own, force, home, weight, lev

    def stage(run, *operands):
        empty = [jnp.zeros(out.shape, out.dtype) for out in jax.eval_shape(run, *operands)]
        return lax.cond(block_turbine[0] >= 0, run, lambda *_: tuple(empty), *operands)

    mine, twin, left, right = stage(gather, blocks, up, down)
    if gx == 4:
        relay = lax.ppermute(relay, "gx", [(3, 2), (0, 1)])
    else:
        relay = lax.ppermute(relay, "gx", across)
    far = lax.ppermute(far, "gx", across)
    own, force, home, weight, lev = stage(blade, mine, twin, velocity)
    result = home[0]
    for shift in range(1, gy):
        result += lax.ppermute(home[shift], "gy", around(gy - shift))

    operator = jnp.asarray(stencil_operator(rows))
    new_velocity, zero = update(
        own, force, operator, near, far, relay, weight, velocity, lev, left, right, result.shape
    )
    return (new_velocity, (result + zero).transpose(1, 0, 2))


def solution(mesh):
    in_specs = (
        P(None, "gz", "gx", "gy"),
        P(("gx", "gy", "gz"), None, None),
        P(("gx", "gy", "gz")),
        P(("gx", "gy", "gz"), None, None),
        P(("gx", "gy", "gz"), None),
    )
    out_specs = (P(None, "gz", "gx", "gy"), P(("gx", "gy", "gz"), None, None))
    return jax.shard_map(local, mesh=mesh, in_specs=in_specs, out_specs=out_specs, check_vma=False)
```

```python
import functools
import math

import jax
import jax.numpy as jnp
import ml_dtypes
import numpy as np
from jax import lax
from jax.experimental import pallas as pl
from jax.experimental.pallas import tpu as pltpu
from jax.sharding import PartitionSpec as P

mean_wind = 1.0
viscosity = 0.2
smag_coeff = 0.17
time_step = 0.2
smear = 2.0
smear_norm = 1.0 / (smear**3 * math.pi**1.5)

F32 = jnp.float32
BF16 = jnp.bfloat16
MIB = 1024 * 1024
LEVELS = 8
STEP = 256
LIGHT = pl.CostEstimate(flops=0, bytes_accessed=0, transcendentals=0)


def split(value):
    high = value.astype(BF16)
    return high, (value - high.astype(F32)).astype(BF16)


def dot(left, right, contract=0):
    return lax.dot_general(
        left, right, (((1,), (contract,)), ((), ())), preferred_element_type=F32
    )


def gaussian(first, count, centers):
    shape = (count, centers.shape[1])
    cells = (first + lax.broadcasted_iota(jnp.int32, shape, 0)).astype(F32)
    gap = cells - centers
    return jnp.exp(-gap * gap / (smear * smear))


def stencil_operator(row_cells):
    inner = (LEVELS + 4) * row_cells
    width = inner + 4 * LEVELS
    op = np.zeros((2, LEVELS, row_cells, width), np.float32)

    def column(level, row):
        if 0 <= row < row_cells:
            return (level + 2) * row_cells + row
        if row < 0:
            return inner + level * 2 + row + 2
        return inner + 2 * LEVELS + level * 2 + row - row_cells

    for level in range(LEVELS):
        for row in range(row_cells):
            for offset, first, second in ((-2, 1, -1), (-1, -8, 16), (1, 8, 16), (2, -1, -1)):
                op[0, level, row, column(level, row + offset)] += first
                op[1, level, row, column(level, row + offset)] += second
                op[1, level, row, column(level + offset, row)] += second
            op[1, level, row, column(level, row)] -= 90
    op = op.reshape(2 * LEVELS * row_cells, width)
    op = np.pad(op, ((0, 0), (0, -width % 128)))
    return np.concatenate([op, op], axis=1).astype(ml_dtypes.bfloat16)


def prep_kernel(
    turb_in, pos_in, speed_in, lift_in, vel_in, blocks_ref, up_ref, down_ref, near_ref, far_ref, relay_ref,
    turb_ref, pos_ref, speed_ref, lift_ref, vel_ref, sems,
):
    components, levels, rows, cols = vel_ref.shape
    coords, owned, points = pos_ref.shape
    small = [
        pltpu.make_async_copy(source, target, sems.at[components + k])
        for k, (source, target) in enumerate(
            ((turb_in, turb_ref), (pos_in, pos_ref), (speed_in, speed_ref), (lift_in, lift_ref))
        )
    ]
    large = [
        pltpu.make_async_copy(vel_in.at[i], vel_ref.at[i], sems.at[i]) for i in range(components)
    ]
    for copy in small + large:
        copy.start()
    for copy in small:
        copy.wait()
    for ref in (blocks_ref, up_ref, down_ref):
        for k in range(owned):
            for i in range(coords):
                ref[k, i : i + 1, :] = pos_ref[i, k : k + 1, :]
                ref[k, coords + i : coords + i + 1, :] = speed_ref[i, k : k + 1, :]
            ref[k, 2 * coords : 2 * coords + 1, :] = lift_ref[k : k + 1, :]
            ref[k, 7:8, :] = jnp.full((1, points), turb_ref[k].astype(F32))
    parts = levels * rows // 128
    odd = lax.axis_index("gx") % 2 == 1
    row = lax.broadcasted_iota(jnp.int32, (8, cols), 0) // 2
    for component in range(components):
        large[component].wait()
        last = vel_ref[component, :, :, cols - 128 :].reshape(levels * rows, 128)
        first = vel_ref[component, :, :, :128].reshape(levels * rows, 128)
        for part in range(parts):
            cells = slice(part * 128, part * 128 + 128)
            up_ref[owned + component * parts + part] = last[cells].T[120:]
            down_ref[owned + component * parts + part] = first[cells].T[:8]
        for group in range(levels // 4):
            head = tail = None
            for k in range(4):
                top = vel_ref[component, group * 4 + k, 0:8, :]
                end = vel_ref[component, group * 4 + k, rows - 8 : rows, :]
                if k:
                    top = pltpu.roll(top, 2 * k, 0)
                if k < 3:
                    end = pltpu.roll(end, 2 * k + 2, 0)
                head = top if head is None else jnp.where(row == k, top, head)
                tail = end if tail is None else jnp.where(row == k, end, tail)
            near_ref[component, group * 8 : group * 8 + 8, :] = jnp.where(odd, head, tail)
            ref, to = (far_ref, group * 8) if group * 8 < levels else (relay_ref, group * 8 - levels)
            ref[component, to : to + 8, :] = jnp.where(odd, tail, head)


def prep(velocity, blade_pos, block_turbine, blade_vel, lift_coeff):
    components, levels, rows, cols = velocity.shape
    owned, coords, points = blade_pos.shape
    tiles = owned + components * levels * rows // 128
    return pl.pallas_call(
        prep_kernel,
        in_specs=[pl.BlockSpec(memory_space=pltpu.HBM)] * 5,
        out_specs=[pl.BlockSpec(memory_space=pltpu.VMEM)] * 6,
        out_shape=[
            jax.ShapeDtypeStruct((owned, 8, points), F32),
            jax.ShapeDtypeStruct((tiles, 8, 128), F32),
            jax.ShapeDtypeStruct((tiles, 8, 128), F32),
            jax.ShapeDtypeStruct((components, 2 * levels, cols), F32),
            jax.ShapeDtypeStruct((components, levels, cols), F32),
            jax.ShapeDtypeStruct((components, levels, cols), F32),
        ],
        scratch_shapes=[
            pltpu.SMEM((owned,), jnp.int32),
            pltpu.VMEM((coords, owned, points), F32),
            pltpu.VMEM((coords, owned, points), F32),
            pltpu.VMEM((owned, points), F32),
            pltpu.VMEM(velocity.shape, F32),
            pltpu.SemaphoreType.DMA((components + 4,)),
        ],
        compiler_params=pltpu.CompilerParams(vmem_limit_bytes=60 * MIB),
        cost_estimate=LIGHT,
        name="prep",
    )(
        block_turbine,
        blade_pos.transpose(1, 0, 2),
        blade_vel.transpose(1, 0, 2),
        lift_coeff,
        velocity,
    )


def match(mine_ref, twin_ref, per_turbine):
    core = lax.axis_index("gz")
    turbine = lax.axis_index("gy").astype(F32)
    half = mine_ref.shape[0]
    first = [(mine_ref[k, 7:8, :] == turbine).astype(F32) for k in range(half)]
    second = [(twin_ref[k, 7:8, :] == turbine).astype(F32) for k in range(half)]
    masks = []
    for hits, others, leads in ((first, second, core == 0), (second, first, core == 1)):
        rank = jnp.where(leads, jnp.zeros_like(hits[0]), sum(others))
        for hit in hits:
            masks.append([(hit > 0.5) & (rank == k) for k in range(per_turbine)])
            rank = rank + hit
    return masks


def sample_kernel(
    per_turbine, mine_ref, twin_ref, vel_in, part_ref, own_ref, mask_ref, weight_out, lev_ref,
    even_ref, odd_ref, center_ref, plane_ref, acc_ref, vel_ref, weight_ref, sems, out_sems, lev_sem,
):
    components, depth, rows, cols = vel_ref.shape
    points = mine_ref.shape[2]
    count = per_turbine * points
    cells = depth * rows
    chunks = cols // STEP
    core = lax.axis_index("gz")
    start = lax.axis_index("gy") * cols

    def column(at):
        return pl.ds(pl.multiple_of(at * STEP, STEP), STEP)

    def column_copy(at):
        return pltpu.make_async_copy(
            vel_in.at[:, :, :, column(at)], vel_ref.at[:, :, :, column(at)], sems.at[at]
        )

    def weight_copy(at):
        return pltpu.make_async_copy(
            weight_ref.at[:, column(at)], weight_out.at[:, column(at)], out_sems.at[at]
        )

    lev_copy = pltpu.make_async_copy(
        vel_in.at[:, pl.ds(jnp.where(core == 0, depth - 2, 0), 2)], lev_ref, lev_sem
    )

    def bell(cell, center):
        gap = cell.astype(F32) - center
        return jnp.exp(gap * gap * (-1.0 / (smear * smear)))

    def weights(at, ref):
        lane = lax.broadcasted_iota(jnp.int32, (1, 128), 1)
        for part in range(STEP // 128):
            cell = start + at * STEP + part * 128 + lane
            ref[:, part * 128 : part * 128 + 128] = bell(cell, center_ref[...])

    def multiply(at, ref):
        vel = vel_ref.at[:, :, :, column(at)]
        out = weight_ref.at[:, column(at)]
        for i in range(components):
            high, low = split(vel[i].reshape(cells, STEP))
            field = dot(plane_ref[...], jnp.concatenate([high, high, low], axis=0))
            product = field * ref[...]
            total = acc_ref[i]
            for part in range(STEP // 128):
                total += product[:, part * 128 : part * 128 + 128]
            acc_ref[i] = total
        high, low = split(ref[...])
        out[:count, :] = high
        out[count:, :] = low

    column_copy(0).start()
    column_copy(1).start()
    masks = match(mine_ref, twin_ref, per_turbine)
    blocks = mine_ref.shape[0]
    lane = lax.broadcasted_iota(jnp.int32, (1, cells), 1)
    level = core * depth + lane // rows
    row = lax.axis_index("gx") * rows + lane % rows
    for k in range(per_turbine):
        total = jnp.zeros((8, points), F32)
        for at, mask in enumerate(masks):
            tile = mine_ref[at] if at < blocks else twin_ref[at - blocks]
            total = jnp.where(mask[k], tile, total)
        band = slice(k * points, (k + 1) * points)
        own_ref[:, band] = total
        turned = total.T
        center_ref[band, :] = jnp.broadcast_to(turned[:, 1:2], (points, 128))
        plane = bell(row, turned[:, 0:1]) * bell(level, turned[:, 2:3])
        high, low = split(plane)
        plane_ref[band, :cells] = high
        plane_ref[band, cells : 2 * cells] = low
        plane_ref[band, 2 * cells :] = high
    for at in range(blocks):
        for k in range(per_turbine):
            mask_ref[at, k : k + 1, :] = masks[at][k].astype(F32)
    acc_ref[...] = jnp.zeros(acc_ref.shape, F32)
    weights(0, even_ref)

    def pair(step):
        column_copy(2 * step).wait()
        column_copy(2 * step + 1).wait()

        if step < chunks // 2 - 1:
            column_copy(2 * step + 2).start()
            column_copy(2 * step + 3).start()
        if step == 1:
            lev_copy.start()

        weights(2 * step + 1, odd_ref)
        multiply(2 * step, even_ref)
        if step < chunks // 2 - 1:
            weights(2 * step + 2, even_ref)
        multiply(2 * step + 1, odd_ref)
        weight_copy(2 * step).start()
        weight_copy(2 * step + 1).start()

    for step in range(chunks // 2):
        pair(step)
    for i in range(components):
        for k in range(per_turbine):
            band = slice(k * points, (k + 1) * points)
            total = jnp.sum(acc_ref[i, band, :].T, axis=0, keepdims=True)
            part_ref[i : i + 1, band] = smear_norm * total
    part_ref[components:, :] = jnp.zeros((8 - components, count), F32)
    lev_copy.wait()
    for at in range(chunks):
        weight_copy(at).wait()


def sample(mine, twin, velocity, per_turbine):
    components, depth, rows, cols = velocity.shape
    points = mine.shape[2]
    count = per_turbine * points
    chunks = cols // STEP
    vmem = pl.BlockSpec(memory_space=pltpu.VMEM)
    hbm = pl.BlockSpec(memory_space=pltpu.HBM)
    return pl.pallas_call(
        functools.partial(sample_kernel, per_turbine),
        in_specs=[vmem, vmem, hbm],
        out_specs=[vmem, vmem, vmem, hbm, vmem],
        out_shape=[
            jax.ShapeDtypeStruct((8, count), F32),
            jax.ShapeDtypeStruct((8, count), F32),
            jax.ShapeDtypeStruct((mine.shape[0], per_turbine, points), F32),
            jax.ShapeDtypeStruct((2 * count, cols), BF16),
            jax.ShapeDtypeStruct((components, 2, rows, cols), F32),
        ],
        scratch_shapes=[
            pltpu.VMEM((count, STEP), F32),
            pltpu.VMEM((count, STEP), F32),
            pltpu.VMEM((count, 128), F32),
            pltpu.VMEM((count, 3 * depth * rows), BF16),
            pltpu.VMEM((components, count, 128), F32),
            pltpu.VMEM(velocity.shape, F32),
            pltpu.VMEM((2 * count, cols), BF16),
            pltpu.SemaphoreType.DMA((chunks,)),
            pltpu.SemaphoreType.DMA((chunks,)),
            pltpu.SemaphoreType.DMA,
        ],
        compiler_params=pltpu.CompilerParams(vmem_limit_bytes=58 * MIB),
        cost_estimate=LIGHT,
        name="sample",
    )(mine, twin, velocity)


def force_kernel(
    per_turbine, owned, mask_ref, part_ref, other_ref, own_ref, force_ref, home_ref
):
    points = own_ref.shape[1] // per_turbine
    relative = part_ref[0:3, :] + other_ref[0:3, :] - own_ref[3:6, :]
    speed = jnp.sqrt(jnp.sum(relative * relative, axis=0, keepdims=True))
    force = -own_ref[6:7, :] * speed * relative
    force_ref[...] = jnp.zeros(force_ref.shape, F32)
    force_ref[0:3, :] = force
    for row in range(mask_ref.shape[0]):
        total = jnp.zeros((3, points), F32)
        for k in range(per_turbine):
            total = jnp.where(mask_ref[row, k : k + 1, :] > 0.5, force[:, k * points : (k + 1) * points], total)
        for i in range(3):
            home_ref[row // owned, i, row % owned : row % owned + 1, :] = total[i : i + 1]


def point_forces(mask, part, other, own, per_turbine, owned):
    count = own.shape[1]
    points = count // per_turbine
    shifts = mask.shape[0] // owned
    return pl.pallas_call(
        functools.partial(force_kernel, per_turbine, owned),
        in_specs=[pl.BlockSpec(memory_space=pltpu.VMEM)] * 4,
        out_specs=[pl.BlockSpec(memory_space=pltpu.VMEM)] * 2,
        out_shape=[
            jax.ShapeDtypeStruct((8, count), F32),
            jax.ShapeDtypeStruct((shifts, 3, owned, points), F32),
        ],
        compiler_params=pltpu.CompilerParams(vmem_limit_bytes=58 * MIB),
        cost_estimate=LIGHT,
        name="force",
    )(mask, part, other, own)


def update_kernel(
    own_ref, force_ref, op_ref, left_ref, right_ref, near_in, far_in, relay_in, weight_in, vel_in, lev_in,
    new_out, zero_ref, pad_ref, new_ref, side_ref, weight_ref, high_ref, low_ref, even, odd,
    vel_sems, side_sems, weight_sems, new_sems, lev_sem,
):
    components, depth, rows, cols = new_ref.shape
    chunks = cols // STEP
    cells = LEVELS * rows
    inner = (LEVELS + 4) * rows
    fill = op_ref.shape[1] // 2 - inner - 4 * LEVELS
    count = own_ref.shape[1]
    core = lax.axis_index("gz")
    turbine = lax.axis_index("gy")
    parity = lax.axis_index("gx") % 2
    lane = lax.broadcasted_iota(jnp.int32, (8, 128), 1)
    shifts = ((1, lane < 1), (2, lane < 2), (127, lane >= 127), (126, lane >= 126))

    def column(at, first=0):
        return pl.ds(pl.multiple_of(at * STEP + first, 128), STEP)

    def arrivals(at):
        return [
            pltpu.make_async_copy(
                vel_in.at[:, :, :, column(at)],
                pad_ref.at[:, pl.ds(2, depth), :, column(at, 128)],
                vel_sems.at[at],
            ),
            pltpu.make_async_copy(
                weight_in.at[:, column(at)], weight_ref.at[:, column(at)], weight_sems.at[at]
            ),
            pltpu.make_async_copy(
                near_in.at[:, :, column(at)], side_ref.at[1 - parity, :, :, column(at)], side_sems.at[0, at]
            ),
            pltpu.make_async_copy(
                far_in.at[:, :, column(at)],
                side_ref.at[parity, :, pl.ds(0, depth), column(at)],
                side_sems.at[1, at],
            ),
            pltpu.make_async_copy(
                relay_in.at[:, :, column(at)],
                side_ref.at[parity, :, pl.ds(depth, depth), column(at)],
                side_sems.at[2, at],
            ),
        ]

    def departure(at):
        return pltpu.make_async_copy(
            new_ref.at[:, :, :, column(at)], new_out.at[:, :, :, column(at)], new_sems.at[at]
        )

    def level_copy(at):
        return pltpu.make_async_copy(
            lev_in, pad_ref.at[:, pl.ds(at, 2), :, pl.ds(128, cols)], lev_sem
        )

    def side_columns(ref, present, lane):
        per_part = 128 // rows
        parts = ref.shape[0] // components
        for tile in range(ref.shape[0]):
            turned = jnp.where(present, ref[tile], 0.0).T
            for k in range(per_part):
                level = (tile % parts) * per_part + k
                pad_ref[tile // parts, level + 2, :, lane : lane + 8] = turned[k * rows : (k + 1) * rows, :]

    def matrix_part(at, bufs):
        grad_ref, lap_ref, body_ref = bufs
        pad = pad_ref.at[:, :, :, column(at, 128)]
        sides = side_ref.at[:, :, :, column(at)]
        weight = weight_ref.at[:, column(at)]
        for i in range(components):
            for half in range(depth // LEVELS):
                levels = slice(half * LEVELS, (half + 1) * LEVELS)
                field = pad[i, half * LEVELS : (half + 1) * LEVELS + 4]
                inner_high, inner_low = split(field.reshape(inner, STEP))
                side = slice(half * 2 * LEVELS, (half + 1) * 2 * LEVELS)
                prev_high, prev_low = split(sides[0, i, side])
                next_high, next_low = split(sides[1, i, side])
                empty = [jnp.zeros((fill, STEP), BF16)] if fill else []
                high = [inner_high, prev_high, next_high] + empty
                low = [inner_low, prev_low, next_low] + empty
                result = dot(op_ref[...], jnp.concatenate(high + low, axis=0))
                grad_ref[i, levels] = result[:cells].reshape(LEVELS, rows, STEP)
                lap_ref[i, levels] = result[cells:].reshape(LEVELS, rows, STEP)
        upper = weight[:count]
        lower = weight[count:]
        wide = jnp.concatenate([high_ref[...], low_ref[...], high_ref[...]], axis=1)
        result = dot(wide, jnp.concatenate([upper, upper, lower], axis=0))
        body_ref[...] = result.reshape(components, depth, rows, STEP)

    def vector_part(at, bufs):
        grad_ref, lap_ref, body_ref = bufs
        pad = pad_ref.at[:, :, :, pl.ds(pl.multiple_of(at * STEP, 128), STEP + 256)]
        new = new_ref.at[:, :, :, column(at)]

        def cell(i, level, band, block):
            return pad[i, level, band, block * 128 : block * 128 + 128]

        def work(level, band):
            here = level + 2
            turned = {}

            def turn(i, block, shift):
                if (i, block, shift) not in turned:
                    turned[i, block, shift] = pltpu.roll(cell(i, here, band, block), shift, 1)
                return turned[i, block, shift]

            for block in range(1, STEP // 128 + 1):
                lanes = slice(block * 128 - 128, block * 128)
                along_y, lap, along_z = [], [], []
                for i in range(components):
                    behind, behind2, ahead, ahead2 = [
                        jnp.where(
                            wrapped,
                            turn(i, block - 1 if shift < 64 else block + 1, shift),
                            turn(i, block, shift),
                        )
                        for shift, wrapped in shifts
                    ]
                    along_y.append(8.0 * (ahead - behind) - (ahead2 - behind2))
                    lap.append(
                        lap_ref[i, level, band, lanes]
                        + (16.0 * (ahead + behind) - (ahead2 + behind2))
                    )
                    near = cell(i, here + 1, band, block) - cell(i, here - 1, band, block)
                    far = cell(i, here + 2, band, block) - cell(i, here - 2, band, block)
                    along_z.append(8.0 * near - far)
                along_x = [grad_ref[i, level, band, lanes] for i in range(components)]
                same = along_x[0] * along_x[0] + along_y[1] * along_y[1] + along_z[2] * along_z[2]
                xy = along_x[1] + along_y[0]
                xz = along_x[2] + along_z[0]
                yz = along_y[2] + along_z[1]
                strain = 2.0 * same + (xy * xy + xz * xz + yz * yz)
                mixing = (time_step / 12.0) * viscosity + (
                    time_step * smag_coeff * smag_coeff / 144.0
                ) * jnp.sqrt(strain)
                for i in range(components):
                    change = mixing * lap[i] - (time_step * mean_wind / 12.0) * along_x[i]
                    new[i, level, band, lanes] = (
                        cell(i, here, band, block) + body_ref[i, level, band, lanes] + change
                    )

        for level in range(depth):
            for row in range(0, rows, 8):
                work(level, slice(row, row + 8))
        departure(at).start()

    for copy in arrivals(0):
        copy.start()
    zero_ref[...] = jnp.zeros(zero_ref.shape, F32)

    @pl.when(core == 1)
    def _():
        level_copy(0).start()
        pad_ref[:, depth + 2 :, :, 128 : cols + 128] = jnp.zeros((components, 2, rows, cols), F32)

    @pl.when(core == 0)
    def _():
        level_copy(depth + 2).start()
        pad_ref[:, 0:2, :, 128 : cols + 128] = jnp.zeros((components, 2, rows, cols), F32)

    side_columns(left_ref, turbine > 0, 120)
    side_columns(right_ref, turbine < lax.axis_size("gy") - 1, cols + 128)
    along_x = gaussian(lax.axis_index("gx") * rows, rows, own_ref[0:1, :])
    along_z = gaussian(core * depth, depth, own_ref[2:3, :])
    for i in range(components):
        scaled = (time_step * smear_norm) * force_ref[i : i + 1, :] * along_x
        for level in range(depth):
            band = slice((i * depth + level) * rows, (i * depth + level + 1) * rows)
            high, low = split(scaled * along_z[level : level + 1, :])
            high_ref[band, :] = high
            low_ref[band, :] = low
    level_copy(0).wait()
    for copy in arrivals(0):
        copy.wait()
    for copy in arrivals(1) + arrivals(2):
        copy.start()
    matrix_part(0, even)

    def pair(step):
        for copy in arrivals(2 * step + 1) + arrivals(2 * step + 2):
            copy.wait()
        for copy in arrivals(2 * step + 3):
            copy.start()

        if step < chunks // 2 - 2:
            for copy in arrivals(2 * step + 4):
                copy.start()
        matrix_part(2 * step + 1, odd)
        vector_part(2 * step, even)
        matrix_part(2 * step + 2, even)
        vector_part(2 * step + 1, odd)

    for step in range(chunks // 2 - 1):
        pair(step)
    for copy in arrivals(chunks - 1):
        copy.wait()
    matrix_part(chunks - 1, odd)
    vector_part(chunks - 2, even)
    vector_part(chunks - 1, odd)
    for at in range(chunks):
        departure(at).wait()


def update(own, force, operator, near, far, relay, weight, velocity, lev, left, right, home_shape):
    components, depth, rows, cols = velocity.shape
    count = own.shape[1]
    chunks = cols // STEP
    vmem = pl.BlockSpec(memory_space=pltpu.VMEM)
    hbm = pl.BlockSpec(memory_space=pltpu.HBM)
    fields = [pltpu.VMEM((components, depth, rows, STEP), F32)] * 3
    macs = components * depth * rows * cols * (3 * count + 4 * 256)
    return pl.pallas_call(
        update_kernel,
        in_specs=[vmem] * 5 + [hbm] * 6,
        out_specs=[hbm, vmem],
        out_shape=[
            jax.ShapeDtypeStruct(velocity.shape, F32),
            jax.ShapeDtypeStruct(home_shape, F32),
        ],
        scratch_shapes=[
            pltpu.VMEM((components, depth + 4, rows, cols + 256), F32),
            pltpu.VMEM(velocity.shape, F32),
            pltpu.VMEM((2, *near.shape), F32),
            pltpu.VMEM((2 * count, cols), BF16),
            pltpu.VMEM((components * depth * rows, count), BF16),
            pltpu.VMEM((components * depth * rows, count), BF16),
            fields,
            fields,
            pltpu.SemaphoreType.DMA((chunks,)),
            pltpu.SemaphoreType.DMA((3, chunks)),
            pltpu.SemaphoreType.DMA((chunks,)),
            pltpu.SemaphoreType.DMA((chunks,)),
            pltpu.SemaphoreType.DMA,
        ],
        compiler_params=pltpu.CompilerParams(vmem_limit_bytes=44 * MIB),
        cost_estimate=pl.CostEstimate(
            flops=2 * macs, bytes_accessed=8 * velocity.size, transcendentals=velocity.size // 3
        ),
        name="update",
    )(own, force, operator, left, right, near, far, relay, weight, velocity, lev)


def local(velocity, blade_pos, block_turbine, blade_vel, lift_coeff):
    components, depth, rows, cols = velocity.shape
    owned, _, points = blade_pos.shape
    gx, gy, gz = (lax.axis_size(axis) for axis in ("gx", "gy", "gz"))
    assert gz == 2 and depth == 2 * LEVELS
    per_turbine = owned * gz
    swap = [(0, 1), (1, 0)]

    def around(shift):
        return [(i, (i + shift) % gy) for i in range(gy)]

    blocks, up, down, near, far, relay = prep(
        velocity, blade_pos, block_turbine, blade_vel, lift_coeff
    )
    near = lax.ppermute(near, "gx", [(i, i ^ 1) for i in range(gx)])
    across = [(i, i + 1) for i in range(1, gx - 1, 2)] + [(i + 1, i) for i in range(1, gx - 1, 2)]
    if gx == 4:
        relay = lax.ppermute(relay, "gx", [(1, 3), (2, 0)])

    def gather(blocks, up, down):
        left = lax.ppermute(up, "gy", around(1))
        right = lax.ppermute(down, "gy", around(gy - 1))
        parts = [blocks, left[:owned]]
        parts += [lax.ppermute(blocks, "gy", around(shift)) for shift in range(2, gy - 1)]
        parts.append(right[:owned])
        mine = jnp.concatenate(parts, axis=0)
        return mine, lax.ppermute(mine, "gz", swap), left[owned:], right[owned:]

    def blade(mine, twin, velocity):
        part, own, mask, weight, facing = sample(mine, twin, velocity, per_turbine)
        other = lax.ppermute(part, "gz", swap)
        lev = lax.ppermute(facing, "gz", swap)
        force, home = point_forces(mask, part, other, own, per_turbine, owned)
        return own, force, home, weight, lev

    def stage(run, *operands):
        empty = [jnp.zeros(out.shape, out.dtype) for out in jax.eval_shape(run, *operands)]
        return lax.cond(block_turbine[0] >= 0, run, lambda *_: tuple(empty), *operands)

    mine, twin, left, right = stage(gather, blocks, up, down)
    if gx == 4:
        relay = lax.ppermute(relay, "gx", [(3, 2), (0, 1)])
    else:
        relay = lax.ppermute(relay, "gx", across)
    far = lax.ppermute(far, "gx", across)
    own, force, home, weight, lev = stage(blade, mine, twin, velocity)
    result = home[0]
    for shift in range(1, gy):
        result += lax.ppermute(home[shift], "gy", around(gy - shift))

    operator = jnp.asarray(stencil_operator(rows))
    new_velocity, zero = update(
        own, force, operator, near, far, relay, weight, velocity, lev, left, right, result.shape
    )
    return (new_velocity, (result + zero).transpose(1, 0, 2))


def solution(mesh):
    in_specs = (
        P(None, "gz", "gx", "gy"),
        P(("gx", "gy", "gz"), None, None),
        P(("gx", "gy", "gz")),
        P(("gx", "gy", "gz"), None, None),
        P(("gx", "gy", "gz"), None),
    )
    out_specs = (P(None, "gz", "gx", "gy"), P(("gx", "gy", "gz"), None, None))
    return jax.shard_map(local, mesh=mesh, in_specs=in_specs, out_specs=out_specs, check_vma=False)
```

```python
import functools
import math

import jax
import jax.numpy as jnp
from jax import lax
from jax.experimental import pallas as pl
from jax.experimental.pallas import tpu as pltpu
from jax.sharding import PartitionSpec as P

mean_wind = 1.0
viscosity = 0.2
smag_coeff = 0.17
time_step = 0.2
smear = 2.0
smear_norm = 1.0 / (smear**3 * math.pi**1.5)

F32 = jnp.float32
BF16 = jnp.bfloat16
MIB = 1024 * 1024
STEP = 256
WIDE = 512
LIGHT = pl.CostEstimate(flops=0, bytes_accessed=0, transcendentals=0)


def split(value):
    high = value.astype(BF16)
    return high, (value - high.astype(F32)).astype(BF16)


def dot(left, right, contract=0):
    return lax.dot_general(
        left, right, (((1,), (contract,)), ((), ())), preferred_element_type=F32
    )


def gaussian(first, count, centers):
    shape = (count, centers.shape[1])
    cells = (first + lax.broadcasted_iota(jnp.int32, shape, 0)).astype(F32)
    gap = cells - centers
    return jnp.exp(-gap * gap / (smear * smear))


def prep_kernel(
    turb_in, pos_in, speed_in, lift_in, vel_in, blocks_ref, up_ref, down_ref, near_ref, far_ref, relay_ref,
    turb_ref, pos_ref, speed_ref, lift_ref, vel_ref, sems,
):
    components, levels, rows, cols = vel_ref.shape
    coords, owned, points = pos_ref.shape
    small = [
        pltpu.make_async_copy(source, target, sems.at[components + k])
        for k, (source, target) in enumerate(
            ((turb_in, turb_ref), (pos_in, pos_ref), (speed_in, speed_ref), (lift_in, lift_ref))
        )
    ]
    large = [
        pltpu.make_async_copy(vel_in.at[i], vel_ref.at[i], sems.at[i]) for i in range(components)
    ]
    for copy in small + large:
        copy.start()
    for copy in small:
        copy.wait()
    for ref in (blocks_ref, up_ref, down_ref):
        for k in range(owned):
            for i in range(coords):
                ref[k, i : i + 1, :] = pos_ref[i, k : k + 1, :]
                ref[k, coords + i : coords + i + 1, :] = speed_ref[i, k : k + 1, :]
            ref[k, 2 * coords : 2 * coords + 1, :] = lift_ref[k : k + 1, :]
            ref[k, 7:8, :] = jnp.full((1, points), turb_ref[k].astype(F32))
    parts = levels * rows // 128
    odd = lax.axis_index("gx") % 2 == 1
    row = lax.broadcasted_iota(jnp.int32, (8, cols), 0) // 2
    for component in range(components):
        large[component].wait()
        last = vel_ref[component, :, :, cols - 128 :].reshape(levels * rows, 128)
        first = vel_ref[component, :, :, :128].reshape(levels * rows, 128)
        for part in range(parts):
            cells = slice(part * 128, part * 128 + 128)
            up_ref[owned + component * parts + part] = last[cells].T[120:]
            down_ref[owned + component * parts + part] = first[cells].T[:8]
        for group in range(levels // 4):
            head = tail = None
            for k in range(4):
                top = vel_ref[component, group * 4 + k, 0:8, :]
                end = vel_ref[component, group * 4 + k, rows - 8 : rows, :]
                if k:
                    top = pltpu.roll(top, 2 * k, 0)
                if k < 3:
                    end = pltpu.roll(end, 2 * k + 2, 0)
                head = top if head is None else jnp.where(row == k, top, head)
                tail = end if tail is None else jnp.where(row == k, end, tail)
            near_ref[component, group * 8 : group * 8 + 8, :] = jnp.where(odd, head, tail)
            ref, to = (far_ref, group * 8) if group * 8 < levels else (relay_ref, group * 8 - levels)
            ref[component, to : to + 8, :] = jnp.where(odd, tail, head)


def prep(velocity, blade_pos, block_turbine, blade_vel, lift_coeff):
    components, levels, rows, cols = velocity.shape
    owned, coords, points = blade_pos.shape
    tiles = owned + components * levels * rows // 128
    return pl.pallas_call(
        prep_kernel,
        in_specs=[pl.BlockSpec(memory_space=pltpu.HBM)] * 5,
        out_specs=[pl.BlockSpec(memory_space=pltpu.VMEM)] * 6,
        out_shape=[
            jax.ShapeDtypeStruct((owned, 8, points), F32),
            jax.ShapeDtypeStruct((tiles, 8, 128), F32),
            jax.ShapeDtypeStruct((tiles, 8, 128), F32),
            jax.ShapeDtypeStruct((components, 2 * levels, cols), F32),
            jax.ShapeDtypeStruct((components, levels, cols), F32),
            jax.ShapeDtypeStruct((components, levels, cols), F32),
        ],
        scratch_shapes=[
            pltpu.SMEM((owned,), jnp.int32),
            pltpu.VMEM((coords, owned, points), F32),
            pltpu.VMEM((coords, owned, points), F32),
            pltpu.VMEM((owned, points), F32),
            pltpu.VMEM(velocity.shape, F32),
            pltpu.SemaphoreType.DMA((components + 4,)),
        ],
        compiler_params=pltpu.CompilerParams(vmem_limit_bytes=60 * MIB),
        cost_estimate=LIGHT,
        name="prep",
    )(
        block_turbine,
        blade_pos.transpose(1, 0, 2),
        blade_vel.transpose(1, 0, 2),
        lift_coeff,
        velocity,
    )


def match(mine_ref, twin_ref, per_turbine):
    core = lax.axis_index("gz")
    turbine = lax.axis_index("gy").astype(F32)
    half = mine_ref.shape[0]
    first = [(mine_ref[k, 7:8, :] == turbine).astype(F32) for k in range(half)]
    second = [(twin_ref[k, 7:8, :] == turbine).astype(F32) for k in range(half)]
    masks = []
    for hits, others, leads in ((first, second, core == 0), (second, first, core == 1)):
        rank = jnp.where(leads, jnp.zeros_like(hits[0]), sum(others))
        for hit in hits:
            masks.append([(hit > 0.5) & (rank == k) for k in range(per_turbine)])
            rank = rank + hit
    return masks


def sample_kernel(
    per_turbine, mine_ref, twin_ref, vel_in, part_ref, own_ref, mask_ref, weight_out, lev_ref,
    even_ref, odd_ref, center_ref, plane_ref, acc_ref, vel_ref, weight_ref, sems, out_sems, lev_sem,
):
    components, depth, rows, cols = vel_ref.shape
    points = mine_ref.shape[2]
    count = per_turbine * points
    cells = depth * rows
    chunks = cols // STEP
    core = lax.axis_index("gz")
    start = lax.axis_index("gy") * cols

    def column(at):
        return pl.ds(pl.multiple_of(at * STEP, STEP), STEP)

    def column_copy(at):
        return pltpu.make_async_copy(
            vel_in.at[:, :, :, column(at)], vel_ref.at[:, :, :, column(at)], sems.at[at]
        )

    def weight_copy(at):
        return pltpu.make_async_copy(
            weight_ref.at[:, column(at)], weight_out.at[:, column(at)], out_sems.at[at]
        )

    lev_copy = pltpu.make_async_copy(
        vel_in.at[:, pl.ds(jnp.where(core == 0, depth - 2, 0), 2)], lev_ref, lev_sem
    )

    def bell(cell, center):
        gap = cell.astype(F32) - center
        return jnp.exp(gap * gap * (-1.0 / (smear * smear)))

    def weights(at, ref):
        lane = lax.broadcasted_iota(jnp.int32, (1, 128), 1)
        for part in range(STEP // 128):
            cell = start + at * STEP + part * 128 + lane
            ref[:, part * 128 : part * 128 + 128] = bell(cell, center_ref[...])

    def multiply(at, ref):
        vel = vel_ref.at[:, :, :, column(at)]
        out = weight_ref.at[:, column(at)]
        for i in range(components):
            high, low = split(vel[i].reshape(cells, STEP))
            field = dot(plane_ref[...], jnp.concatenate([high, high, low], axis=0))
            product = field * ref[...]
            total = acc_ref[i]
            for part in range(STEP // 128):
                total += product[:, part * 128 : part * 128 + 128]
            acc_ref[i] = total
        high, low = split(ref[...])
        out[:count, :] = high
        out[count:, :] = low

    column_copy(0).start()
    column_copy(1).start()
    masks = match(mine_ref, twin_ref, per_turbine)
    blocks = mine_ref.shape[0]
    lane = lax.broadcasted_iota(jnp.int32, (1, cells), 1)
    level = core * depth + lane // rows
    row = lax.axis_index("gx") * rows + lane % rows
    for k in range(per_turbine):
        total = jnp.zeros((8, points), F32)
        for at, mask in enumerate(masks):
            tile = mine_ref[at] if at < blocks else twin_ref[at - blocks]
            total = jnp.where(mask[k], tile, total)
        band = slice(k * points, (k + 1) * points)
        own_ref[:, band] = total
        turned = total.T
        center_ref[band, :] = jnp.broadcast_to(turned[:, 1:2], (points, 128))
        plane = bell(row, turned[:, 0:1]) * bell(level, turned[:, 2:3])
        high, low = split(plane)
        plane_ref[band, :cells] = high
        plane_ref[band, cells : 2 * cells] = low
        plane_ref[band, 2 * cells :] = high
    for at in range(blocks):
        for k in range(per_turbine):
            mask_ref[at, k : k + 1, :] = masks[at][k].astype(F32)
    acc_ref[...] = jnp.zeros(acc_ref.shape, F32)
    weights(0, even_ref)

    def pair(step, carry):
        column_copy(2 * step).wait()
        column_copy(2 * step + 1).wait()

        @pl.when(step < chunks // 2 - 1)
        def _():
            column_copy(2 * step + 2).start()
            column_copy(2 * step + 3).start()

        @pl.when(step == chunks // 2 - 1)
        def _():
            lev_copy.start()

        weights(2 * step + 1, odd_ref)
        multiply(2 * step, even_ref)
        weights(2 * step + 2, even_ref)
        multiply(2 * step + 1, odd_ref)
        weight_copy(2 * step).start()
        weight_copy(2 * step + 1).start()
        return carry

    lax.fori_loop(0, chunks // 2, pair, 0)
    for i in range(components):
        for k in range(per_turbine):
            band = slice(k * points, (k + 1) * points)
            total = jnp.sum(acc_ref[i, band, :].T, axis=0, keepdims=True)
            part_ref[i : i + 1, band] = smear_norm * total
    part_ref[components:, :] = jnp.zeros((8 - components, count), F32)
    lev_copy.wait()
    for at in range(chunks):
        weight_copy(at).wait()


def sample(mine, twin, velocity, per_turbine):
    components, depth, rows, cols = velocity.shape
    points = mine.shape[2]
    count = per_turbine * points
    chunks = cols // STEP
    vmem = pl.BlockSpec(memory_space=pltpu.VMEM)
    hbm = pl.BlockSpec(memory_space=pltpu.HBM)
    return pl.pallas_call(
        functools.partial(sample_kernel, per_turbine),
        in_specs=[vmem, vmem, hbm],
        out_specs=[vmem, vmem, vmem, hbm, vmem],
        out_shape=[
            jax.ShapeDtypeStruct((8, count), F32),
            jax.ShapeDtypeStruct((8, count), F32),
            jax.ShapeDtypeStruct((mine.shape[0], per_turbine, points), F32),
            jax.ShapeDtypeStruct((2 * count, cols), BF16),
            jax.ShapeDtypeStruct((components, 2, rows, cols), F32),
        ],
        scratch_shapes=[
            pltpu.VMEM((count, STEP), F32),
            pltpu.VMEM((count, STEP), F32),
            pltpu.VMEM((count, 128), F32),
            pltpu.VMEM((count, 3 * depth * rows), BF16),
            pltpu.VMEM((components, count, 128), F32),
            pltpu.VMEM(velocity.shape, F32),
            pltpu.VMEM((2 * count, cols), BF16),
            pltpu.SemaphoreType.DMA((chunks,)),
            pltpu.SemaphoreType.DMA((chunks,)),
            pltpu.SemaphoreType.DMA,
        ],
        compiler_params=pltpu.CompilerParams(vmem_limit_bytes=58 * MIB),
        cost_estimate=LIGHT,
        name="sample",
    )(mine, twin, velocity)


def force_kernel(
    per_turbine, owned, mask_ref, part_ref, other_ref, own_ref, force_ref, home_ref
):
    points = own_ref.shape[1] // per_turbine
    relative = part_ref[0:3, :] + other_ref[0:3, :] - own_ref[3:6, :]
    speed = jnp.sqrt(jnp.sum(relative * relative, axis=0, keepdims=True))
    force = -own_ref[6:7, :] * speed * relative
    force_ref[...] = jnp.zeros(force_ref.shape, F32)
    force_ref[0:3, :] = force
    for row in range(mask_ref.shape[0]):
        total = jnp.zeros((3, points), F32)
        for k in range(per_turbine):
            total = jnp.where(mask_ref[row, k : k + 1, :] > 0.5, force[:, k * points : (k + 1) * points], total)
        for i in range(3):
            home_ref[row // owned, i, row % owned : row % owned + 1, :] = total[i : i + 1]


def point_forces(mask, part, other, own, per_turbine, owned):
    count = own.shape[1]
    points = count // per_turbine
    shifts = mask.shape[0] // owned
    return pl.pallas_call(
        functools.partial(force_kernel, per_turbine, owned),
        in_specs=[pl.BlockSpec(memory_space=pltpu.VMEM)] * 4,
        out_specs=[pl.BlockSpec(memory_space=pltpu.VMEM)] * 2,
        out_shape=[
            jax.ShapeDtypeStruct((8, count), F32),
            jax.ShapeDtypeStruct((shifts, 3, owned, points), F32),
        ],
        compiler_params=pltpu.CompilerParams(vmem_limit_bytes=58 * MIB),
        cost_estimate=LIGHT,
        name="force",
    )(mask, part, other, own)


def update_kernel(
    own_ref, force_ref, left_ref, right_ref, near_in, far_in, relay_in, weight_in, vel_in, lev_in,
    new_out, zero_ref, pad_ref, new_ref, side_ref, weight_ref, high_ref, low_ref, body_ref,
    vel_sems, side_sems, weight_sems, new_sems, lev_sem,
):
    components, depth, rows, cols = new_ref.shape
    chunks = cols // WIDE
    count = own_ref.shape[1]
    core = lax.axis_index("gz")
    turbine = lax.axis_index("gy")
    parity = lax.axis_index("gx") % 2
    lane = lax.broadcasted_iota(jnp.int32, (8, 128), 1)
    sublane = lax.broadcasted_iota(jnp.int32, (8, 128), 0)
    lower = {1: sublane < 1, 2: sublane < 2, 7: sublane >= 7, 6: sublane >= 6}
    shifts = ((1, lane < 1), (2, lane < 2), (127, lane >= 127), (126, lane >= 126))

    def column(at, first=0):
        return pl.ds(pl.multiple_of(at * WIDE + first, 128), WIDE)

    def arrivals(at):
        return [
            pltpu.make_async_copy(
                vel_in.at[:, :, :, column(at)],
                pad_ref.at[:, pl.ds(2, depth), :, column(at, 128)],
                vel_sems.at[at],
            ),
            pltpu.make_async_copy(
                weight_in.at[:, column(at)], weight_ref.at[:, column(at)], weight_sems.at[at]
            ),
            pltpu.make_async_copy(
                near_in.at[:, :, column(at)], side_ref.at[1 - parity, :, :, column(at)], side_sems.at[0, at]
            ),
            pltpu.make_async_copy(
                far_in.at[:, :, column(at)],
                side_ref.at[parity, :, pl.ds(0, depth), column(at)],
                side_sems.at[1, at],
            ),
            pltpu.make_async_copy(
                relay_in.at[:, :, column(at)],
                side_ref.at[parity, :, pl.ds(depth, depth), column(at)],
                side_sems.at[2, at],
            ),
        ]

    def departure(at):
        return pltpu.make_async_copy(
            new_ref.at[:, :, :, column(at)], new_out.at[:, :, :, column(at)], new_sems.at[at]
        )

    def level_copy(at):
        return pltpu.make_async_copy(
            lev_in, pad_ref.at[:, pl.ds(at, 2), :, pl.ds(128, cols)], lev_sem
        )

    def side_columns(ref, present, lane):
        per_part = 128 // rows
        parts = ref.shape[0] // components
        for tile in range(ref.shape[0]):
            turned = jnp.where(present, ref[tile], 0.0).T
            for k in range(per_part):
                level = (tile % parts) * per_part + k
                pad_ref[tile // parts, level + 2, :, lane : lane + 8] = turned[k * rows : (k + 1) * rows, :]

    def matrix_part(at):
        weight = weight_ref.at[:, column(at)]
        upper = weight[:count]
        wide = jnp.concatenate([high_ref[...], low_ref[...], high_ref[...]], axis=1)
        result = dot(wide, jnp.concatenate([upper, upper, weight[count:]], axis=0))
        body_ref[...] = result.reshape(components, depth, rows, WIDE)

    def vector_part(at):
        pad = pad_ref.at[:, :, :, pl.ds(pl.multiple_of(at * WIDE, 128), WIDE + 256)]
        sides = side_ref.at[:, :, :, column(at)]
        new = new_ref.at[:, :, :, column(at)]
        bands = [slice(row, row + 8) for row in range(0, rows, 8)]

        def cell(i, level, band, block):
            return pad[i, level, band, block * 128 : block * 128 + 128]

        def work(level):
            here = level + 2
            group = slice(level // 4 * 8, level // 4 * 8 + 8)
            row = level % 4 * 2
            turned = {}

            def turn(i, band, block, shift):
                key = (i, band.start, block, shift)
                if key not in turned:
                    turned[key] = pltpu.roll(cell(i, here, band, block), shift, 1)
                return turned[key]

            def rows_moved(own, before, after, lanes, i):
                moved = []
                for shift, to, edge in ((1, -row - 1, 0), (2, -row, 0), (7, 7 - row, 1), (6, 6 - row, 1)):
                    side = (before, after)[edge]
                    side = pltpu.roll(side, to % 8, 0) if to % 8 else side
                    rolled = [pltpu.roll(tile, shift, 0) for tile in own]
                    if edge:
                        ring = rolled + [side]
                        moved.append([jnp.where(lower[shift], ring[k + 1], ring[k]) for k in range(len(own))])
                    else:
                        ring = [side] + rolled
                        moved.append([jnp.where(lower[shift], ring[k], ring[k + 1]) for k in range(len(own))])
                return moved

            for block in range(1, WIDE // 128 + 1):
                lanes = slice(block * 128 - 128, block * 128)
                along = [[], [], []]
                lap = []
                middle = []
                for i in range(components):
                    own = [cell(i, here, band, block) for band in bands]
                    middle.append(own)
                    b1, b2, a1, a2 = rows_moved(
                        own, sides[0, i, group, lanes], sides[1, i, group, lanes], lanes, i
                    )
                    along_x, along_y, along_z, total = [], [], [], []
                    for k, band in enumerate(bands):
                        yb1, yb2, ya1, ya2 = [
                            jnp.where(
                                wrapped,
                                turn(i, band, block - 1 if shift < 64 else block + 1, shift),
                                turn(i, band, block, shift),
                            )
                            for shift, wrapped in shifts
                        ]
                        zb1, zb2 = cell(i, here - 1, band, block), cell(i, here - 2, band, block)
                        za1, za2 = cell(i, here + 1, band, block), cell(i, here + 2, band, block)
                        along_x.append(8.0 * (a1[k] - b1[k]) - (a2[k] - b2[k]))
                        along_y.append(8.0 * (ya1 - yb1) - (ya2 - yb2))
                        along_z.append(8.0 * (za1 - zb1) - (za2 - zb2))
                        near = ((a1[k] + b1[k]) + (ya1 + yb1)) + (za1 + zb1)
                        far = ((a2[k] + b2[k]) + (ya2 + yb2)) + (za2 + zb2)
                        total.append((16.0 * near - far) - 90.0 * own[k])
                    along[0].append(along_x)
                    along[1].append(along_y)
                    along[2].append(along_z)
                    lap.append(total)
                for k, band in enumerate(bands):
                    gx, gy, gz = [[part[k] for part in parts] for parts in along]
                    same = gx[0] * gx[0] + gy[1] * gy[1] + gz[2] * gz[2]
                    xy, xz, yz = gx[1] + gy[0], gx[2] + gz[0], gy[2] + gz[1]
                    strain = 2.0 * same + (xy * xy + xz * xz + yz * yz)
                    mixing = (time_step / 12.0) * viscosity + (
                        time_step * smag_coeff * smag_coeff / 144.0
                    ) * jnp.sqrt(strain)
                    for i in range(components):
                        change = mixing * lap[i][k] - (time_step * mean_wind / 12.0) * gx[i]
                        new[i, level, band, lanes] = (
                            middle[i][k] + body_ref[i, level, band, lanes] + change
                        )

        for level in range(depth):
            work(level)
        departure(at).start()

    for copy in arrivals(0):
        copy.start()
    zero_ref[...] = jnp.zeros(zero_ref.shape, F32)

    @pl.when(core == 1)
    def _():
        level_copy(0).start()
        pad_ref[:, depth + 2 :, :, 128 : cols + 128] = jnp.zeros((components, 2, rows, cols), F32)

    @pl.when(core == 0)
    def _():
        level_copy(depth + 2).start()
        pad_ref[:, 0:2, :, 128 : cols + 128] = jnp.zeros((components, 2, rows, cols), F32)

    side_columns(left_ref, turbine > 0, 120)
    side_columns(right_ref, turbine < lax.axis_size("gy") - 1, cols + 128)
    along_x = gaussian(lax.axis_index("gx") * rows, rows, own_ref[0:1, :])
    along_z = gaussian(core * depth, depth, own_ref[2:3, :])
    for i in range(components):
        scaled = (time_step * smear_norm) * force_ref[i : i + 1, :] * along_x
        for level in range(depth):
            band = slice((i * depth + level) * rows, (i * depth + level + 1) * rows)
            high, low = split(scaled * along_z[level : level + 1, :])
            high_ref[band, :] = high
            low_ref[band, :] = low
    level_copy(0).wait()

    def chunk(at, carry):
        @pl.when(at < chunks - 2)
        def _():
            for copy in arrivals(at + 2):
                copy.start()

        @pl.when(at < chunks - 1)
        def _():
            for copy in arrivals(at + 1):
                copy.wait()

        matrix_part(at)
        vector_part(at)
        return carry

    for copy in arrivals(1):
        copy.start()
    for copy in arrivals(0):
        copy.wait()
    lax.fori_loop(0, chunks, chunk, 0)
    for at in range(chunks):
        departure(at).wait()


def update(own, force, near, far, relay, weight, velocity, lev, left, right, home_shape):
    components, depth, rows, cols = velocity.shape
    count = own.shape[1]
    chunks = cols // WIDE
    vmem = pl.BlockSpec(memory_space=pltpu.VMEM)
    hbm = pl.BlockSpec(memory_space=pltpu.HBM)
    macs = components * depth * rows * cols * 3 * count
    return pl.pallas_call(
        update_kernel,
        in_specs=[vmem] * 4 + [hbm] * 6,
        out_specs=[hbm, vmem],
        out_shape=[
            jax.ShapeDtypeStruct(velocity.shape, F32),
            jax.ShapeDtypeStruct(home_shape, F32),
        ],
        scratch_shapes=[
            pltpu.VMEM((components, depth + 4, rows, cols + 256), F32),
            pltpu.VMEM(velocity.shape, F32),
            pltpu.VMEM((2, *near.shape), F32),
            pltpu.VMEM((2 * count, cols), BF16),
            pltpu.VMEM((components * depth * rows, count), BF16),
            pltpu.VMEM((components * depth * rows, count), BF16),
            pltpu.VMEM((components, depth, rows, WIDE), F32),
            pltpu.SemaphoreType.DMA((chunks,)),
            pltpu.SemaphoreType.DMA((3, chunks)),
            pltpu.SemaphoreType.DMA((chunks,)),
            pltpu.SemaphoreType.DMA((chunks,)),
            pltpu.SemaphoreType.DMA,
        ],
        compiler_params=pltpu.CompilerParams(vmem_limit_bytes=44 * MIB),
        cost_estimate=pl.CostEstimate(
            flops=2 * macs, bytes_accessed=8 * velocity.size, transcendentals=velocity.size // 3
        ),
        name="update",
    )(own, force, left, right, near, far, relay, weight, velocity, lev)


def local(velocity, blade_pos, block_turbine, blade_vel, lift_coeff):
    components, depth, rows, cols = velocity.shape
    owned, _, points = blade_pos.shape
    gx, gy, gz = (lax.axis_size(axis) for axis in ("gx", "gy", "gz"))
    assert gz == 2 and depth % 8 == 0 and rows == 16
    per_turbine = owned * gz
    swap = [(0, 1), (1, 0)]

    def around(shift):
        return [(i, (i + shift) % gy) for i in range(gy)]

    blocks, up, down, near, far, relay = prep(
        velocity, blade_pos, block_turbine, blade_vel, lift_coeff
    )
    near = lax.ppermute(near, "gx", [(i, i ^ 1) for i in range(gx)])
    across = [(i, i + 1) for i in range(1, gx - 1, 2)] + [(i + 1, i) for i in range(1, gx - 1, 2)]
    if gx == 4:
        relay = lax.ppermute(relay, "gx", [(1, 3), (2, 0)])

    def gather(blocks, up, down):
        left = lax.ppermute(up, "gy", around(1))
        right = lax.ppermute(down, "gy", around(gy - 1))
        parts = [blocks, left[:owned]]
        parts += [lax.ppermute(blocks, "gy", around(shift)) for shift in range(2, gy - 1)]
        parts.append(right[:owned])
        mine = jnp.concatenate(parts, axis=0)
        return mine, lax.ppermute(mine, "gz", swap), left[owned:], right[owned:]

    def blade(mine, twin, velocity):
        part, own, mask, weight, facing = sample(mine, twin, velocity, per_turbine)
        other = lax.ppermute(part, "gz", swap)
        lev = lax.ppermute(facing, "gz", swap)
        force, home = point_forces(mask, part, other, own, per_turbine, owned)
        return own, force, home, weight, lev

    def stage(run, *operands):
        empty = [jnp.zeros(out.shape, out.dtype) for out in jax.eval_shape(run, *operands)]
        return lax.cond(block_turbine[0] >= 0, run, lambda *_: tuple(empty), *operands)

    mine, twin, left, right = stage(gather, blocks, up, down)
    if gx == 4:
        relay = lax.ppermute(relay, "gx", [(3, 2), (0, 1)])
    else:
        relay = lax.ppermute(relay, "gx", across)
    far = lax.ppermute(far, "gx", across)
    own, force, home, weight, lev = stage(blade, mine, twin, velocity)
    result = home[0]
    for shift in range(1, gy):
        result += lax.ppermute(home[shift], "gy", around(gy - shift))

    new_velocity, zero = update(
        own, force, near, far, relay, weight, velocity, lev, left, right, result.shape
    )
    return (new_velocity, (result + zero).transpose(1, 0, 2))


def solution(mesh):
    in_specs = (
        P(None, "gz", "gx", "gy"),
        P(("gx", "gy", "gz"), None, None),
        P(("gx", "gy", "gz")),
        P(("gx", "gy", "gz"), None, None),
        P(("gx", "gy", "gz"), None),
    )
    out_specs = (P(None, "gz", "gx", "gy"), P(("gx", "gy", "gz"), None, None))
    return jax.shard_map(local, mesh=mesh, in_specs=in_specs, out_specs=out_specs, check_vma=False)
```

```python
import functools
import math

import jax
import jax.numpy as jnp
import ml_dtypes
import numpy as np
from jax import lax
from jax.experimental import pallas as pl
from jax.experimental.pallas import tpu as pltpu
from jax.sharding import PartitionSpec as P

mean_wind = 1.0
viscosity = 0.2
smag_coeff = 0.17
time_step = 0.2
smear = 2.0
smear_norm = 1.0 / (smear**3 * math.pi**1.5)

F32 = jnp.float32
BF16 = jnp.bfloat16
SMALLEST = float(jnp.finfo(F32).tiny)
MIB = 1024 * 1024
LEVELS = 8
STEP = 256
LIGHT = pl.CostEstimate(flops=0, bytes_accessed=0, transcendentals=0)


def split(value):
    high = value.astype(BF16)
    return high, (value - high.astype(F32)).astype(BF16)


def dot(left, right, contract=0):
    return lax.dot_general(
        left, right, (((1,), (contract,)), ((), ())), preferred_element_type=F32
    )


def gaussian(first, count, centers):
    shape = (count, centers.shape[1])
    cells = (first + lax.broadcasted_iota(jnp.int32, shape, 0)).astype(F32)
    gap = cells - centers
    return jnp.exp(-gap * gap / (smear * smear))


def stencil_operator(row_cells):
    inner = (LEVELS + 4) * row_cells
    width = inner + 4 * LEVELS
    op = np.zeros((2, LEVELS, row_cells, width), np.float32)

    def column(level, row):
        if 0 <= row < row_cells:
            return (level + 2) * row_cells + row
        if row < 0:
            return inner + level * 2 + row + 2
        return inner + 2 * LEVELS + level * 2 + row - row_cells

    for level in range(LEVELS):
        for row in range(row_cells):
            for offset, first, second in ((-2, 1, -1), (-1, -8, 16), (1, 8, 16), (2, -1, -1)):
                op[0, level, row, column(level, row + offset)] += first
                op[1, level, row, column(level, row + offset)] += second
                op[1, level, row, column(level + offset, row)] += second
            op[1, level, row, column(level, row)] -= 90
    op = op.reshape(2 * LEVELS * row_cells, width)
    op = np.pad(op, ((0, 0), (0, -width % 128)))
    return np.concatenate([op, op], axis=1).astype(ml_dtypes.bfloat16)


def prep_kernel(
    turb_in, pos_in, speed_in, lift_in, vel_in, blocks_ref, up_ref, down_ref, near_ref, far_ref, relay_ref,
    turb_ref, pos_ref, speed_ref, lift_ref, vel_ref, sems,
):
    components, levels, rows, cols = vel_ref.shape
    coords, owned, points = pos_ref.shape
    small = [
        pltpu.make_async_copy(source, target, sems.at[components + k])
        for k, (source, target) in enumerate(
            ((turb_in, turb_ref), (pos_in, pos_ref), (speed_in, speed_ref), (lift_in, lift_ref))
        )
    ]
    large = [
        pltpu.make_async_copy(vel_in.at[i], vel_ref.at[i], sems.at[i]) for i in range(components)
    ]
    for copy in small + large:
        copy.start()
    for copy in small:
        copy.wait()
    for ref in (blocks_ref, up_ref, down_ref):
        for k in range(owned):
            for i in range(coords):
                ref[k, i : i + 1, :] = pos_ref[i, k : k + 1, :]
                ref[k, coords + i : coords + i + 1, :] = speed_ref[i, k : k + 1, :]
            ref[k, 2 * coords : 2 * coords + 1, :] = lift_ref[k : k + 1, :]
            ref[k, 7:8, :] = jnp.full((1, points), turb_ref[k].astype(F32))
    parts = levels * rows // 128
    odd = lax.axis_index("gx") % 2 == 1
    row = lax.broadcasted_iota(jnp.int32, (8, cols), 0) // 2
    for component in range(components):
        large[component].wait()
        last = vel_ref[component, :, :, cols - 128 :].reshape(levels * rows, 128)
        first = vel_ref[component, :, :, :128].reshape(levels * rows, 128)
        for part in range(parts):
            cells = slice(part * 128, part * 128 + 128)
            up_ref[owned + component * parts + part] = last[cells].T[120:]
            down_ref[owned + component * parts + part] = first[cells].T[:8]
        for group in range(levels // 4):
            head = tail = None
            for k in range(4):
                top = vel_ref[component, group * 4 + k, 0:8, :]
                end = vel_ref[component, group * 4 + k, rows - 8 : rows, :]
                if k:
                    top = pltpu.roll(top, 2 * k, 0)
                if k < 3:
                    end = pltpu.roll(end, 2 * k + 2, 0)
                head = top if head is None else jnp.where(row == k, top, head)
                tail = end if tail is None else jnp.where(row == k, end, tail)
            near_ref[component, group * 8 : group * 8 + 8, :] = jnp.where(odd, head, tail)
            ref, to = (far_ref, group * 8) if group * 8 < levels else (relay_ref, group * 8 - levels)
            ref[component, to : to + 8, :] = jnp.where(odd, tail, head)


def prep(velocity, blade_pos, block_turbine, blade_vel, lift_coeff):
    components, levels, rows, cols = velocity.shape
    owned, coords, points = blade_pos.shape
    tiles = owned + components * levels * rows // 128
    return pl.pallas_call(
        prep_kernel,
        in_specs=[pl.BlockSpec(memory_space=pltpu.HBM)] * 5,
        out_specs=[pl.BlockSpec(memory_space=pltpu.VMEM)] * 6,
        out_shape=[
            jax.ShapeDtypeStruct((owned, 8, points), F32),
            jax.ShapeDtypeStruct((tiles, 8, 128), F32),
            jax.ShapeDtypeStruct((tiles, 8, 128), F32),
            jax.ShapeDtypeStruct((components, 2 * levels, cols), F32),
            jax.ShapeDtypeStruct((components, levels, cols), F32),
            jax.ShapeDtypeStruct((components, levels, cols), F32),
        ],
        scratch_shapes=[
            pltpu.SMEM((owned,), jnp.int32),
            pltpu.VMEM((coords, owned, points), F32),
            pltpu.VMEM((coords, owned, points), F32),
            pltpu.VMEM((owned, points), F32),
            pltpu.VMEM(velocity.shape, F32),
            pltpu.SemaphoreType.DMA((components + 4,)),
        ],
        compiler_params=pltpu.CompilerParams(vmem_limit_bytes=60 * MIB),
        cost_estimate=LIGHT,
        name="prep",
    )(
        block_turbine,
        blade_pos.transpose(1, 0, 2),
        blade_vel.transpose(1, 0, 2),
        lift_coeff,
        velocity,
    )


def match(mine_ref, twin_ref, per_turbine):
    core = lax.axis_index("gz")
    turbine = lax.axis_index("gy").astype(F32)
    half = mine_ref.shape[0]
    first = [(mine_ref[k, 7:8, :] == turbine).astype(F32) for k in range(half)]
    second = [(twin_ref[k, 7:8, :] == turbine).astype(F32) for k in range(half)]
    masks = []
    for hits, others, leads in ((first, second, core == 0), (second, first, core == 1)):
        rank = jnp.where(leads, jnp.zeros_like(hits[0]), sum(others))
        for hit in hits:
            masks.append([(hit > 0.5) & (rank == k) for k in range(per_turbine)])
            rank = rank + hit
    return masks


def sample_kernel(
    per_turbine, mine_ref, twin_ref, vel_in, part_ref, own_ref, mask_ref, weight_out, lev_ref,
    even_ref, odd_ref, center_ref, plane_ref, acc_ref, vel_ref, weight_ref, sems, out_sems, lev_sem,
):
    components, depth, rows, cols = vel_ref.shape
    points = mine_ref.shape[2]
    count = per_turbine * points
    cells = depth * rows
    chunks = cols // STEP
    core = lax.axis_index("gz")
    start = lax.axis_index("gy") * cols

    def column(at):
        return pl.ds(pl.multiple_of(at * STEP, STEP), STEP)

    def column_copy(at):
        return pltpu.make_async_copy(
            vel_in.at[:, :, :, column(at)], vel_ref.at[:, :, :, column(at)], sems.at[at]
        )

    def weight_copy(at):
        return pltpu.make_async_copy(
            weight_ref.at[:, column(at)], weight_out.at[:, column(at)], out_sems.at[at]
        )

    lev_copy = pltpu.make_async_copy(
        vel_in.at[:, pl.ds(jnp.where(core == 0, depth - 2, 0), 2)], lev_ref, lev_sem
    )

    def bell(cell, center):
        gap = cell.astype(F32) - center
        return jnp.exp(gap * gap * (-1.0 / (smear * smear)))

    def weights(at, ref):
        lane = lax.broadcasted_iota(jnp.int32, (1, 128), 1)
        for part in range(STEP // 128):
            cell = start + at * STEP + part * 128 + lane
            ref[:, part * 128 : part * 128 + 128] = bell(cell, center_ref[...])

    def multiply(at, ref):
        vel = vel_ref.at[:, :, :, column(at)]
        out = weight_ref.at[:, column(at)]
        for i in range(components):
            high, low = split(vel[i].reshape(cells, STEP))
            field = dot(plane_ref[...], jnp.concatenate([high, high, low], axis=0))
            product = field * ref[...]
            total = acc_ref[i]
            for part in range(STEP // 128):
                total += product[:, part * 128 : part * 128 + 128]
            acc_ref[i] = total
        high, low = split(ref[...])
        out[:count, :] = high
        out[count:, :] = low

    column_copy(0).start()
    masks = match(mine_ref, twin_ref, per_turbine)
    blocks = mine_ref.shape[0]
    lane = lax.broadcasted_iota(jnp.int32, (1, cells), 1)
    level = core * depth + lane // rows
    row = lax.axis_index("gx") * rows + lane % rows
    for k in range(per_turbine):
        total = jnp.zeros((8, points), F32)
        for at, mask in enumerate(masks):
            tile = mine_ref[at] if at < blocks else twin_ref[at - blocks]
            total = jnp.where(mask[k], tile, total)
        band = slice(k * points, (k + 1) * points)
        own_ref[:, band] = total
        turned = total.T
        center_ref[band, :] = jnp.broadcast_to(turned[:, 1:2], (points, 128))
        plane = bell(row, turned[:, 0:1]) * bell(level, turned[:, 2:3])
        high, low = split(plane)
        plane_ref[band, :cells] = high
        plane_ref[band, cells : 2 * cells] = low
        plane_ref[band, 2 * cells :] = high
    for at in range(blocks):
        for k in range(per_turbine):
            mask_ref[at, k : k + 1, :] = masks[at][k].astype(F32)
    acc_ref[...] = jnp.zeros(acc_ref.shape, F32)
    weights(0, even_ref)

    def pair(step, carry):
        column_copy(2 * step + 1).start()
        column_copy(2 * step).wait()
        weights(2 * step + 1, odd_ref)
        multiply(2 * step, even_ref)
        weight_copy(2 * step).start()

        @pl.when(step < chunks // 2 - 1)
        def _():
            column_copy(2 * step + 2).start()

        @pl.when(step == 1)
        def _():
            lev_copy.start()

        column_copy(2 * step + 1).wait()
        weights(2 * step + 2, even_ref)
        multiply(2 * step + 1, odd_ref)
        weight_copy(2 * step + 1).start()
        return carry

    lax.fori_loop(0, chunks // 2, pair, 0)
    for i in range(components):
        for k in range(per_turbine):
            band = slice(k * points, (k + 1) * points)
            total = jnp.sum(acc_ref[i, band, :].T, axis=0, keepdims=True)
            part_ref[i : i + 1, band] = smear_norm * total
    part_ref[components:, :] = jnp.zeros((8 - components, count), F32)
    lev_copy.wait()
    for at in range(chunks):
        weight_copy(at).wait()


def sample(mine, twin, velocity, per_turbine):
    components, depth, rows, cols = velocity.shape
    points = mine.shape[2]
    count = per_turbine * points
    chunks = cols // STEP
    vmem = pl.BlockSpec(memory_space=pltpu.VMEM)
    hbm = pl.BlockSpec(memory_space=pltpu.HBM)
    return pl.pallas_call(
        functools.partial(sample_kernel, per_turbine),
        in_specs=[vmem, vmem, hbm],
        out_specs=[vmem, vmem, vmem, hbm, vmem],
        out_shape=[
            jax.ShapeDtypeStruct((8, count), F32),
            jax.ShapeDtypeStruct((8, count), F32),
            jax.ShapeDtypeStruct((mine.shape[0], per_turbine, points), F32),
            jax.ShapeDtypeStruct((2 * count, cols), BF16),
            jax.ShapeDtypeStruct((components, 2, rows, cols), F32),
        ],
        scratch_shapes=[
            pltpu.VMEM((count, STEP), F32),
            pltpu.VMEM((count, STEP), F32),
            pltpu.VMEM((count, 128), F32),
            pltpu.VMEM((count, 3 * depth * rows), BF16),
            pltpu.VMEM((components, count, 128), F32),
            pltpu.VMEM(velocity.shape, F32),
            pltpu.VMEM((2 * count, cols), BF16),
            pltpu.SemaphoreType.DMA((chunks,)),
            pltpu.SemaphoreType.DMA((chunks,)),
            pltpu.SemaphoreType.DMA,
        ],
        compiler_params=pltpu.CompilerParams(vmem_limit_bytes=58 * MIB),
        cost_estimate=LIGHT,
        name="sample",
    )(mine, twin, velocity)


def force_kernel(
    per_turbine, owned, mask_ref, part_ref, other_ref, own_ref, force_ref, home_ref
):
    points = own_ref.shape[1] // per_turbine
    relative = part_ref[0:3, :] + other_ref[0:3, :] - own_ref[3:6, :]
    speed = jnp.sqrt(jnp.sum(relative * relative, axis=0, keepdims=True))
    force = -own_ref[6:7, :] * speed * relative
    force_ref[...] = jnp.zeros(force_ref.shape, F32)
    force_ref[0:3, :] = force
    for row in range(mask_ref.shape[0]):
        total = jnp.zeros((3, points), F32)
        for k in range(per_turbine):
            total = jnp.where(mask_ref[row, k : k + 1, :] > 0.5, force[:, k * points : (k + 1) * points], total)
        for i in range(3):
            home_ref[row // owned, i, row % owned : row % owned + 1, :] = total[i : i + 1]


def point_forces(mask, part, other, own, per_turbine, owned):
    count = own.shape[1]
    points = count // per_turbine
    shifts = mask.shape[0] // owned
    return pl.pallas_call(
        functools.partial(force_kernel, per_turbine, owned),
        in_specs=[pl.BlockSpec(memory_space=pltpu.VMEM)] * 4,
        out_specs=[pl.BlockSpec(memory_space=pltpu.VMEM)] * 2,
        out_shape=[
            jax.ShapeDtypeStruct((8, count), F32),
            jax.ShapeDtypeStruct((shifts, 3, owned, points), F32),
        ],
        compiler_params=pltpu.CompilerParams(vmem_limit_bytes=58 * MIB),
        cost_estimate=LIGHT,
        name="force",
    )(mask, part, other, own)


def update_kernel(
    own_ref, force_ref, op_ref, left_ref, right_ref, near_in, far_in, relay_in, weight_in, vel_in, lev_in,
    new_out, zero_ref, pad_ref, new_ref, side_ref, weight_ref, high_ref, low_ref, even, odd,
    vel_sems, side_sems, weight_sems, new_sems, lev_sem,
):
    components, depth, rows, cols = new_ref.shape
    chunks = cols // STEP
    cells = LEVELS * rows
    inner = (LEVELS + 4) * rows
    fill = op_ref.shape[1] // 2 - inner - 4 * LEVELS
    count = own_ref.shape[1]
    core = lax.axis_index("gz")
    turbine = lax.axis_index("gy")
    parity = lax.axis_index("gx") % 2
    lane = lax.broadcasted_iota(jnp.int32, (8, 128), 1)
    shifts = ((1, lane < 1), (2, lane < 2), (127, lane >= 127), (126, lane >= 126))

    def column(at, first=0):
        return pl.ds(pl.multiple_of(at * STEP + first, 128), STEP)

    def arrivals(at):
        return [
            pltpu.make_async_copy(
                vel_in.at[:, :, :, column(at)],
                pad_ref.at[:, pl.ds(2, depth), :, column(at, 128)],
                vel_sems.at[at],
            ),
            pltpu.make_async_copy(
                weight_in.at[:, column(at)], weight_ref.at[:, column(at)], weight_sems.at[at]
            ),
            pltpu.make_async_copy(
                near_in.at[:, :, column(at)], side_ref.at[1 - parity, :, :, column(at)], side_sems.at[0, at]
            ),
            pltpu.make_async_copy(
                far_in.at[:, :, column(at)],
                side_ref.at[parity, :, pl.ds(0, depth), column(at)],
                side_sems.at[1, at],
            ),
            pltpu.make_async_copy(
                relay_in.at[:, :, column(at)],
                side_ref.at[parity, :, pl.ds(depth, depth), column(at)],
                side_sems.at[2, at],
            ),
        ]

    def departure(at):
        return pltpu.make_async_copy(
            new_ref.at[:, :, :, column(at)], new_out.at[:, :, :, column(at)], new_sems.at[at]
        )

    def level_copy(at):
        return pltpu.make_async_copy(
            lev_in, pad_ref.at[:, pl.ds(at, 2), :, pl.ds(128, cols)], lev_sem
        )

    def side_columns(ref, present, lane):
        per_part = 128 // rows
        parts = ref.shape[0] // components
        for tile in range(ref.shape[0]):
            turned = jnp.where(present, ref[tile], 0.0).T
            for k in range(per_part):
                level = (tile % parts) * per_part + k
                pad_ref[tile // parts, level + 2, :, lane : lane + 8] = turned[k * rows : (k + 1) * rows, :]

    def matrix_part(at, bufs):
        grad_ref, lap_ref, body_ref = bufs
        pad = pad_ref.at[:, :, :, column(at, 128)]
        sides = side_ref.at[:, :, :, column(at)]
        weight = weight_ref.at[:, column(at)]
        for i in range(components):
            for half in range(depth // LEVELS):
                levels = slice(half * LEVELS, (half + 1) * LEVELS)
                field = pad[i, half * LEVELS : (half + 1) * LEVELS + 4]
                inner_high, inner_low = split(field.reshape(inner, STEP))
                side = slice(half * 2 * LEVELS, (half + 1) * 2 * LEVELS)
                prev_high, prev_low = split(sides[0, i, side])
                next_high, next_low = split(sides[1, i, side])
                empty = [jnp.zeros((fill, STEP), BF16)] if fill else []
                high = [inner_high, prev_high, next_high] + empty
                low = [inner_low, prev_low, next_low] + empty
                result = dot(op_ref[...], jnp.concatenate(high + low, axis=0))
                grad_ref[i, levels] = result[:cells].reshape(LEVELS, rows, STEP)
                lap_ref[i, levels] = result[cells:].reshape(LEVELS, rows, STEP)
        upper = weight[:count]
        lower = weight[count:]
        wide = jnp.concatenate([high_ref[...], low_ref[...], high_ref[...]], axis=1)
        result = dot(wide, jnp.concatenate([upper, upper, lower], axis=0))
        body_ref[...] = result.reshape(components, depth, rows, STEP)

    def vector_part(at, bufs):
        grad_ref, lap_ref, body_ref = bufs
        pad = pad_ref.at[:, :, :, pl.ds(pl.multiple_of(at * STEP, 128), STEP + 256)]
        new = new_ref.at[:, :, :, column(at)]

        def cell(i, level, band, block):
            return pad[i, level, band, block * 128 : block * 128 + 128]

        def work(level, band):
            here = level + 2
            turned, center = {}, {}

            def middle(i, block):
                if (i, block) not in center:
                    center[i, block] = cell(i, here, band, block)
                return center[i, block]

            def turn(i, block, shift):
                if (i, block, shift) not in turned:
                    turned[i, block, shift] = pltpu.roll(middle(i, block), shift, 1)
                return turned[i, block, shift]

            for block in range(1, STEP // 128 + 1):
                lanes = slice(block * 128 - 128, block * 128)
                along_y, lap, along_z = [], [], []
                for i in range(components):
                    behind, behind2, ahead, ahead2 = [
                        jnp.where(
                            wrapped,
                            turn(i, block - 1 if shift < 64 else block + 1, shift),
                            turn(i, block, shift),
                        )
                        for shift, wrapped in shifts
                    ]
                    along_y.append(8.0 * (ahead - behind) - (ahead2 - behind2))
                    lap.append(
                        lap_ref[i, level, band, lanes]
                        + (16.0 * (ahead + behind) - (ahead2 + behind2))
                    )
                    near = cell(i, here + 1, band, block) - cell(i, here - 1, band, block)
                    far = cell(i, here + 2, band, block) - cell(i, here - 2, band, block)
                    along_z.append(8.0 * near - far)
                along_x = [grad_ref[i, level, band, lanes] for i in range(components)]
                same = along_x[0] * along_x[0] + along_y[1] * along_y[1] + along_z[2] * along_z[2]
                xy = along_x[1] + along_y[0]
                xz = along_x[2] + along_z[0]
                yz = along_y[2] + along_z[1]
                strain = 2.0 * same + (xy * xy + xz * xz + yz * yz)
                mixing = (time_step / 12.0) * viscosity + (
                    time_step * smag_coeff * smag_coeff / 144.0
                ) * (strain * lax.rsqrt(jnp.maximum(strain, SMALLEST)))
                for i in range(components):
                    change = mixing * lap[i] - (time_step * mean_wind / 12.0) * along_x[i]
                    new[i, level, band, lanes] = (
                        middle(i, block) + body_ref[i, level, band, lanes] + change
                    )

        for level in range(depth):
            for row in range(0, rows, 8):
                work(level, slice(row, row + 8))
        departure(at).start()

    for copy in arrivals(0):
        copy.start()
    zero_ref[...] = jnp.zeros(zero_ref.shape, F32)

    @pl.when(core == 1)
    def _():
        level_copy(0).start()
        pad_ref[:, depth + 2 :, :, 128 : cols + 128] = jnp.zeros((components, 2, rows, cols), F32)

    @pl.when(core == 0)
    def _():
        level_copy(depth + 2).start()
        pad_ref[:, 0:2, :, 128 : cols + 128] = jnp.zeros((components, 2, rows, cols), F32)

    side_columns(left_ref, turbine > 0, 120)
    side_columns(right_ref, turbine < lax.axis_size("gy") - 1, cols + 128)
    along_x = gaussian(lax.axis_index("gx") * rows, rows, own_ref[0:1, :])
    along_z = gaussian(core * depth, depth, own_ref[2:3, :])
    for i in range(components):
        scaled = (time_step * smear_norm) * force_ref[i : i + 1, :] * along_x
        for level in range(depth):
            band = slice((i * depth + level) * rows, (i * depth + level + 1) * rows)
            high, low = split(scaled * along_z[level : level + 1, :])
            high_ref[band, :] = high
            low_ref[band, :] = low
    level_copy(0).wait()
    for copy in arrivals(0):
        copy.wait()
    for copy in arrivals(1) + arrivals(2):
        copy.start()
    matrix_part(0, even)

    def pair(step, carry):
        for copy in arrivals(2 * step + 1) + arrivals(2 * step + 2):
            copy.wait()
        for copy in arrivals(2 * step + 3):
            copy.start()

        @pl.when(step < chunks // 2 - 2)
        def _():
            for copy in arrivals(2 * step + 4):
                copy.start()

        matrix_part(2 * step + 1, odd)
        vector_part(2 * step, even)
        matrix_part(2 * step + 2, even)
        vector_part(2 * step + 1, odd)
        return carry

    lax.fori_loop(0, chunks // 2 - 1, pair, 0)
    for copy in arrivals(chunks - 1):
        copy.wait()
    matrix_part(chunks - 1, odd)
    vector_part(chunks - 2, even)
    vector_part(chunks - 1, odd)
    for at in range(chunks):
        departure(at).wait()


def update(own, force, operator, near, far, relay, weight, velocity, lev, left, right, home_shape):
    components, depth, rows, cols = velocity.shape
    count = own.shape[1]
    chunks = cols // STEP
    vmem = pl.BlockSpec(memory_space=pltpu.VMEM)
    hbm = pl.BlockSpec(memory_space=pltpu.HBM)
    fields = [pltpu.VMEM((components, depth, rows, STEP), F32)] * 3
    macs = components * depth * rows * cols * (3 * count + 4 * 256)
    return pl.pallas_call(
        update_kernel,
        in_specs=[vmem] * 5 + [hbm] * 6,
        out_specs=[hbm, vmem],
        out_shape=[
            jax.ShapeDtypeStruct(velocity.shape, F32),
            jax.ShapeDtypeStruct(home_shape, F32),
        ],
        scratch_shapes=[
            pltpu.VMEM((components, depth + 4, rows, cols + 256), F32),
            pltpu.VMEM(velocity.shape, F32),
            pltpu.VMEM((2, *near.shape), F32),
            pltpu.VMEM((2 * count, cols), BF16),
            pltpu.VMEM((components * depth * rows, count), BF16),
            pltpu.VMEM((components * depth * rows, count), BF16),
            fields,
            fields,
            pltpu.SemaphoreType.DMA((chunks,)),
            pltpu.SemaphoreType.DMA((3, chunks)),
            pltpu.SemaphoreType.DMA((chunks,)),
            pltpu.SemaphoreType.DMA((chunks,)),
            pltpu.SemaphoreType.DMA,
        ],
        compiler_params=pltpu.CompilerParams(vmem_limit_bytes=44 * MIB),
        cost_estimate=pl.CostEstimate(
            flops=2 * macs, bytes_accessed=8 * velocity.size, transcendentals=velocity.size // 3
        ),
        name="update",
    )(own, force, operator, left, right, near, far, relay, weight, velocity, lev)


def local(velocity, blade_pos, block_turbine, blade_vel, lift_coeff):
    components, depth, rows, cols = velocity.shape
    owned, _, points = blade_pos.shape
    gx, gy, gz = (lax.axis_size(axis) for axis in ("gx", "gy", "gz"))
    assert gz == 2 and depth == 2 * LEVELS
    per_turbine = owned * gz
    swap = [(0, 1), (1, 0)]

    def around(shift):
        return [(i, (i + shift) % gy) for i in range(gy)]

    blocks, up, down, near, far, relay = prep(
        velocity, blade_pos, block_turbine, blade_vel, lift_coeff
    )
    near = lax.ppermute(near, "gx", [(i, i ^ 1) for i in range(gx)])
    across = [(i, i + 1) for i in range(1, gx - 1, 2)] + [(i + 1, i) for i in range(1, gx - 1, 2)]
    if gx == 4:
        relay = lax.ppermute(relay, "gx", [(1, 3), (2, 0)])

    def gather(blocks, up, down):
        left = lax.ppermute(up, "gy", around(1))
        right = lax.ppermute(down, "gy", around(gy - 1))
        parts = [blocks, left[:owned]]
        parts += [lax.ppermute(blocks, "gy", around(shift)) for shift in range(2, gy - 1)]
        parts.append(right[:owned])
        mine = jnp.concatenate(parts, axis=0)
        return mine, lax.ppermute(mine, "gz", swap), left[owned:], right[owned:]

    def blade(mine, twin, velocity):
        part, own, mask, weight, facing = sample(mine, twin, velocity, per_turbine)
        other = lax.ppermute(part, "gz", swap)
        lev = lax.ppermute(facing, "gz", swap)
        force, home = point_forces(mask, part, other, own, per_turbine, owned)
        return own, force, home, weight, lev

    def stage(run, *operands):
        empty = [jnp.zeros(out.shape, out.dtype) for out in jax.eval_shape(run, *operands)]
        return lax.cond(block_turbine[0] >= 0, run, lambda *_: tuple(empty), *operands)

    mine, twin, left, right = stage(gather, blocks, up, down)
    if gx == 4:
        relay = lax.ppermute(relay, "gx", [(3, 2), (0, 1)])
    else:
        relay = lax.ppermute(relay, "gx", across)
    far = lax.ppermute(far, "gx", across)
    own, force, home, weight, lev = stage(blade, mine, twin, velocity)
    result = home[0]
    for shift in range(1, gy):
        result += lax.ppermute(home[shift], "gy", around(gy - shift))

    operator = jnp.asarray(stencil_operator(rows))
    new_velocity, zero = update(
        own, force, operator, near, far, relay, weight, velocity, lev, left, right, result.shape
    )
    return (new_velocity, (result + zero).transpose(1, 0, 2))


def solution(mesh):
    in_specs = (
        P(None, "gz", "gx", "gy"),
        P(("gx", "gy", "gz"), None, None),
        P(("gx", "gy", "gz")),
        P(("gx", "gy", "gz"), None, None),
        P(("gx", "gy", "gz"), None),
    )
    out_specs = (P(None, "gz", "gx", "gy"), P(("gx", "gy", "gz"), None, None))
    return jax.shard_map(local, mesh=mesh, in_specs=in_specs, out_specs=out_specs, check_vma=False)
```

```python
import functools
import math

import jax
import jax.numpy as jnp
import ml_dtypes
import numpy as np
from jax import lax
from jax.experimental import pallas as pl
from jax.experimental.pallas import tpu as pltpu
from jax.sharding import PartitionSpec as P

mean_wind = 1.0
viscosity = 0.2
smag_coeff = 0.17
time_step = 0.2
smear = 2.0
smear_norm = 1.0 / (smear**3 * math.pi**1.5)

F32 = jnp.float32
BF16 = jnp.bfloat16
SMALLEST = float(jnp.finfo(F32).tiny)
MIB = 1024 * 1024
LEVELS = 8
STEP = 256
LIGHT = pl.CostEstimate(flops=0, bytes_accessed=0, transcendentals=0)


def split(value):
    high = value.astype(BF16)
    return high, (value - high.astype(F32)).astype(BF16)


def dot(left, right, contract=0):
    return lax.dot_general(
        left, right, (((1,), (contract,)), ((), ())), preferred_element_type=F32
    )


def gaussian(first, count, centers):
    shape = (count, centers.shape[1])
    cells = (first + lax.broadcasted_iota(jnp.int32, shape, 0)).astype(F32)
    gap = cells - centers
    return jnp.exp(-gap * gap / (smear * smear))


def stencil_operator(row_cells):
    inner = (LEVELS + 4) * row_cells
    width = inner + 4 * LEVELS
    op = np.zeros((2, LEVELS, row_cells, width), np.float32)

    def column(level, row):
        if 0 <= row < row_cells:
            return (level + 2) * row_cells + row
        if row < 0:
            return inner + level * 2 + row + 2
        return inner + 2 * LEVELS + level * 2 + row - row_cells

    for level in range(LEVELS):
        for row in range(row_cells):
            for offset, first, second in ((-2, 1, -1), (-1, -8, 16), (1, 8, 16), (2, -1, -1)):
                op[0, level, row, column(level, row + offset)] += first
                op[1, level, row, column(level, row + offset)] += second
                op[1, level, row, column(level + offset, row)] += second
            op[1, level, row, column(level, row)] -= 90
    op = op.reshape(2 * LEVELS * row_cells, width)
    op = np.pad(op, ((0, 0), (0, -width % 128)))
    return np.concatenate([op, op], axis=1).astype(ml_dtypes.bfloat16)


def prep_kernel(
    turb_in, pos_in, speed_in, lift_in, vel_in, blocks_ref, up_ref, down_ref, near_ref, far_ref, relay_ref,
    turb_ref, pos_ref, speed_ref, lift_ref, vel_ref, sems,
):
    components, levels, rows, cols = vel_ref.shape
    coords, owned, points = pos_ref.shape
    small = [
        pltpu.make_async_copy(source, target, sems.at[components + k])
        for k, (source, target) in enumerate(
            ((turb_in, turb_ref), (pos_in, pos_ref), (speed_in, speed_ref), (lift_in, lift_ref))
        )
    ]
    large = [
        pltpu.make_async_copy(vel_in.at[i], vel_ref.at[i], sems.at[i]) for i in range(components)
    ]
    for copy in small + large:
        copy.start()
    for copy in small:
        copy.wait()
    for ref in (blocks_ref, up_ref, down_ref):
        for k in range(owned):
            for i in range(coords):
                ref[k, i : i + 1, :] = pos_ref[i, k : k + 1, :]
                ref[k, coords + i : coords + i + 1, :] = speed_ref[i, k : k + 1, :]
            ref[k, 2 * coords : 2 * coords + 1, :] = lift_ref[k : k + 1, :]
            ref[k, 7:8, :] = jnp.full((1, points), turb_ref[k].astype(F32))
    parts = levels * rows // 128
    odd = lax.axis_index("gx") % 2 == 1
    row = lax.broadcasted_iota(jnp.int32, (8, cols), 0) // 2
    for component in range(components):
        large[component].wait()
        last = vel_ref[component, :, :, cols - 128 :].reshape(levels * rows, 128)
        first = vel_ref[component, :, :, :128].reshape(levels * rows, 128)
        for part in range(parts):
            cells = slice(part * 128, part * 128 + 128)
            up_ref[owned + component * parts + part] = last[cells].T[120:]
            down_ref[owned + component * parts + part] = first[cells].T[:8]
        for group in range(levels // 4):
            head = tail = None
            for k in range(4):
                top = vel_ref[component, group * 4 + k, 0:8, :]
                end = vel_ref[component, group * 4 + k, rows - 8 : rows, :]
                if k:
                    top = pltpu.roll(top, 2 * k, 0)
                if k < 3:
                    end = pltpu.roll(end, 2 * k + 2, 0)
                head = top if head is None else jnp.where(row == k, top, head)
                tail = end if tail is None else jnp.where(row == k, end, tail)
            near_ref[component, group * 8 : group * 8 + 8, :] = jnp.where(odd, head, tail)
            ref, to = (far_ref, group * 8) if group * 8 < levels else (relay_ref, group * 8 - levels)
            ref[component, to : to + 8, :] = jnp.where(odd, tail, head)


def prep(velocity, blade_pos, block_turbine, blade_vel, lift_coeff):
    components, levels, rows, cols = velocity.shape
    owned, coords, points = blade_pos.shape
    tiles = owned + components * levels * rows // 128
    return pl.pallas_call(
        prep_kernel,
        in_specs=[pl.BlockSpec(memory_space=pltpu.HBM)] * 5,
        out_specs=[pl.BlockSpec(memory_space=pltpu.VMEM)] * 6,
        out_shape=[
            jax.ShapeDtypeStruct((owned, 8, points), F32),
            jax.ShapeDtypeStruct((tiles, 8, 128), F32),
            jax.ShapeDtypeStruct((tiles, 8, 128), F32),
            jax.ShapeDtypeStruct((components, 2 * levels, cols), F32),
            jax.ShapeDtypeStruct((components, levels, cols), F32),
            jax.ShapeDtypeStruct((components, levels, cols), F32),
        ],
        scratch_shapes=[
            pltpu.SMEM((owned,), jnp.int32),
            pltpu.VMEM((coords, owned, points), F32),
            pltpu.VMEM((coords, owned, points), F32),
            pltpu.VMEM((owned, points), F32),
            pltpu.VMEM(velocity.shape, F32),
            pltpu.SemaphoreType.DMA((components + 4,)),
        ],
        compiler_params=pltpu.CompilerParams(vmem_limit_bytes=60 * MIB),
        cost_estimate=LIGHT,
        name="prep",
    )(
        block_turbine,
        blade_pos.transpose(1, 0, 2),
        blade_vel.transpose(1, 0, 2),
        lift_coeff,
        velocity,
    )


def match(mine_ref, twin_ref, per_turbine):
    core = lax.axis_index("gz")
    turbine = lax.axis_index("gy").astype(F32)
    half = mine_ref.shape[0]
    first = [(mine_ref[k, 7:8, :] == turbine).astype(F32) for k in range(half)]
    second = [(twin_ref[k, 7:8, :] == turbine).astype(F32) for k in range(half)]
    masks = []
    for hits, others, leads in ((first, second, core == 0), (second, first, core == 1)):
        rank = jnp.where(leads, jnp.zeros_like(hits[0]), sum(others))
        for hit in hits:
            masks.append([(hit > 0.5) & (rank == k) for k in range(per_turbine)])
            rank = rank + hit
    return masks


def sample_kernel(
    per_turbine, mine_ref, twin_ref, vel_in, part_ref, own_ref, mask_ref, weight_out, lev_ref,
    bell_ref, center_ref, plane_ref, acc_ref, vel_ref, weight_ref, sems, out_sem, lev_sem,
):
    components, depth, rows, cols = vel_ref.shape
    points = mine_ref.shape[2]
    count = per_turbine * points
    cells = depth * rows
    chunks = cols // STEP
    core = lax.axis_index("gz")
    start = lax.axis_index("gy") * cols
    arrivals = [
        pltpu.make_async_copy(vel_in.at[i], vel_ref.at[i], sems.at[i]) for i in range(components)
    ]
    weight_copy = pltpu.make_async_copy(weight_ref, weight_out, out_sem)
    lev_copy = pltpu.make_async_copy(
        vel_in.at[:, pl.ds(jnp.where(core == 0, depth - 2, 0), 2)], lev_ref, lev_sem
    )

    def column(at):
        return pl.ds(pl.multiple_of(at * STEP, STEP), STEP)

    def bell(cell, center):
        gap = cell.astype(F32) - center
        return jnp.exp(gap * gap * (-1.0 / (smear * smear)))

    def weights(at):
        lane = lax.broadcasted_iota(jnp.int32, (1, 128), 1)
        keep = bell_ref.at[:, column(at)]
        out = weight_ref.at[:, column(at)]
        for part in range(STEP // 128):
            cell = start + at * STEP + part * 128 + lane
            value = bell(cell, center_ref[...])
            high, low = split(value)
            keep[:, part * 128 : part * 128 + 128] = value
            out[:count, part * 128 : part * 128 + 128] = high
            out[count:, part * 128 : part * 128 + 128] = low

    def multiply(i, at):
        high, low = split(vel_ref.at[i, :, :, column(at)][...].reshape(cells, STEP))
        field = dot(plane_ref[...], jnp.concatenate([high, high, low], axis=0))
        product = field * bell_ref[:, column(at)]
        total = acc_ref[i]
        for part in range(STEP // 128):
            total += product[:, part * 128 : part * 128 + 128]
        acc_ref[i] = total

    arrivals[0].start()
    masks = match(mine_ref, twin_ref, per_turbine)
    blocks = mine_ref.shape[0]
    lane = lax.broadcasted_iota(jnp.int32, (1, cells), 1)
    level = core * depth + lane // rows
    row = lax.axis_index("gx") * rows + lane % rows
    for k in range(per_turbine):
        total = jnp.zeros((8, points), F32)
        for at, mask in enumerate(masks):
            tile = mine_ref[at] if at < blocks else twin_ref[at - blocks]
            total = jnp.where(mask[k], tile, total)
        band = slice(k * points, (k + 1) * points)
        own_ref[:, band] = total
        turned = total.T
        center_ref[band, :] = jnp.broadcast_to(turned[:, 1:2], (points, 128))
        plane = bell(row, turned[:, 0:1]) * bell(level, turned[:, 2:3])
        high, low = split(plane)
        plane_ref[band, :cells] = high
        plane_ref[band, cells : 2 * cells] = low
        plane_ref[band, 2 * cells :] = high
    for at in range(blocks):
        for k in range(per_turbine):
            mask_ref[at, k : k + 1, :] = masks[at][k].astype(F32)
    acc_ref[...] = jnp.zeros(acc_ref.shape, F32)
    weights(0)
    arrivals[0].wait()
    for copy in arrivals[1:] + [lev_copy]:
        copy.start()

    def first(at, carry):
        weights(at + 1)
        multiply(0, at)
        return carry

    lax.fori_loop(0, chunks - 1, first, 0)
    multiply(0, chunks - 1)
    weight_copy.start()
    for copy in arrivals[1:]:
        copy.wait()

    def others(at, carry):
        for i in range(1, components):
            multiply(i, at)
        return carry

    lax.fori_loop(0, chunks, others, 0)
    for i in range(components):
        for k in range(per_turbine):
            band = slice(k * points, (k + 1) * points)
            total = jnp.sum(acc_ref[i, band, :].T, axis=0, keepdims=True)
            part_ref[i : i + 1, band] = smear_norm * total
    part_ref[components:, :] = jnp.zeros((8 - components, count), F32)
    lev_copy.wait()
    weight_copy.wait()


def sample(mine, twin, velocity, per_turbine):
    components, depth, rows, cols = velocity.shape
    points = mine.shape[2]
    count = per_turbine * points
    vmem = pl.BlockSpec(memory_space=pltpu.VMEM)
    hbm = pl.BlockSpec(memory_space=pltpu.HBM)
    return pl.pallas_call(
        functools.partial(sample_kernel, per_turbine),
        in_specs=[vmem, vmem, hbm],
        out_specs=[vmem, vmem, vmem, hbm, vmem],
        out_shape=[
            jax.ShapeDtypeStruct((8, count), F32),
            jax.ShapeDtypeStruct((8, count), F32),
            jax.ShapeDtypeStruct((mine.shape[0], per_turbine, points), F32),
            jax.ShapeDtypeStruct((2 * count, cols), BF16),
            jax.ShapeDtypeStruct((components, 2, rows, cols), F32),
        ],
        scratch_shapes=[
            pltpu.VMEM((count, cols), F32),
            pltpu.VMEM((count, 128), F32),
            pltpu.VMEM((count, 3 * depth * rows), BF16),
            pltpu.VMEM((components, count, 128), F32),
            pltpu.VMEM(velocity.shape, F32),
            pltpu.VMEM((2 * count, cols), BF16),
            pltpu.SemaphoreType.DMA((components,)),
            pltpu.SemaphoreType.DMA,
            pltpu.SemaphoreType.DMA,
        ],
        compiler_params=pltpu.CompilerParams(vmem_limit_bytes=58 * MIB),
        cost_estimate=LIGHT,
        name="sample",
    )(mine, twin, velocity)


def force_kernel(
    per_turbine, owned, mask_ref, part_ref, other_ref, own_ref, force_ref, home_ref
):
    points = own_ref.shape[1] // per_turbine
    relative = part_ref[0:3, :] + other_ref[0:3, :] - own_ref[3:6, :]
    speed = jnp.sqrt(jnp.sum(relative * relative, axis=0, keepdims=True))
    force = -own_ref[6:7, :] * speed * relative
    force_ref[...] = jnp.zeros(force_ref.shape, F32)
    force_ref[0:3, :] = force
    for row in range(mask_ref.shape[0]):
        total = jnp.zeros((3, points), F32)
        for k in range(per_turbine):
            total = jnp.where(mask_ref[row, k : k + 1, :] > 0.5, force[:, k * points : (k + 1) * points], total)
        for i in range(3):
            home_ref[row // owned, i, row % owned : row % owned + 1, :] = total[i : i + 1]


def point_forces(mask, part, other, own, per_turbine, owned):
    count = own.shape[1]
    points = count // per_turbine
    shifts = mask.shape[0] // owned
    return pl.pallas_call(
        functools.partial(force_kernel, per_turbine, owned),
        in_specs=[pl.BlockSpec(memory_space=pltpu.VMEM)] * 4,
        out_specs=[pl.BlockSpec(memory_space=pltpu.VMEM)] * 2,
        out_shape=[
            jax.ShapeDtypeStruct((8, count), F32),
            jax.ShapeDtypeStruct((shifts, 3, owned, points), F32),
        ],
        compiler_params=pltpu.CompilerParams(vmem_limit_bytes=58 * MIB),
        cost_estimate=LIGHT,
        name="force",
    )(mask, part, other, own)


def update_kernel(
    own_ref, force_ref, op_ref, left_ref, right_ref, near_in, far_in, relay_in, weight_in, vel_in, lev_in,
    new_out, zero_ref, pad_ref, new_ref, side_ref, weight_ref, high_ref, low_ref, even, odd,
    vel_sems, side_sems, weight_sem, new_sems, lev_sem,
):
    components, depth, rows, cols = new_ref.shape
    chunks = cols // STEP
    cells = LEVELS * rows
    inner = (LEVELS + 4) * rows
    fill = op_ref.shape[1] // 2 - inner - 4 * LEVELS
    count = own_ref.shape[1]
    core = lax.axis_index("gz")
    turbine = lax.axis_index("gy")
    parity = lax.axis_index("gx") % 2
    lane = lax.broadcasted_iota(jnp.int32, (8, 128), 1)
    shifts = ((1, lane < 1), (2, lane < 2), (127, lane >= 127), (126, lane >= 126))

    def column(at, first=0):
        return pl.ds(pl.multiple_of(at * STEP + first, 128), STEP)

    copies = [
        pltpu.make_async_copy(
            vel_in.at[i], pad_ref.at[i, pl.ds(2, depth), :, pl.ds(128, cols)], vel_sems.at[i]
        )
        for i in range(components)
    ]
    copies += [
        pltpu.make_async_copy(near_in, side_ref.at[1 - parity], side_sems.at[0]),
        pltpu.make_async_copy(far_in, side_ref.at[parity, :, pl.ds(0, depth)], side_sems.at[1]),
        pltpu.make_async_copy(relay_in, side_ref.at[parity, :, pl.ds(depth, depth)], side_sems.at[2]),
    ]
    weight_copy = pltpu.make_async_copy(weight_in, weight_ref, weight_sem)

    def departure(at):
        return pltpu.make_async_copy(
            new_ref.at[:, :, :, column(at)], new_out.at[:, :, :, column(at)], new_sems.at[at]
        )

    def level_copy(at):
        return pltpu.make_async_copy(
            lev_in, pad_ref.at[:, pl.ds(at, 2), :, pl.ds(128, cols)], lev_sem
        )

    def side_columns(ref, present, lane):
        per_part = 128 // rows
        parts = ref.shape[0] // components
        for tile in range(ref.shape[0]):
            turned = jnp.where(present, ref[tile], 0.0).T
            for k in range(per_part):
                level = (tile % parts) * per_part + k
                pad_ref[tile // parts, level + 2, :, lane : lane + 8] = turned[k * rows : (k + 1) * rows, :]

    def matrix_part(at, bufs):
        stencil_part(at, bufs)
        body_part(at, bufs)

    def stencil_part(at, bufs):
        grad_ref, lap_ref, _ = bufs
        pad = pad_ref.at[:, :, :, column(at, 128)]
        sides = side_ref.at[:, :, :, column(at)]
        for i in range(components):
            for half in range(depth // LEVELS):
                levels = slice(half * LEVELS, (half + 1) * LEVELS)
                field = pad[i, half * LEVELS : (half + 1) * LEVELS + 4]
                inner_high, inner_low = split(field.reshape(inner, STEP))
                side = slice(half * 2 * LEVELS, (half + 1) * 2 * LEVELS)
                prev_high, prev_low = split(sides[0, i, side])
                next_high, next_low = split(sides[1, i, side])
                empty = [jnp.zeros((fill, STEP), BF16)] if fill else []
                high = [inner_high, prev_high, next_high] + empty
                low = [inner_low, prev_low, next_low] + empty
                result = dot(op_ref[...], jnp.concatenate(high + low, axis=0))
                grad_ref[i, levels] = result[:cells].reshape(LEVELS, rows, STEP)
                lap_ref[i, levels] = result[cells:].reshape(LEVELS, rows, STEP)

    def body_part(at, bufs):
        body_ref = bufs[2]
        weight = weight_ref.at[:, column(at)]
        upper = weight[:count]
        lower = weight[count:]
        wide = jnp.concatenate([high_ref[...], low_ref[...], high_ref[...]], axis=1)
        result = dot(wide, jnp.concatenate([upper, upper, lower], axis=0))
        body_ref[...] = result.reshape(components, depth, rows, STEP)

    def vector_part(at, bufs):
        grad_ref, lap_ref, body_ref = bufs
        pad = pad_ref.at[:, :, :, pl.ds(pl.multiple_of(at * STEP, 128), STEP + 256)]
        new = new_ref.at[:, :, :, column(at)]

        def cell(i, level, band, block):
            return pad[i, level, band, block * 128 : block * 128 + 128]

        def work(level, band):
            here = level + 2
            turned, center = {}, {}

            def middle(i, block):
                if (i, block) not in center:
                    center[i, block] = cell(i, here, band, block)
                return center[i, block]

            def turn(i, block, shift):
                if (i, block, shift) not in turned:
                    turned[i, block, shift] = pltpu.roll(middle(i, block), shift, 1)
                return turned[i, block, shift]

            for block in range(1, STEP // 128 + 1):
                lanes = slice(block * 128 - 128, block * 128)
                along_y, lap, along_z = [], [], []
                for i in range(components):
                    behind, behind2, ahead, ahead2 = [
                        jnp.where(
                            wrapped,
                            turn(i, block - 1 if shift < 64 else block + 1, shift),
                            turn(i, block, shift),
                        )
                        for shift, wrapped in shifts
                    ]
                    along_y.append(8.0 * (ahead - behind) - (ahead2 - behind2))
                    lap.append(
                        lap_ref[i, level, band, lanes]
                        + (16.0 * (ahead + behind) - (ahead2 + behind2))
                    )
                    near = cell(i, here + 1, band, block) - cell(i, here - 1, band, block)
                    far = cell(i, here + 2, band, block) - cell(i, here - 2, band, block)
                    along_z.append(8.0 * near - far)
                along_x = [grad_ref[i, level, band, lanes] for i in range(components)]
                same = along_x[0] * along_x[0] + along_y[1] * along_y[1] + along_z[2] * along_z[2]
                xy = along_x[1] + along_y[0]
                xz = along_x[2] + along_z[0]
                yz = along_y[2] + along_z[1]
                strain = 2.0 * same + (xy * xy + xz * xz + yz * yz)
                mixing = (time_step / 12.0) * viscosity + (
                    time_step * smag_coeff * smag_coeff / 144.0
                ) * (strain * lax.rsqrt(jnp.maximum(strain, SMALLEST)))
                for i in range(components):
                    change = mixing * lap[i] - (time_step * mean_wind / 12.0) * along_x[i]
                    new[i, level, band, lanes] = (
                        middle(i, block) + body_ref[i, level, band, lanes] + change
                    )

        for level in range(depth):
            for row in range(0, rows, 8):
                work(level, slice(row, row + 8))
        departure(at).start()

    for copy in copies:
        copy.start()
    zero_ref[...] = jnp.zeros(zero_ref.shape, F32)

    @pl.when(core == 1)
    def _():
        level_copy(0).start()
        pad_ref[:, depth + 2 :, :, 128 : cols + 128] = jnp.zeros((components, 2, rows, cols), F32)

    @pl.when(core == 0)
    def _():
        level_copy(depth + 2).start()
        pad_ref[:, 0:2, :, 128 : cols + 128] = jnp.zeros((components, 2, rows, cols), F32)

    side_columns(left_ref, turbine > 0, 120)
    side_columns(right_ref, turbine < lax.axis_size("gy") - 1, cols + 128)
    along_x = gaussian(lax.axis_index("gx") * rows, rows, own_ref[0:1, :])
    along_z = gaussian(core * depth, depth, own_ref[2:3, :])
    for i in range(components):
        scaled = (time_step * smear_norm) * force_ref[i : i + 1, :] * along_x
        for level in range(depth):
            band = slice((i * depth + level) * rows, (i * depth + level + 1) * rows)
            high, low = split(scaled * along_z[level : level + 1, :])
            high_ref[band, :] = high
            low_ref[band, :] = low
    level_copy(0).wait()
    for copy in copies:
        copy.wait()
    weight_copy.start()
    stencil_part(0, even)
    weight_copy.wait()
    body_part(0, even)

    def pair(step, carry):
        matrix_part(2 * step + 1, odd)
        vector_part(2 * step, even)
        matrix_part(2 * step + 2, even)
        vector_part(2 * step + 1, odd)
        return carry

    lax.fori_loop(0, chunks // 2 - 1, pair, 0)
    matrix_part(chunks - 1, odd)
    vector_part(chunks - 2, even)
    vector_part(chunks - 1, odd)
    for at in range(chunks):
        departure(at).wait()


def update(own, force, operator, near, far, relay, weight, velocity, lev, left, right, home_shape):
    components, depth, rows, cols = velocity.shape
    count = own.shape[1]
    chunks = cols // STEP
    vmem = pl.BlockSpec(memory_space=pltpu.VMEM)
    hbm = pl.BlockSpec(memory_space=pltpu.HBM)
    fields = [pltpu.VMEM((components, depth, rows, STEP), F32)] * 3
    macs = components * depth * rows * cols * (3 * count + 4 * 256)
    return pl.pallas_call(
        update_kernel,
        in_specs=[vmem] * 5 + [hbm] * 6,
        out_specs=[hbm, vmem],
        out_shape=[
            jax.ShapeDtypeStruct(velocity.shape, F32),
            jax.ShapeDtypeStruct(home_shape, F32),
        ],
        scratch_shapes=[
            pltpu.VMEM((components, depth + 4, rows, cols + 256), F32),
            pltpu.VMEM(velocity.shape, F32),
            pltpu.VMEM((2, *near.shape), F32),
            pltpu.VMEM((2 * count, cols), BF16),
            pltpu.VMEM((components * depth * rows, count), BF16),
            pltpu.VMEM((components * depth * rows, count), BF16),
            fields,
            fields,
            pltpu.SemaphoreType.DMA((components,)),
            pltpu.SemaphoreType.DMA((3,)),
            pltpu.SemaphoreType.DMA,
            pltpu.SemaphoreType.DMA((chunks,)),
            pltpu.SemaphoreType.DMA,
        ],
        compiler_params=pltpu.CompilerParams(vmem_limit_bytes=44 * MIB),
        cost_estimate=pl.CostEstimate(
            flops=2 * macs, bytes_accessed=8 * velocity.size, transcendentals=velocity.size // 3
        ),
        name="update",
    )(own, force, operator, left, right, near, far, relay, weight, velocity, lev)


def local(velocity, blade_pos, block_turbine, blade_vel, lift_coeff):
    components, depth, rows, cols = velocity.shape
    owned, _, points = blade_pos.shape
    gx, gy, gz = (lax.axis_size(axis) for axis in ("gx", "gy", "gz"))
    assert gz == 2 and depth == 2 * LEVELS
    per_turbine = owned * gz
    swap = [(0, 1), (1, 0)]

    def around(shift):
        return [(i, (i + shift) % gy) for i in range(gy)]

    blocks, up, down, near, far, relay = prep(
        velocity, blade_pos, block_turbine, blade_vel, lift_coeff
    )
    near = lax.ppermute(near, "gx", [(i, i ^ 1) for i in range(gx)])
    across = [(i, i + 1) for i in range(1, gx - 1, 2)] + [(i + 1, i) for i in range(1, gx - 1, 2)]
    if gx == 4:
        relay = lax.ppermute(relay, "gx", [(1, 3), (2, 0)])

    def gather(blocks, up, down):
        left = lax.ppermute(up, "gy", around(1))
        right = lax.ppermute(down, "gy", around(gy - 1))
        parts = [blocks, left[:owned]]
        parts += [lax.ppermute(blocks, "gy", around(shift)) for shift in range(2, gy - 1)]
        parts.append(right[:owned])
        mine = jnp.concatenate(parts, axis=0)
        return mine, lax.ppermute(mine, "gz", swap), left[owned:], right[owned:]

    def blade(mine, twin, velocity):
        part, own, mask, weight, facing = sample(mine, twin, velocity, per_turbine)
        other = lax.ppermute(part, "gz", swap)
        lev = lax.ppermute(facing, "gz", swap)
        force, home = point_forces(mask, part, other, own, per_turbine, owned)
        return own, force, home, weight, lev

    def stage(run, *operands):
        empty = [jnp.zeros(out.shape, out.dtype) for out in jax.eval_shape(run, *operands)]
        return lax.cond(block_turbine[0] >= 0, run, lambda *_: tuple(empty), *operands)

    mine, twin, left, right = stage(gather, blocks, up, down)
    if gx == 4:
        relay = lax.ppermute(relay, "gx", [(3, 2), (0, 1)])
    else:
        relay = lax.ppermute(relay, "gx", across)
    far = lax.ppermute(far, "gx", across)
    own, force, home, weight, lev = stage(blade, mine, twin, velocity)
    result = home[0]
    for shift in range(1, gy):
        result += lax.ppermute(home[shift], "gy", around(gy - shift))

    operator = jnp.asarray(stencil_operator(rows))
    new_velocity, zero = update(
        own, force, operator, near, far, relay, weight, velocity, lev, left, right, result.shape
    )
    return (new_velocity, (result + zero).transpose(1, 0, 2))


def solution(mesh):
    in_specs = (
        P(None, "gz", "gx", "gy"),
        P(("gx", "gy", "gz"), None, None),
        P(("gx", "gy", "gz")),
        P(("gx", "gy", "gz"), None, None),
        P(("gx", "gy", "gz"), None),
    )
    out_specs = (P(None, "gz", "gx", "gy"), P(("gx", "gy", "gz"), None, None))
    return jax.shard_map(local, mesh=mesh, in_specs=in_specs, out_specs=out_specs, check_vma=False)
```

```python
import functools
import math

import jax
import jax.numpy as jnp
import ml_dtypes
import numpy as np
from jax import lax
from jax.experimental import pallas as pl
from jax.experimental.pallas import tpu as pltpu
from jax.sharding import PartitionSpec as P

mean_wind = 1.0
viscosity = 0.2
smag_coeff = 0.17
time_step = 0.2
smear = 2.0
smear_norm = 1.0 / (smear**3 * math.pi**1.5)

F32 = jnp.float32
BF16 = jnp.bfloat16
MIB = 1024 * 1024
PREP, SAMPLE, UPDATE = 54, 32, 42
LEVELS = 8
STEP = 256
LIGHT = pl.CostEstimate(flops=0, bytes_accessed=0, transcendentals=0)


def split(value):
    high = value.astype(BF16)
    return high, (value - high.astype(F32)).astype(BF16)


def dot(left, right, contract=0):
    return lax.dot_general(
        left, right, (((1,), (contract,)), ((), ())), preferred_element_type=F32
    )


def gaussian(first, count, centers):
    shape = (count, centers.shape[1])
    cells = (first + lax.broadcasted_iota(jnp.int32, shape, 0)).astype(F32)
    gap = cells - centers
    return jnp.exp(-gap * gap / (smear * smear))


def stencil_operator(row_cells):
    inner = (LEVELS + 4) * row_cells
    width = inner + 4 * LEVELS
    op = np.zeros((2, LEVELS, row_cells, width), np.float32)

    def column(level, row):
        if 0 <= row < row_cells:
            return (level + 2) * row_cells + row
        if row < 0:
            return inner + level * 2 + row + 2
        return inner + 2 * LEVELS + level * 2 + row - row_cells

    for level in range(LEVELS):
        for row in range(row_cells):
            for offset, first, second in ((-2, 1, -1), (-1, -8, 16), (1, 8, 16), (2, -1, -1)):
                op[0, level, row, column(level, row + offset)] += first
                op[1, level, row, column(level, row + offset)] += second
                op[1, level, row, column(level + offset, row)] += second
            op[1, level, row, column(level, row)] -= 90
    op = op.reshape(2 * LEVELS * row_cells, width)
    op = np.pad(op, ((0, 0), (0, -width % 128)))
    return np.concatenate([op, op], axis=1).astype(ml_dtypes.bfloat16)


def prep_kernel(
    turb_in, pos_in, speed_in, lift_in, vel_in, vel_ref, blocks_ref, up_ref, down_ref, near_ref, far_ref,
    relay_ref, turb_ref, pos_ref, speed_ref, lift_ref, sems,
):
    components, levels, rows, cols = vel_ref.shape
    coords, owned, points = pos_ref.shape
    small = [
        pltpu.make_async_copy(source, target, sems.at[components + k])
        for k, (source, target) in enumerate(
            ((turb_in, turb_ref), (pos_in, pos_ref), (speed_in, speed_ref), (lift_in, lift_ref))
        )
    ]
    large = [
        pltpu.make_async_copy(vel_in.at[i], vel_ref.at[i], sems.at[i]) for i in range(components)
    ]
    for copy in small + large:
        copy.start()
    for copy in small:
        copy.wait()
    for ref in (blocks_ref, up_ref, down_ref):
        for k in range(owned):
            for i in range(coords):
                ref[k, i : i + 1, :] = pos_ref[i, k : k + 1, :]
                ref[k, coords + i : coords + i + 1, :] = speed_ref[i, k : k + 1, :]
            ref[k, 2 * coords : 2 * coords + 1, :] = lift_ref[k : k + 1, :]
            ref[k, 7:8, :] = jnp.full((1, points), turb_ref[k].astype(F32))
    parts = levels * rows // 128
    odd = lax.axis_index("gx") % 2 == 1
    row = lax.broadcasted_iota(jnp.int32, (8, cols), 0) // 2
    for component in range(components):
        large[component].wait()
        last = vel_ref[component, :, :, cols - 128 :].reshape(levels * rows, 128)
        first = vel_ref[component, :, :, :128].reshape(levels * rows, 128)
        for part in range(parts):
            cells = slice(part * 128, part * 128 + 128)
            up_ref[owned + component * parts + part] = last[cells].T[120:]
            down_ref[owned + component * parts + part] = first[cells].T[:8]
        for group in range(levels // 4):
            head = tail = None
            for k in range(4):
                top = vel_ref[component, group * 4 + k, 0:8, :]
                end = vel_ref[component, group * 4 + k, rows - 8 : rows, :]
                if k:
                    top = pltpu.roll(top, 2 * k, 0)
                if k < 3:
                    end = pltpu.roll(end, 2 * k + 2, 0)
                head = top if head is None else jnp.where(row == k, top, head)
                tail = end if tail is None else jnp.where(row == k, end, tail)
            near_ref[component, group * 8 : group * 8 + 8, :] = jnp.where(odd, head, tail)
            ref, to = (far_ref, group * 8) if group * 8 < levels else (relay_ref, group * 8 - levels)
            ref[component, to : to + 8, :] = jnp.where(odd, tail, head)


def prep(velocity, blade_pos, block_turbine, blade_vel, lift_coeff):
    components, levels, rows, cols = velocity.shape
    owned, coords, points = blade_pos.shape
    tiles = owned + components * levels * rows // 128
    return pl.pallas_call(
        prep_kernel,
        in_specs=[pl.BlockSpec(memory_space=pltpu.HBM)] * 5,
        out_specs=[pl.BlockSpec(memory_space=pltpu.VMEM)] * 7,
        out_shape=[
            jax.ShapeDtypeStruct(velocity.shape, F32),
            jax.ShapeDtypeStruct((owned, 8, points), F32),
            jax.ShapeDtypeStruct((tiles, 8, 128), F32),
            jax.ShapeDtypeStruct((tiles, 8, 128), F32),
            jax.ShapeDtypeStruct((components, 2 * levels, cols), F32),
            jax.ShapeDtypeStruct((components, levels, cols), F32),
            jax.ShapeDtypeStruct((components, levels, cols), F32),
        ],
        scratch_shapes=[
            pltpu.SMEM((owned,), jnp.int32),
            pltpu.VMEM((coords, owned, points), F32),
            pltpu.VMEM((coords, owned, points), F32),
            pltpu.VMEM((owned, points), F32),
            pltpu.SemaphoreType.DMA((components + 4,)),
        ],
        compiler_params=pltpu.CompilerParams(vmem_limit_bytes=PREP * MIB),
        cost_estimate=LIGHT,
        name="prep",
    )(
        block_turbine,
        blade_pos.transpose(1, 0, 2),
        blade_vel.transpose(1, 0, 2),
        lift_coeff,
        velocity,
    )


def match(mine_ref, twin_ref, per_turbine):
    core = lax.axis_index("gz")
    turbine = lax.axis_index("gy").astype(F32)
    half = mine_ref.shape[0]
    first = [(mine_ref[k, 7:8, :] == turbine).astype(F32) for k in range(half)]
    second = [(twin_ref[k, 7:8, :] == turbine).astype(F32) for k in range(half)]
    masks = []
    for hits, others, leads in ((first, second, core == 0), (second, first, core == 1)):
        rank = jnp.where(leads, jnp.zeros_like(hits[0]), sum(others))
        for hit in hits:
            masks.append([(hit > 0.5) & (rank == k) for k in range(per_turbine)])
            rank = rank + hit
    return masks


def sample_kernel(
    per_turbine, mine_ref, twin_ref, vel_ref, part_ref, own_ref, mask_ref, weight_ref, lev_ref,
    even_ref, odd_ref, center_ref, plane_ref, acc_ref,
):
    components, depth, rows, cols = vel_ref.shape
    points = mine_ref.shape[2]
    count = per_turbine * points
    cells = depth * rows
    chunks = cols // STEP
    core = lax.axis_index("gz")
    start = lax.axis_index("gy") * cols

    def column(at):
        return slice(at * STEP, (at + 1) * STEP)

    def bell(cell, center):
        gap = cell.astype(F32) - center
        return jnp.exp(gap * gap * (-1.0 / (smear * smear)))

    def weights(at, ref):
        lane = lax.broadcasted_iota(jnp.int32, (1, 128), 1)
        for part in range(STEP // 128):
            cell = start + at * STEP + part * 128 + lane
            ref[:, part * 128 : part * 128 + 128] = bell(cell, center_ref[...])

    def multiply(at, ref):
        for i in range(components):
            high, low = split(vel_ref[i, :, :, column(at)].reshape(cells, STEP))
            field = dot(plane_ref[...], jnp.concatenate([high, high, low], axis=0))
            product = field * ref[...]
            total = acc_ref[i]
            for part in range(STEP // 128):
                total += product[:, part * 128 : part * 128 + 128]
            acc_ref[i] = total
        high, low = split(ref[...])
        weight_ref[:count, column(at)] = high
        weight_ref[count:, column(at)] = low

    lev_ref[...] = vel_ref[:, pl.ds(jnp.where(core == 0, depth - 2, 0), 2)]
    masks = match(mine_ref, twin_ref, per_turbine)
    blocks = mine_ref.shape[0]
    lane = lax.broadcasted_iota(jnp.int32, (1, cells), 1)
    level = core * depth + lane // rows
    row = lax.axis_index("gx") * rows + lane % rows
    for k in range(per_turbine):
        total = jnp.zeros((8, points), F32)
        for at, mask in enumerate(masks):
            tile = mine_ref[at] if at < blocks else twin_ref[at - blocks]
            total = jnp.where(mask[k], tile, total)
        band = slice(k * points, (k + 1) * points)
        own_ref[:, band] = total
        turned = total.T
        center_ref[band, :] = jnp.broadcast_to(turned[:, 1:2], (points, 128))
        plane = bell(row, turned[:, 0:1]) * bell(level, turned[:, 2:3])
        high, low = split(plane)
        plane_ref[band, :cells] = high
        plane_ref[band, cells : 2 * cells] = low
        plane_ref[band, 2 * cells :] = high
    for at in range(blocks):
        for k in range(per_turbine):
            mask_ref[at, k : k + 1, :] = masks[at][k].astype(F32)
    acc_ref[...] = jnp.zeros(acc_ref.shape, F32)
    weights(0, even_ref)

    for at in range(chunks):
        now, later = (even_ref, odd_ref) if at % 2 == 0 else (odd_ref, even_ref)
        if at < chunks - 1:
            weights(at + 1, later)
        multiply(at, now)
    for i in range(components):
        for k in range(per_turbine):
            band = slice(k * points, (k + 1) * points)
            total = jnp.sum(acc_ref[i, band, :].T, axis=0, keepdims=True)
            part_ref[i : i + 1, band] = smear_norm * total
    part_ref[components:, :] = jnp.zeros((8 - components, count), F32)


def sample(mine, twin, velocity, per_turbine):
    components, depth, rows, cols = velocity.shape
    points = mine.shape[2]
    count = per_turbine * points
    vmem = pl.BlockSpec(memory_space=pltpu.VMEM)
    return pl.pallas_call(
        functools.partial(sample_kernel, per_turbine),
        in_specs=[vmem] * 3,
        out_specs=[vmem] * 5,
        out_shape=[
            jax.ShapeDtypeStruct((8, count), F32),
            jax.ShapeDtypeStruct((8, count), F32),
            jax.ShapeDtypeStruct((mine.shape[0], per_turbine, points), F32),
            jax.ShapeDtypeStruct((2 * count, cols), BF16),
            jax.ShapeDtypeStruct((components, 2, rows, cols), F32),
        ],
        scratch_shapes=[
            pltpu.VMEM((count, STEP), F32),
            pltpu.VMEM((count, STEP), F32),
            pltpu.VMEM((count, 128), F32),
            pltpu.VMEM((count, 3 * depth * rows), BF16),
            pltpu.VMEM((components, count, 128), F32),
        ],
        compiler_params=pltpu.CompilerParams(vmem_limit_bytes=SAMPLE * MIB),
        cost_estimate=LIGHT,
        name="sample",
    )(mine, twin, velocity)


def force_kernel(
    per_turbine, owned, mask_ref, part_ref, other_ref, own_ref, force_ref, home_ref
):
    points = own_ref.shape[1] // per_turbine
    relative = part_ref[0:3, :] + other_ref[0:3, :] - own_ref[3:6, :]
    speed = jnp.sqrt(jnp.sum(relative * relative, axis=0, keepdims=True))
    force = -own_ref[6:7, :] * speed * relative
    force_ref[...] = jnp.zeros(force_ref.shape, F32)
    force_ref[0:3, :] = force
    for row in range(mask_ref.shape[0]):
        total = jnp.zeros((3, points), F32)
        for k in range(per_turbine):
            total = jnp.where(mask_ref[row, k : k + 1, :] > 0.5, force[:, k * points : (k + 1) * points], total)
        for i in range(3):
            home_ref[row // owned, i, row % owned : row % owned + 1, :] = total[i : i + 1]


def point_forces(mask, part, other, own, per_turbine, owned):
    count = own.shape[1]
    points = count // per_turbine
    shifts = mask.shape[0] // owned
    return pl.pallas_call(
        functools.partial(force_kernel, per_turbine, owned),
        in_specs=[pl.BlockSpec(memory_space=pltpu.VMEM)] * 4,
        out_specs=[pl.BlockSpec(memory_space=pltpu.VMEM)] * 2,
        out_shape=[
            jax.ShapeDtypeStruct((8, count), F32),
            jax.ShapeDtypeStruct((shifts, 3, owned, points), F32),
        ],
        compiler_params=pltpu.CompilerParams(vmem_limit_bytes=8 * MIB),
        cost_estimate=LIGHT,
        name="force",
    )(mask, part, other, own)


def update_kernel(
    own_ref, force_ref, op_ref, left_ref, right_ref, near_in, far_in, relay_in, weight_in, vel_in, lev_in,
    new_out, zero_ref, pad_ref, new_ref, side_ref, weight_ref, high_ref, low_ref, even, odd,
    vel_sems, side_sems, weight_sems, new_sems, lev_sem,
):
    components, depth, rows, cols = new_ref.shape
    chunks = cols // STEP
    cells = LEVELS * rows
    inner = (LEVELS + 4) * rows
    fill = op_ref.shape[1] // 2 - inner - 4 * LEVELS
    count = own_ref.shape[1]
    core = lax.axis_index("gz")
    turbine = lax.axis_index("gy")
    parity = lax.axis_index("gx") % 2
    lane = lax.broadcasted_iota(jnp.int32, (8, 128), 1)
    shifts = ((1, lane < 1), (2, lane < 2), (127, lane >= 127), (126, lane >= 126))

    def column(at, first=0):
        return pl.ds(pl.multiple_of(at * STEP + first, 128), STEP)

    def arrivals(at):
        return [
            pltpu.make_async_copy(
                vel_in.at[:, :, :, column(at)],
                pad_ref.at[:, pl.ds(2, depth), :, column(at, 128)],
                vel_sems.at[at],
            ),
            pltpu.make_async_copy(
                weight_in.at[:, column(at)], weight_ref.at[:, column(at)], weight_sems.at[at]
            ),
            pltpu.make_async_copy(
                near_in.at[:, :, column(at)], side_ref.at[1 - parity, :, :, column(at)], side_sems.at[0, at]
            ),
            pltpu.make_async_copy(
                far_in.at[:, :, column(at)],
                side_ref.at[parity, :, pl.ds(0, depth), column(at)],
                side_sems.at[1, at],
            ),
            pltpu.make_async_copy(
                relay_in.at[:, :, column(at)],
                side_ref.at[parity, :, pl.ds(depth, depth), column(at)],
                side_sems.at[2, at],
            ),
        ]

    def departure(at):
        return pltpu.make_async_copy(
            new_ref.at[:, :, :, column(at)], new_out.at[:, :, :, column(at)], new_sems.at[at]
        )

    def level_copy(at):
        return pltpu.make_async_copy(
            lev_in, pad_ref.at[:, pl.ds(at, 2), :, pl.ds(128, cols)], lev_sem
        )

    def side_columns(ref, present, lane):
        per_part = 128 // rows
        parts = ref.shape[0] // components
        for tile in range(ref.shape[0]):
            turned = jnp.where(present, ref[tile], 0.0).T
            for k in range(per_part):
                level = (tile % parts) * per_part + k
                pad_ref[tile // parts, level + 2, :, lane : lane + 8] = turned[k * rows : (k + 1) * rows, :]

    def matrix_part(at, bufs):
        grad_ref, lap_ref, body_ref = bufs
        pad = pad_ref.at[:, :, :, column(at, 128)]
        sides = side_ref.at[:, :, :, column(at)]
        weight = weight_ref.at[:, column(at)]
        for i in range(components):
            for half in range(depth // LEVELS):
                levels = slice(half * LEVELS, (half + 1) * LEVELS)
                field = pad[i, half * LEVELS : (half + 1) * LEVELS + 4]
                inner_high, inner_low = split(field.reshape(inner, STEP))
                side = slice(half * 2 * LEVELS, (half + 1) * 2 * LEVELS)
                prev_high, prev_low = split(sides[0, i, side])
                next_high, next_low = split(sides[1, i, side])
                empty = [jnp.zeros((fill, STEP), BF16)] if fill else []
                high = [inner_high, prev_high, next_high] + empty
                low = [inner_low, prev_low, next_low] + empty
                result = dot(op_ref[...], jnp.concatenate(high + low, axis=0))
                grad_ref[i, levels] = result[:cells].reshape(LEVELS, rows, STEP)
                lap_ref[i, levels] = result[cells:].reshape(LEVELS, rows, STEP)
        upper = weight[:count]
        lower = weight[count:]
        wide = jnp.concatenate([high_ref[...], low_ref[...], high_ref[...]], axis=1)
        result = dot(wide, jnp.concatenate([upper, upper, lower], axis=0))
        body_ref[...] = result.reshape(components, depth, rows, STEP)

    def vector_part(at, bufs):
        grad_ref, lap_ref, body_ref = bufs
        pad = pad_ref.at[:, :, :, pl.ds(pl.multiple_of(at * STEP, 128), STEP + 256)]
        new = new_ref.at[:, :, :, column(at)]

        def cell(i, level, band, block):
            return pad[i, level, band, block * 128 : block * 128 + 128]

        def work(level, band):
            here = level + 2
            turned = {}

            def turn(i, block, shift):
                if (i, block, shift) not in turned:
                    turned[i, block, shift] = pltpu.roll(cell(i, here, band, block), shift, 1)
                return turned[i, block, shift]

            for block in range(1, STEP // 128 + 1):
                lanes = slice(block * 128 - 128, block * 128)
                along_y, lap, along_z = [], [], []
                for i in range(components):
                    behind, behind2, ahead, ahead2 = [
                        jnp.where(
                            wrapped,
                            turn(i, block - 1 if shift < 64 else block + 1, shift),
                            turn(i, block, shift),
                        )
                        for shift, wrapped in shifts
                    ]
                    along_y.append(8.0 * (ahead - behind) - (ahead2 - behind2))
                    lap.append(
                        lap_ref[i, level, band, lanes]
                        + (16.0 * (ahead + behind) - (ahead2 + behind2))
                    )
                    near = cell(i, here + 1, band, block) - cell(i, here - 1, band, block)
                    far = cell(i, here + 2, band, block) - cell(i, here - 2, band, block)
                    along_z.append(8.0 * near - far)
                along_x = [grad_ref[i, level, band, lanes] for i in range(components)]
                same = along_x[0] * along_x[0] + along_y[1] * along_y[1] + along_z[2] * along_z[2]
                xy = along_x[1] + along_y[0]
                xz = along_x[2] + along_z[0]
                yz = along_y[2] + along_z[1]
                strain = 2.0 * same + (xy * xy + xz * xz + yz * yz)
                mixing = (time_step / 12.0) * viscosity + (
                    time_step * smag_coeff * smag_coeff / 144.0
                ) * jnp.sqrt(strain)
                for i in range(components):
                    change = mixing * lap[i] - (time_step * mean_wind / 12.0) * along_x[i]
                    new[i, level, band, lanes] = (
                        cell(i, here, band, block) + body_ref[i, level, band, lanes] + change
                    )

        for level in range(depth):
            for row in range(0, rows, 8):
                work(level, slice(row, row + 8))
        departure(at).start()

    for copy in arrivals(0):
        copy.start()
    zero_ref[...] = jnp.zeros(zero_ref.shape, F32)

    @pl.when(core == 1)
    def _():
        level_copy(0).start()
        pad_ref[:, depth + 2 :, :, 128 : cols + 128] = jnp.zeros((components, 2, rows, cols), F32)

    @pl.when(core == 0)
    def _():
        level_copy(depth + 2).start()
        pad_ref[:, 0:2, :, 128 : cols + 128] = jnp.zeros((components, 2, rows, cols), F32)

    side_columns(left_ref, turbine > 0, 120)
    side_columns(right_ref, turbine < lax.axis_size("gy") - 1, cols + 128)
    along_x = gaussian(lax.axis_index("gx") * rows, rows, own_ref[0:1, :])
    along_z = gaussian(core * depth, depth, own_ref[2:3, :])
    for i in range(components):
        scaled = (time_step * smear_norm) * force_ref[i : i + 1, :] * along_x
        for level in range(depth):
            band = slice((i * depth + level) * rows, (i * depth + level + 1) * rows)
            high, low = split(scaled * along_z[level : level + 1, :])
            high_ref[band, :] = high
            low_ref[band, :] = low
    level_copy(0).wait()
    for copy in arrivals(0):
        copy.wait()
    for copy in arrivals(1) + arrivals(2):
        copy.start()
    matrix_part(0, even)

    def pair(step, carry):
        for copy in arrivals(2 * step + 1) + arrivals(2 * step + 2):
            copy.wait()
        for copy in arrivals(2 * step + 3):
            copy.start()

        @pl.when(step < chunks // 2 - 2)
        def _():
            for copy in arrivals(2 * step + 4):
                copy.start()

        matrix_part(2 * step + 1, odd)
        vector_part(2 * step, even)
        matrix_part(2 * step + 2, even)
        vector_part(2 * step + 1, odd)
        return carry

    lax.fori_loop(0, chunks // 2 - 1, pair, 0)
    for copy in arrivals(chunks - 1):
        copy.wait()
    matrix_part(chunks - 1, odd)
    vector_part(chunks - 2, even)
    vector_part(chunks - 1, odd)
    for at in range(chunks):
        departure(at).wait()


def update(own, force, operator, near, far, relay, weight, velocity, lev, left, right, home_shape):
    components, depth, rows, cols = velocity.shape
    count = own.shape[1]
    chunks = cols // STEP
    vmem = pl.BlockSpec(memory_space=pltpu.VMEM)
    hbm = pl.BlockSpec(memory_space=pl.ANY)
    fields = [pltpu.VMEM((components, depth, rows, STEP), F32)] * 3
    macs = components * depth * rows * cols * (3 * count + 4 * 256)
    return pl.pallas_call(
        update_kernel,
        in_specs=[vmem] * 5 + [hbm] * 6,
        out_specs=[hbm, vmem],
        out_shape=[
            jax.ShapeDtypeStruct(velocity.shape, F32),
            jax.ShapeDtypeStruct(home_shape, F32),
        ],
        scratch_shapes=[
            pltpu.VMEM((components, depth + 4, rows, cols + 256), F32),
            pltpu.VMEM(velocity.shape, F32),
            pltpu.VMEM((2, *near.shape), F32),
            pltpu.VMEM((2 * count, cols), BF16),
            pltpu.VMEM((components * depth * rows, count), BF16),
            pltpu.VMEM((components * depth * rows, count), BF16),
            fields,
            fields,
            pltpu.SemaphoreType.DMA((chunks,)),
            pltpu.SemaphoreType.DMA((3, chunks)),
            pltpu.SemaphoreType.DMA((chunks,)),
            pltpu.SemaphoreType.DMA((chunks,)),
            pltpu.SemaphoreType.DMA,
        ],
        compiler_params=pltpu.CompilerParams(vmem_limit_bytes=UPDATE * MIB),
        cost_estimate=pl.CostEstimate(
            flops=2 * macs, bytes_accessed=8 * velocity.size, transcendentals=velocity.size // 3
        ),
        name="update",
    )(own, force, operator, left, right, near, far, relay, weight, velocity, lev)


def local(velocity, blade_pos, block_turbine, blade_vel, lift_coeff):
    components, depth, rows, cols = velocity.shape
    owned, _, points = blade_pos.shape
    gx, gy, gz = (lax.axis_size(axis) for axis in ("gx", "gy", "gz"))
    assert gz == 2 and depth == 2 * LEVELS
    per_turbine = owned * gz
    swap = [(0, 1), (1, 0)]

    def around(shift):
        return [(i, (i + shift) % gy) for i in range(gy)]

    held, blocks, up, down, near, far, relay = prep(
        velocity, blade_pos, block_turbine, blade_vel, lift_coeff
    )
    near = lax.ppermute(near, "gx", [(i, i ^ 1) for i in range(gx)])
    across = [(i, i + 1) for i in range(1, gx - 1, 2)] + [(i + 1, i) for i in range(1, gx - 1, 2)]
    if gx == 4:
        relay = lax.ppermute(relay, "gx", [(1, 3), (2, 0)])

    def gather(blocks, up, down):
        left = lax.ppermute(up, "gy", around(1))
        right = lax.ppermute(down, "gy", around(gy - 1))
        parts = [blocks, left[:owned]]
        parts += [lax.ppermute(blocks, "gy", around(shift)) for shift in range(2, gy - 1)]
        parts.append(right[:owned])
        mine = jnp.concatenate(parts, axis=0)
        return mine, lax.ppermute(mine, "gz", swap), left[owned:], right[owned:]

    def blade(mine, twin, velocity):
        part, own, mask, weight, facing = sample(mine, twin, velocity, per_turbine)
        other = lax.ppermute(part, "gz", swap)
        lev = lax.ppermute(facing, "gz", swap)
        force, home = point_forces(mask, part, other, own, per_turbine, owned)
        return own, force, home, weight, lev

    def stage(run, *operands):
        empty = [jnp.zeros(out.shape, out.dtype) for out in jax.eval_shape(run, *operands)]
        return lax.cond(block_turbine[0] >= 0, run, lambda *_: tuple(empty), *operands)

    mine, twin, left, right = stage(gather, blocks, up, down)
    if gx == 4:
        relay = lax.ppermute(relay, "gx", [(3, 2), (0, 1)])
    else:
        relay = lax.ppermute(relay, "gx", across)
    far = lax.ppermute(far, "gx", across)
    own, force, home, weight, lev = stage(blade, mine, twin, held)
    result = home[0]
    for shift in range(1, gy):
        result += lax.ppermute(home[shift], "gy", around(gy - shift))

    operator = jnp.asarray(stencil_operator(rows))
    new_velocity, zero = update(
        own, force, operator, near, far, relay, weight, held, lev, left, right, result.shape
    )
    return (new_velocity, (result + zero).transpose(1, 0, 2))


def solution(mesh):
    in_specs = (
        P(None, "gz", "gx", "gy"),
        P(("gx", "gy", "gz"), None, None),
        P(("gx", "gy", "gz")),
        P(("gx", "gy", "gz"), None, None),
        P(("gx", "gy", "gz"), None),
    )
    out_specs = (P(None, "gz", "gx", "gy"), P(("gx", "gy", "gz"), None, None))
    return jax.shard_map(local, mesh=mesh, in_specs=in_specs, out_specs=out_specs, check_vma=False)
```

```python
import functools
import math

import jax
import jax.numpy as jnp
import ml_dtypes
import numpy as np
from jax import lax
from jax.experimental import pallas as pl
from jax.experimental.pallas import tpu as pltpu
from jax.sharding import PartitionSpec as P

mean_wind = 1.0
viscosity = 0.2
smag_coeff = 0.17
time_step = 0.2
smear = 2.0
smear_norm = 1.0 / (smear**3 * math.pi**1.5)

F32 = jnp.float32
BF16 = jnp.bfloat16
MIB = 1024 * 1024
PREP, SAMPLE, UPDATE = 54, 32, 42
LEVELS = 8
STEP = 256
LIGHT = pl.CostEstimate(flops=0, bytes_accessed=0, transcendentals=0)


def split(value):
    high = value.astype(BF16)
    return high, (value - high.astype(F32)).astype(BF16)


def dot(left, right, contract=0):
    return lax.dot_general(
        left, right, (((1,), (contract,)), ((), ())), preferred_element_type=F32
    )


def gaussian(first, count, centers):
    shape = (count, centers.shape[1])
    cells = (first + lax.broadcasted_iota(jnp.int32, shape, 0)).astype(F32)
    gap = cells - centers
    return jnp.exp(-gap * gap / (smear * smear))


def stencil_operator(row_cells):
    inner = (LEVELS + 4) * row_cells
    width = inner + 4 * LEVELS
    op = np.zeros((2, LEVELS, row_cells, width), np.float32)

    def column(level, row):
        if 0 <= row < row_cells:
            return (level + 2) * row_cells + row
        if row < 0:
            return inner + level * 2 + row + 2
        return inner + 2 * LEVELS + level * 2 + row - row_cells

    for level in range(LEVELS):
        for row in range(row_cells):
            for offset, first, second in ((-2, 1, -1), (-1, -8, 16), (1, 8, 16), (2, -1, -1)):
                op[0, level, row, column(level, row + offset)] += first
                op[1, level, row, column(level, row + offset)] += second
                op[1, level, row, column(level + offset, row)] += second
            op[1, level, row, column(level, row)] -= 90
    op = op.reshape(2 * LEVELS * row_cells, width)
    op = np.pad(op, ((0, 0), (0, -width % 128)))
    return np.concatenate([op, op], axis=1).astype(ml_dtypes.bfloat16)


def prep_kernel(
    turb_in, pos_in, speed_in, lift_in, vel_in, vel_ref, blocks_ref, up_ref, down_ref, near_out, far_out,
    relay_out, turb_ref, pos_ref, speed_ref, lift_ref, near_ref, far_ref, relay_ref, sems, out_sems,
):
    components, levels, rows, cols = vel_ref.shape
    coords, owned, points = pos_ref.shape
    small = [
        pltpu.make_async_copy(source, target, sems.at[components + k])
        for k, (source, target) in enumerate(
            ((turb_in, turb_ref), (pos_in, pos_ref), (speed_in, speed_ref), (lift_in, lift_ref))
        )
    ]
    large = [
        pltpu.make_async_copy(vel_in.at[i], vel_ref.at[i], sems.at[i]) for i in range(components)
    ]
    for copy in small + large:
        copy.start()
    for copy in small:
        copy.wait()
    for ref in (blocks_ref, up_ref, down_ref):
        for k in range(owned):
            for i in range(coords):
                ref[k, i : i + 1, :] = pos_ref[i, k : k + 1, :]
                ref[k, coords + i : coords + i + 1, :] = speed_ref[i, k : k + 1, :]
            ref[k, 2 * coords : 2 * coords + 1, :] = lift_ref[k : k + 1, :]
            ref[k, 7:8, :] = jnp.full((1, points), turb_ref[k].astype(F32))
    parts = levels * rows // 128
    odd = lax.axis_index("gx") % 2 == 1
    leaving = []
    row = lax.broadcasted_iota(jnp.int32, (8, cols), 0) // 2
    for component in range(components):
        large[component].wait()
        last = vel_ref[component, :, :, cols - 128 :].reshape(levels * rows, 128)
        first = vel_ref[component, :, :, :128].reshape(levels * rows, 128)
        for part in range(parts):
            cells = slice(part * 128, part * 128 + 128)
            up_ref[owned + component * parts + part] = last[cells].T[120:]
            down_ref[owned + component * parts + part] = first[cells].T[:8]
        for group in range(levels // 4):
            head = tail = None
            for k in range(4):
                top = vel_ref[component, group * 4 + k, 0:8, :]
                end = vel_ref[component, group * 4 + k, rows - 8 : rows, :]
                if k:
                    top = pltpu.roll(top, 2 * k, 0)
                if k < 3:
                    end = pltpu.roll(end, 2 * k + 2, 0)
                head = top if head is None else jnp.where(row == k, top, head)
                tail = end if tail is None else jnp.where(row == k, end, tail)
            near_ref[component, group * 8 : group * 8 + 8, :] = jnp.where(odd, head, tail)
            ref, to = (far_ref, group * 8) if group * 8 < levels else (relay_ref, group * 8 - levels)
            ref[component, to : to + 8, :] = jnp.where(odd, tail, head)
        for k, (source, target) in enumerate(
            ((near_ref, near_out), (far_ref, far_out), (relay_ref, relay_out))
        ):
            copy = pltpu.make_async_copy(
                source.at[component], target.at[component], out_sems.at[component, k]
            )
            copy.start()
            leaving.append(copy)
    for copy in leaving:
        copy.wait()


def prep(velocity, blade_pos, block_turbine, blade_vel, lift_coeff):
    components, levels, rows, cols = velocity.shape
    owned, coords, points = blade_pos.shape
    tiles = owned + components * levels * rows // 128
    return pl.pallas_call(
        prep_kernel,
        in_specs=[pl.BlockSpec(memory_space=pltpu.HBM)] * 5,
        out_specs=[pl.BlockSpec(memory_space=pltpu.VMEM)] * 4
        + [pl.BlockSpec(memory_space=pltpu.HBM)] * 3,
        out_shape=[
            jax.ShapeDtypeStruct(velocity.shape, F32),
            jax.ShapeDtypeStruct((owned, 8, points), F32),
            jax.ShapeDtypeStruct((tiles, 8, 128), F32),
            jax.ShapeDtypeStruct((tiles, 8, 128), F32),
            jax.ShapeDtypeStruct((components, 2 * levels, cols), F32),
            jax.ShapeDtypeStruct((components, levels, cols), F32),
            jax.ShapeDtypeStruct((components, levels, cols), F32),
        ],
        scratch_shapes=[
            pltpu.SMEM((owned,), jnp.int32),
            pltpu.VMEM((coords, owned, points), F32),
            pltpu.VMEM((coords, owned, points), F32),
            pltpu.VMEM((owned, points), F32),
            pltpu.VMEM((components, 2 * levels, cols), F32),
            pltpu.VMEM((components, levels, cols), F32),
            pltpu.VMEM((components, levels, cols), F32),
            pltpu.SemaphoreType.DMA((components + 4,)),
            pltpu.SemaphoreType.DMA((components, 3)),
        ],
        compiler_params=pltpu.CompilerParams(vmem_limit_bytes=PREP * MIB),
        cost_estimate=LIGHT,
        name="prep",
    )(
        block_turbine,
        blade_pos.transpose(1, 0, 2),
        blade_vel.transpose(1, 0, 2),
        lift_coeff,
        velocity,
    )


def match(mine_ref, twin_ref, per_turbine):
    core = lax.axis_index("gz")
    turbine = lax.axis_index("gy").astype(F32)
    half = mine_ref.shape[0]
    first = [(mine_ref[k, 7:8, :] == turbine).astype(F32) for k in range(half)]
    second = [(twin_ref[k, 7:8, :] == turbine).astype(F32) for k in range(half)]
    masks = []
    for hits, others, leads in ((first, second, core == 0), (second, first, core == 1)):
        rank = jnp.where(leads, jnp.zeros_like(hits[0]), sum(others))
        for hit in hits:
            masks.append([(hit > 0.5) & (rank == k) for k in range(per_turbine)])
            rank = rank + hit
    return masks


def sample_kernel(
    per_turbine, mine_ref, twin_ref, vel_ref, part_ref, own_ref, mask_ref, weight_ref, lev_ref,
    even_ref, odd_ref, center_ref, plane_ref, acc_ref,
):
    components, depth, rows, cols = vel_ref.shape
    points = mine_ref.shape[2]
    count = per_turbine * points
    cells = depth * rows
    chunks = cols // STEP
    core = lax.axis_index("gz")
    start = lax.axis_index("gy") * cols

    def column(at):
        return slice(at * STEP, (at + 1) * STEP)

    def bell(cell, center):
        gap = cell.astype(F32) - center
        return jnp.exp(gap * gap * (-1.0 / (smear * smear)))

    def weights(at, ref):
        lane = lax.broadcasted_iota(jnp.int32, (1, 128), 1)
        for part in range(STEP // 128):
            cell = start + at * STEP + part * 128 + lane
            ref[:, part * 128 : part * 128 + 128] = bell(cell, center_ref[...])

    def multiply(at, ref):
        for i in range(components):
            high, low = split(vel_ref[i, :, :, column(at)].reshape(cells, STEP))
            field = dot(plane_ref[...], jnp.concatenate([high, high, low], axis=0))
            product = field * ref[...]
            total = acc_ref[i]
            for part in range(STEP // 128):
                total += product[:, part * 128 : part * 128 + 128]
            acc_ref[i] = total
        high, low = split(ref[...])
        weight_ref[:count, column(at)] = high
        weight_ref[count:, column(at)] = low

    lev_ref[...] = vel_ref[:, pl.ds(jnp.where(core == 0, depth - 2, 0), 2)]
    masks = match(mine_ref, twin_ref, per_turbine)
    blocks = mine_ref.shape[0]
    lane = lax.broadcasted_iota(jnp.int32, (1, cells), 1)
    level = core * depth + lane // rows
    row = lax.axis_index("gx") * rows + lane % rows
    for k in range(per_turbine):
        total = jnp.zeros((8, points), F32)
        for at, mask in enumerate(masks):
            tile = mine_ref[at] if at < blocks else twin_ref[at - blocks]
            total = jnp.where(mask[k], tile, total)
        band = slice(k * points, (k + 1) * points)
        own_ref[:, band] = total
        turned = total.T
        center_ref[band, :] = jnp.broadcast_to(turned[:, 1:2], (points, 128))
        plane = bell(row, turned[:, 0:1]) * bell(level, turned[:, 2:3])
        high, low = split(plane)
        plane_ref[band, :cells] = high
        plane_ref[band, cells : 2 * cells] = low
        plane_ref[band, 2 * cells :] = high
    for at in range(blocks):
        for k in range(per_turbine):
            mask_ref[at, k : k + 1, :] = masks[at][k].astype(F32)
    acc_ref[...] = jnp.zeros(acc_ref.shape, F32)
    weights(0, even_ref)

    for at in range(chunks):
        now, later = (even_ref, odd_ref) if at % 2 == 0 else (odd_ref, even_ref)
        if at < chunks - 1:
            weights(at + 1, later)
        multiply(at, now)
    for i in range(components):
        for k in range(per_turbine):
            band = slice(k * points, (k + 1) * points)
            total = jnp.sum(acc_ref[i, band, :].T, axis=0, keepdims=True)
            part_ref[i : i + 1, band] = smear_norm * total
    part_ref[components:, :] = jnp.zeros((8 - components, count), F32)


def sample(mine, twin, velocity, per_turbine):
    components, depth, rows, cols = velocity.shape
    points = mine.shape[2]
    count = per_turbine * points
    vmem = pl.BlockSpec(memory_space=pltpu.VMEM)
    return pl.pallas_call(
        functools.partial(sample_kernel, per_turbine),
        in_specs=[vmem] * 3,
        out_specs=[vmem] * 5,
        out_shape=[
            jax.ShapeDtypeStruct((8, count), F32),
            jax.ShapeDtypeStruct((8, count), F32),
            jax.ShapeDtypeStruct((mine.shape[0], per_turbine, points), F32),
            jax.ShapeDtypeStruct((2 * count, cols), BF16),
            jax.ShapeDtypeStruct((components, 2, rows, cols), F32),
        ],
        scratch_shapes=[
            pltpu.VMEM((count, STEP), F32),
            pltpu.VMEM((count, STEP), F32),
            pltpu.VMEM((count, 128), F32),
            pltpu.VMEM((count, 3 * depth * rows), BF16),
            pltpu.VMEM((components, count, 128), F32),
        ],
        compiler_params=pltpu.CompilerParams(vmem_limit_bytes=SAMPLE * MIB),
        cost_estimate=LIGHT,
        name="sample",
    )(mine, twin, velocity)


def force_kernel(
    per_turbine, owned, mask_ref, part_ref, other_ref, own_ref, force_ref, home_ref
):
    points = own_ref.shape[1] // per_turbine
    relative = part_ref[0:3, :] + other_ref[0:3, :] - own_ref[3:6, :]
    speed = jnp.sqrt(jnp.sum(relative * relative, axis=0, keepdims=True))
    force = -own_ref[6:7, :] * speed * relative
    force_ref[...] = jnp.zeros(force_ref.shape, F32)
    force_ref[0:3, :] = force
    for row in range(mask_ref.shape[0]):
        total = jnp.zeros((3, points), F32)
        for k in range(per_turbine):
            total = jnp.where(mask_ref[row, k : k + 1, :] > 0.5, force[:, k * points : (k + 1) * points], total)
        for i in range(3):
            home_ref[row // owned, i, row % owned : row % owned + 1, :] = total[i : i + 1]


def point_forces(mask, part, other, own, per_turbine, owned):
    count = own.shape[1]
    points = count // per_turbine
    shifts = mask.shape[0] // owned
    return pl.pallas_call(
        functools.partial(force_kernel, per_turbine, owned),
        in_specs=[pl.BlockSpec(memory_space=pltpu.VMEM)] * 4,
        out_specs=[pl.BlockSpec(memory_space=pltpu.VMEM)] * 2,
        out_shape=[
            jax.ShapeDtypeStruct((8, count), F32),
            jax.ShapeDtypeStruct((shifts, 3, owned, points), F32),
        ],
        compiler_params=pltpu.CompilerParams(vmem_limit_bytes=8 * MIB),
        cost_estimate=LIGHT,
        name="force",
    )(mask, part, other, own)


def update_kernel(
    own_ref, force_ref, op_ref, left_ref, right_ref, near_in, far_in, relay_in, weight_in, vel_in, lev_in,
    new_out, zero_ref, pad_ref, new_ref, side_ref, weight_ref, high_ref, low_ref, even, odd,
    vel_sems, side_sems, weight_sems, new_sems, lev_sem,
):
    components, depth, rows, cols = new_ref.shape
    chunks = cols // STEP
    cells = LEVELS * rows
    inner = (LEVELS + 4) * rows
    fill = op_ref.shape[1] // 2 - inner - 4 * LEVELS
    count = own_ref.shape[1]
    core = lax.axis_index("gz")
    turbine = lax.axis_index("gy")
    parity = lax.axis_index("gx") % 2
    lane = lax.broadcasted_iota(jnp.int32, (8, 128), 1)
    shifts = ((1, lane < 1), (2, lane < 2), (127, lane >= 127), (126, lane >= 126))

    def column(at, first=0):
        return pl.ds(pl.multiple_of(at * STEP + first, 128), STEP)

    def arrivals(at):
        return [
            pltpu.make_async_copy(
                vel_in.at[:, :, :, column(at)],
                pad_ref.at[:, pl.ds(2, depth), :, column(at, 128)],
                vel_sems.at[at],
            ),
            pltpu.make_async_copy(
                weight_in.at[:, column(at)], weight_ref.at[:, column(at)], weight_sems.at[at]
            ),
            pltpu.make_async_copy(
                near_in.at[:, :, column(at)], side_ref.at[1 - parity, :, :, column(at)], side_sems.at[0, at]
            ),
            pltpu.make_async_copy(
                far_in.at[:, :, column(at)],
                side_ref.at[parity, :, pl.ds(0, depth), column(at)],
                side_sems.at[1, at],
            ),
            pltpu.make_async_copy(
                relay_in.at[:, :, column(at)],
                side_ref.at[parity, :, pl.ds(depth, depth), column(at)],
                side_sems.at[2, at],
            ),
        ]

    def departure(at):
        return pltpu.make_async_copy(
            new_ref.at[:, :, :, column(at)], new_out.at[:, :, :, column(at)], new_sems.at[at]
        )

    def level_copy(at):
        return pltpu.make_async_copy(
            lev_in, pad_ref.at[:, pl.ds(at, 2), :, pl.ds(128, cols)], lev_sem
        )

    def side_columns(ref, present, lane):
        per_part = 128 // rows
        parts = ref.shape[0] // components
        for tile in range(ref.shape[0]):
            turned = jnp.where(present, ref[tile], 0.0).T
            for k in range(per_part):
                level = (tile % parts) * per_part + k
                pad_ref[tile // parts, level + 2, :, lane : lane + 8] = turned[k * rows : (k + 1) * rows, :]

    def matrix_part(at, bufs):
        grad_ref, lap_ref, body_ref = bufs
        pad = pad_ref.at[:, :, :, column(at, 128)]
        sides = side_ref.at[:, :, :, column(at)]
        weight = weight_ref.at[:, column(at)]
        for i in range(components):
            for half in range(depth // LEVELS):
                levels = slice(half * LEVELS, (half + 1) * LEVELS)
                field = pad[i, half * LEVELS : (half + 1) * LEVELS + 4]
                inner_high, inner_low = split(field.reshape(inner, STEP))
                side = slice(half * 2 * LEVELS, (half + 1) * 2 * LEVELS)
                prev_high, prev_low = split(sides[0, i, side])
                next_high, next_low = split(sides[1, i, side])
                empty = [jnp.zeros((fill, STEP), BF16)] if fill else []
                high = [inner_high, prev_high, next_high] + empty
                low = [inner_low, prev_low, next_low] + empty
                result = dot(op_ref[...], jnp.concatenate(high + low, axis=0))
                grad_ref[i, levels] = result[:cells].reshape(LEVELS, rows, STEP)
                lap_ref[i, levels] = result[cells:].reshape(LEVELS, rows, STEP)
        upper = weight[:count]
        lower = weight[count:]
        wide = jnp.concatenate([high_ref[...], low_ref[...], high_ref[...]], axis=1)
        result = dot(wide, jnp.concatenate([upper, upper, lower], axis=0))
        body_ref[...] = result.reshape(components, depth, rows, STEP)

    def vector_part(at, bufs):
        grad_ref, lap_ref, body_ref = bufs
        pad = pad_ref.at[:, :, :, pl.ds(pl.multiple_of(at * STEP, 128), STEP + 256)]
        new = new_ref.at[:, :, :, column(at)]

        def cell(i, level, band, block):
            return pad[i, level, band, block * 128 : block * 128 + 128]

        def work(level, band):
            here = level + 2
            turned = {}

            def turn(i, block, shift):
                if (i, block, shift) not in turned:
                    turned[i, block, shift] = pltpu.roll(cell(i, here, band, block), shift, 1)
                return turned[i, block, shift]

            for block in range(1, STEP // 128 + 1):
                lanes = slice(block * 128 - 128, block * 128)
                along_y, lap, along_z = [], [], []
                for i in range(components):
                    behind, behind2, ahead, ahead2 = [
                        jnp.where(
                            wrapped,
                            turn(i, block - 1 if shift < 64 else block + 1, shift),
                            turn(i, block, shift),
                        )
                        for shift, wrapped in shifts
                    ]
                    along_y.append(8.0 * (ahead - behind) - (ahead2 - behind2))
                    lap.append(
                        lap_ref[i, level, band, lanes]
                        + (16.0 * (ahead + behind) - (ahead2 + behind2))
                    )
                    near = cell(i, here + 1, band, block) - cell(i, here - 1, band, block)
                    far = cell(i, here + 2, band, block) - cell(i, here - 2, band, block)
                    along_z.append(8.0 * near - far)
                along_x = [grad_ref[i, level, band, lanes] for i in range(components)]
                same = along_x[0] * along_x[0] + along_y[1] * along_y[1] + along_z[2] * along_z[2]
                xy = along_x[1] + along_y[0]
                xz = along_x[2] + along_z[0]
                yz = along_y[2] + along_z[1]
                strain = 2.0 * same + (xy * xy + xz * xz + yz * yz)
                mixing = (time_step / 12.0) * viscosity + (
                    time_step * smag_coeff * smag_coeff / 144.0
                ) * jnp.sqrt(strain)
                for i in range(components):
                    change = mixing * lap[i] - (time_step * mean_wind / 12.0) * along_x[i]
                    new[i, level, band, lanes] = (
                        cell(i, here, band, block) + body_ref[i, level, band, lanes] + change
                    )

        for level in range(depth):
            for row in range(0, rows, 8):
                work(level, slice(row, row + 8))
        departure(at).start()

    for copy in arrivals(0):
        copy.start()
    zero_ref[...] = jnp.zeros(zero_ref.shape, F32)

    @pl.when(core == 1)
    def _():
        level_copy(0).start()
        pad_ref[:, depth + 2 :, :, 128 : cols + 128] = jnp.zeros((components, 2, rows, cols), F32)

    @pl.when(core == 0)
    def _():
        level_copy(depth + 2).start()
        pad_ref[:, 0:2, :, 128 : cols + 128] = jnp.zeros((components, 2, rows, cols), F32)

    side_columns(left_ref, turbine > 0, 120)
    side_columns(right_ref, turbine < lax.axis_size("gy") - 1, cols + 128)
    along_x = gaussian(lax.axis_index("gx") * rows, rows, own_ref[0:1, :])
    along_z = gaussian(core * depth, depth, own_ref[2:3, :])
    for i in range(components):
        scaled = (time_step * smear_norm) * force_ref[i : i + 1, :] * along_x
        for level in range(depth):
            band = slice((i * depth + level) * rows, (i * depth + level + 1) * rows)
            high, low = split(scaled * along_z[level : level + 1, :])
            high_ref[band, :] = high
            low_ref[band, :] = low
    level_copy(0).wait()
    for copy in arrivals(0):
        copy.wait()
    for copy in arrivals(1) + arrivals(2):
        copy.start()
    matrix_part(0, even)

    def pair(step, carry):
        for copy in arrivals(2 * step + 1) + arrivals(2 * step + 2):
            copy.wait()
        for copy in arrivals(2 * step + 3):
            copy.start()

        @pl.when(step < chunks // 2 - 2)
        def _():
            for copy in arrivals(2 * step + 4):
                copy.start()

        matrix_part(2 * step + 1, odd)
        vector_part(2 * step, even)
        matrix_part(2 * step + 2, even)
        vector_part(2 * step + 1, odd)
        return carry

    lax.fori_loop(0, chunks // 2 - 1, pair, 0)
    for copy in arrivals(chunks - 1):
        copy.wait()
    matrix_part(chunks - 1, odd)
    vector_part(chunks - 2, even)
    vector_part(chunks - 1, odd)
    for at in range(chunks):
        departure(at).wait()


def update(own, force, operator, near, far, relay, weight, velocity, lev, left, right, home_shape):
    components, depth, rows, cols = velocity.shape
    count = own.shape[1]
    chunks = cols // STEP
    vmem = pl.BlockSpec(memory_space=pltpu.VMEM)
    hbm = pl.BlockSpec(memory_space=pl.ANY)
    fields = [pltpu.VMEM((components, depth, rows, STEP), F32)] * 3
    macs = components * depth * rows * cols * (3 * count + 4 * 256)
    return pl.pallas_call(
        update_kernel,
        in_specs=[vmem] * 5 + [hbm] * 6,
        out_specs=[hbm, vmem],
        out_shape=[
            jax.ShapeDtypeStruct(velocity.shape, F32),
            jax.ShapeDtypeStruct(home_shape, F32),
        ],
        scratch_shapes=[
            pltpu.VMEM((components, depth + 4, rows, cols + 256), F32),
            pltpu.VMEM(velocity.shape, F32),
            pltpu.VMEM((2, *near.shape), F32),
            pltpu.VMEM((2 * count, cols), BF16),
            pltpu.VMEM((components * depth * rows, count), BF16),
            pltpu.VMEM((components * depth * rows, count), BF16),
            fields,
            fields,
            pltpu.SemaphoreType.DMA((chunks,)),
            pltpu.SemaphoreType.DMA((3, chunks)),
            pltpu.SemaphoreType.DMA((chunks,)),
            pltpu.SemaphoreType.DMA((chunks,)),
            pltpu.SemaphoreType.DMA,
        ],
        compiler_params=pltpu.CompilerParams(vmem_limit_bytes=UPDATE * MIB),
        cost_estimate=pl.CostEstimate(
            flops=2 * macs, bytes_accessed=8 * velocity.size, transcendentals=velocity.size // 3
        ),
        name="update",
    )(own, force, operator, left, right, near, far, relay, weight, velocity, lev)


def local(velocity, blade_pos, block_turbine, blade_vel, lift_coeff):
    components, depth, rows, cols = velocity.shape
    owned, _, points = blade_pos.shape
    gx, gy, gz = (lax.axis_size(axis) for axis in ("gx", "gy", "gz"))
    assert gz == 2 and depth == 2 * LEVELS
    per_turbine = owned * gz
    swap = [(0, 1), (1, 0)]

    def around(shift):
        return [(i, (i + shift) % gy) for i in range(gy)]

    held, blocks, up, down, near, far, relay = prep(
        velocity, blade_pos, block_turbine, blade_vel, lift_coeff
    )
    near = lax.ppermute(near, "gx", [(i, i ^ 1) for i in range(gx)])
    across = [(i, i + 1) for i in range(1, gx - 1, 2)] + [(i + 1, i) for i in range(1, gx - 1, 2)]
    if gx == 4:
        relay = lax.ppermute(relay, "gx", [(1, 3), (2, 0)])

    def gather(blocks, up, down):
        left = lax.ppermute(up, "gy", around(1))
        right = lax.ppermute(down, "gy", around(gy - 1))
        parts = [blocks, left[:owned]]
        parts += [lax.ppermute(blocks, "gy", around(shift)) for shift in range(2, gy - 1)]
        parts.append(right[:owned])
        mine = jnp.concatenate(parts, axis=0)
        return mine, lax.ppermute(mine, "gz", swap), left[owned:], right[owned:]

    def blade(mine, twin, velocity):
        part, own, mask, weight, facing = sample(mine, twin, velocity, per_turbine)
        other = lax.ppermute(part, "gz", swap)
        lev = lax.ppermute(facing, "gz", swap)
        force, home = point_forces(mask, part, other, own, per_turbine, owned)
        return own, force, home, weight, lev

    def stage(run, *operands):
        empty = [jnp.zeros(out.shape, out.dtype) for out in jax.eval_shape(run, *operands)]
        return lax.cond(block_turbine[0] >= 0, run, lambda *_: tuple(empty), *operands)

    mine, twin, left, right = stage(gather, blocks, up, down)
    if gx == 4:
        relay = lax.ppermute(relay, "gx", [(3, 2), (0, 1)])
    else:
        relay = lax.ppermute(relay, "gx", across)
    far = lax.ppermute(far, "gx", across)
    own, force, home, weight, lev = stage(blade, mine, twin, held)
    result = home[0]
    for shift in range(1, gy):
        result += lax.ppermute(home[shift], "gy", around(gy - shift))

    operator = jnp.asarray(stencil_operator(rows))
    new_velocity, zero = update(
        own, force, operator, near, far, relay, weight, held, lev, left, right, result.shape
    )
    return (new_velocity, (result + zero).transpose(1, 0, 2))


def solution(mesh):
    in_specs = (
        P(None, "gz", "gx", "gy"),
        P(("gx", "gy", "gz"), None, None),
        P(("gx", "gy", "gz")),
        P(("gx", "gy", "gz"), None, None),
        P(("gx", "gy", "gz"), None),
    )
    out_specs = (P(None, "gz", "gx", "gy"), P(("gx", "gy", "gz"), None, None))
    return jax.shard_map(local, mesh=mesh, in_specs=in_specs, out_specs=out_specs, check_vma=False)
```
